128 devices in a mesh: dp: 32 (over z, x, core), mp: 4 (over y).
Axes of the slice: x: 4, y: 4, z: 4, core: 2. Of those that a mesh axis runs over, the one named last changes fastest.
Arguments:
- features: bfloat16 [40960, 512], P(('dp', 'mp')), may hold values from -6 to 6
- lengths: int32 [32], P('dp'), may hold values from 961 to 1280, as said below
- first_gain: bfloat16 [512], replicated, may hold values from 0.099609375 to 1.8984375
- first_shift: bfloat16 [512], replicated, may hold values from -1.75 to 1.75
- first_up: bfloat16 [512, 2048], P(None, 'mp'), may hold values from -0.25 to 0.25
- first_down: bfloat16 [2048, 512], P('mp'), may hold values from -0.25 to 0.25
- attn_gain: bfloat16 [512], replicated, may hold values from 0.099609375 to 1.8984375
- attn_shift: bfloat16 [512], replicated, may hold values from -1.75 to 1.75
- w_query: bfloat16 [512, 512], P(None, 'mp'), may hold values from -0.25 to 0.25
- w_key: bfloat16 [512, 512], P(None, 'mp'), may hold values from -0.25 to 0.25
- w_value: bfloat16 [512, 512], P(None, 'mp'), may hold values from -0.25 to 0.25
- w_pos: bfloat16 [512, 512], P(None, 'mp'), may hold values from -0.25 to 0.25
- bias_content: bfloat16 [8, 64], P('mp'), may hold values from -3 to 3
- bias_position: bfloat16 [8, 64], P('mp'), may hold values from -3 to 3
- attn_out: bfloat16 [512, 512], P('mp'), may hold values from -1.5 to 1.5
- cgmlp_gain: bfloat16 [512], replicated, may hold values from 0.099609375 to 1.8984375
- cgmlp_shift: bfloat16 [512], replicated, may hold values from -1.75 to 1.75
- cgmlp_up: bfloat16 [512, 2, 1536], P(None, None, 'mp'), may hold values from -0.25 to 0.25
- gate_gain: bfloat16 [1536], P('mp'), may hold values from 0.099609375 to 1.8984375
- gate_shift: bfloat16 [1536], P('mp'), may hold values from -1.75 to 1.75
- gate_taps: bfloat16 [31, 1536], P(None, 'mp'), may hold values from -1 to 1
- cgmlp_down: bfloat16 [1536, 512], P('mp'), may hold values from -0.3125 to 0.3125
- merge_taps: bfloat16 [31, 1024], replicated, may hold values from -1 to 1
- merge_proj: bfloat16 [1024, 512], replicated, may hold values from -0.1875 to 0.1875
- second_gain: bfloat16 [512], replicated, may hold values from 0.099609375 to 1.8984375
- second_shift: bfloat16 [512], replicated, may hold values from -1.75 to 1.75
- second_up: bfloat16 [512, 2048], P(None, 'mp'), may hold values from -0.25 to 0.25
- second_down: bfloat16 [2048, 512], P('mp'), may hold values from -0.25 to 0.25
- final_gain: bfloat16 [512], replicated, may hold values from 0.099609375 to 1.8984375
- final_shift: bfloat16 [512], replicated, may hold values from -1.75 to 1.75
- cotangent: bfloat16 [40960, 512], P(('dp', 'mp')), may hold values from -6 to 6
Outputs:
- encoded: float32 [40960, 512], P(('dp', 'mp'))
- grad_features: float32 [40960, 512], P(('dp', 'mp'))
- grad_first_gain: float32 [512], replicated
- grad_first_shift: float32 [512], replicated
- grad_first_up: float32 [512, 2048], P(None, 'mp')
- grad_first_down: float32 [2048, 512], P('mp')
- grad_attn_gain: float32 [512], replicated
- grad_attn_shift: float32 [512], replicated
- grad_w_query: float32 [512, 512], P(None, 'mp')
- grad_w_key: float32 [512, 512], P(None, 'mp')
- grad_w_value: float32 [512, 512], P(None, 'mp')
- grad_w_pos: float32 [512, 512], P(None, 'mp')
- grad_bias_content: float32 [8, 64], P('mp')
- grad_bias_position: float32 [8, 64], P('mp')
- grad_attn_out: float32 [512, 512], P('mp')
- grad_cgmlp_gain: float32 [512], replicated
- grad_cgmlp_shift: float32 [512], replicated
- grad_cgmlp_up: float32 [512, 2, 1536], P(None, None, 'mp')
- grad_gate_gain: float32 [1536], P('mp')
- grad_gate_shift: float32 [1536], P('mp')
- grad_gate_taps: float32 [31, 1536], P(None, 'mp')
- grad_cgmlp_down: float32 [1536, 512], P('mp')
- grad_merge_taps: float32 [31, 1024], replicated
- grad_merge_proj: float32 [1024, 512], replicated
- grad_second_gain: float32 [512], replicated
- grad_second_shift: float32 [512], replicated
- grad_second_up: float32 [512, 2048], P(None, 'mp')
- grad_second_down: float32 [2048, 512], P('mp')
- grad_final_gain: float32 [512], replicated
- grad_final_shift: float32 [512], replicated
The draws below stay inside these ranges and needn't reach their ends.
Inputs may be any that keep to these rules, and one draw needn't show every extreme that they name: `lengths`: each utterance's count of real frames; some utterance has all 1280.
All inputs are finite; a program needn't handle non-finite values.
Results may differ from the reference program's by a relative error of at most 0.04.
Values may be sent and summed in bfloat16 or wider, within the bound.
A program may use at most 256 MiB of HBM per device.

```python
import math
import jax
import jax.numpy as jnp
from jax import lax

D = 512
HEADS = 8
HEAD = 64
FF = 2048
GATE = 1536
KERNEL = 31
LEN = 1280
FRAMES_DEV = 320
UTTS = 32
TOKENS = 40960


def draw_lengths(key, part):
    key = jax.random.fold_in(key, 7)
    first_key, second_key = jax.random.split(key)
    drawn = jax.random.randint(first_key, (UTTS,), LEN - FRAMES_DEV + 1, LEN + 1)
    chosen = jax.random.randint(second_key, (), 0, UTTS)
    return jnp.where(jnp.arange(UTTS, dtype=jnp.int32) == chosen, LEN, drawn).astype(jnp.int32)


def level_of(key, extent, shards, least, high):
    def one(position, parts):
        steps = jax.random.uniform(jax.random.fold_in(jax.random.fold_in(key, 6), position), (parts,), jnp.float32, least / len(shards), high / len(shards))
        return jnp.repeat(jnp.exp(steps), extent[position] // parts).reshape((-1,) + (1,) * (len(extent) - position - 1))

    level = one(*shards[0])
    for cut in shards[1:]:
        level = level * one(*cut)
    return level


def normal_values(own_key, shape, width, limit, pieces=(), held_as=jnp.bfloat16):
    loudness = level_of(own_key, shape, pieces, -0.22, 0.18) if pieces else 1.0
    entries = jax.random.normal(own_key, shape, jnp.float32) * width * loudness
    return jnp.minimum(jnp.maximum(entries, -limit), limit).astype(held_as)


def setup_inputs(seed: int = 0) -> dict:
    key_of = jax.random.split(jax.random.key(seed), 32)
    features = normal_values(key_of[0], (TOKENS, D), 1.0, 6.0, ((0, 128),))
    lengths = draw_lengths(jax.random.fold_in(key_of[31], 71), 0)
    first_gain = jnp.clip(1.0 + 0.18 * jax.random.normal(key_of[2], (D,), jnp.float32), 0.099609375, 1.8984375).astype(jnp.bfloat16)
    first_shift = normal_values(key_of[3], (D,), 0.3, 1.75)
    first_up = normal_values(key_of[4], (D, FF), D ** -0.5, 0.25, ((1, 4),))
    first_down = normal_values(key_of[5], (FF, D), (FF // 4) ** -0.5, 0.25, ((0, 4),))
    attn_gain = jnp.clip(1.0 + 0.18 * jax.random.normal(key_of[6], (D,), jnp.float32), 0.099609375, 1.8984375).astype(jnp.bfloat16)
    attn_shift = normal_values(key_of[7], (D,), 0.3, 1.75)
    w_query = normal_values(key_of[8], (D, HEADS * HEAD), D ** -0.5, 0.25, ((1, 4),))
    w_key = normal_values(key_of[9], (D, HEADS * HEAD), D ** -0.5, 0.25, ((1, 4),))
    w_value = normal_values(key_of[10], (D, HEADS * HEAD), D ** -0.5, 0.25, ((1, 4),))
    w_pos = normal_values(key_of[11], (D, HEADS * HEAD), D ** -0.5, 0.25, ((1, 4),))
    bias_content = normal_values(key_of[12], (HEADS, HEAD), 0.5, 3.0, ((0, 4),))
    bias_position = normal_values(key_of[13], (HEADS, HEAD), 0.5, 3.0, ((0, 4),))
    attn_out = normal_values(key_of[14], (HEADS * HEAD, D), (HEAD // 4) ** -0.5, 1.5, ((0, 4),))
    cgmlp_gain = jnp.clip(1.0 + 0.18 * jax.random.normal(key_of[15], (D,), jnp.float32), 0.099609375, 1.8984375).astype(jnp.bfloat16)
    cgmlp_shift = normal_values(key_of[16], (D,), 0.3, 1.75)
    cgmlp_up = normal_values(key_of[17], (D, 2, GATE), D ** -0.5, 0.25, ((2, 4),))
    gate_gain = jnp.clip(1.0 + 0.18 * jax.random.normal(key_of[18], (GATE,), jnp.float32), 0.099609375, 1.8984375).astype(jnp.bfloat16)
    gate_shift = normal_values(key_of[19], (GATE,), 0.3, 1.75, ((0, 4),))
    gate_taps = normal_values(key_of[20], (KERNEL, GATE), KERNEL ** -0.5, 1.0, ((1, 4),))
    cgmlp_down = normal_values(key_of[21], (GATE, D), (GATE // 4) ** -0.5, 0.3125, ((0, 4),))
    merge_taps = normal_values(key_of[22], (KERNEL, 2 * D), KERNEL ** -0.5, 1.0)
    merge_proj = normal_values(key_of[23], (2 * D, D), (2 * D) ** -0.5, 0.1875)
    second_gain = jnp.clip(1.0 + 0.18 * jax.random.normal(key_of[24], (D,), jnp.float32), 0.099609375, 1.8984375).astype(jnp.bfloat16)
    second_shift = normal_values(key_of[25], (D,), 0.3, 1.75)
    second_up = normal_values(key_of[26], (D, FF), D ** -0.5, 0.25, ((1, 4),))
    second_down = normal_values(key_of[27], (FF, D), (FF // 4) ** -0.5, 0.25, ((0, 4),))
    final_gain = jnp.clip(1.0 + 0.18 * jax.random.normal(key_of[28], (D,), jnp.float32), 0.099609375, 1.8984375).astype(jnp.bfloat16)
    final_shift = normal_values(key_of[29], (D,), 0.3, 1.75)
    cotangent = normal_values(key_of[30], (TOKENS, D), 1.0, 6.0, ((0, 128),))
    return dict(features=features, lengths=lengths, first_gain=first_gain, first_shift=first_shift, first_up=first_up, first_down=first_down, attn_gain=attn_gain, attn_shift=attn_shift, w_query=w_query, w_key=w_key, w_value=w_value, w_pos=w_pos, bias_content=bias_content, bias_position=bias_position, attn_out=attn_out, cgmlp_gain=cgmlp_gain, cgmlp_shift=cgmlp_shift, cgmlp_up=cgmlp_up, gate_gain=gate_gain, gate_shift=gate_shift, gate_taps=gate_taps, cgmlp_down=cgmlp_down, merge_taps=merge_taps, merge_proj=merge_proj, second_gain=second_gain, second_shift=second_shift, second_up=second_up, second_down=second_down, final_gain=final_gain, final_shift=final_shift, cotangent=cotangent)


highest = lax.Precision.HIGHEST
epsilon = 1e-05

@jax.custom_vjp
def low(v):
    return lax.optimization_barrier(v.astype(jnp.bfloat16)).astype(jnp.float32)

@jax.custom_vjp
def low_back(v):
    return v

def low_keep(v):
    return (low(v), None)

def low_pass(kept, grad):
    return (grad,)

def back_keep(v):
    return (v, None)

def back_low(kept, grad):
    return (low(grad),)
low.defvjp(low_keep, low_pass)
low_back.defvjp(back_keep, back_low)

def matmul(left_op, right_op):
    return jnp.dot(left_op, right_op, precision=highest)

def norm_rows(rows_in, gain_vec, shift_vec):
    average = lax.optimization_barrier(jnp.mean(rows_in, -1, keepdims=True))
    center = rows_in - average
    spread = lax.optimization_barrier(jnp.mean(center * center, -1, keepdims=True))
    return center * lax.rsqrt(spread + epsilon) * gain_vec + shift_vec

def position_table(frames, model_width):
    distance = (frames - 1 - jnp.arange(2 * frames - 1, dtype=jnp.int32)).astype(jnp.float32)
    frequency = jnp.exp(jnp.arange(model_width // 2, dtype=jnp.int32).astype(jnp.float32) * (-2.0 * math.log(10000.0) / model_width))
    angles = distance[:, None] * frequency[None, :]
    return jnp.concatenate([jnp.sin(angles), jnp.cos(angles)], axis=1)

def shift_relative(scores_z, row_count, frames):
    head_count = scores_z.shape[0]
    span_width = scores_z.shape[2]
    flattened = scores_z.reshape(head_count, row_count * span_width)
    flattened = lax.slice_in_dim(flattened, row_count - 1, row_count - 1 + row_count * (span_width - 1), axis=1)
    return flattened.reshape(head_count, row_count, span_width - 1)[:, :, :frames]

def depthwise(signal, kernel_taps):
    half_width = kernel_taps.shape[0] // 2
    padded = jnp.pad(signal, ((half_width, half_width), (0, 0)))
    result = jnp.zeros_like(signal)
    for offset in range(kernel_taps.shape[0]):
        result = result + kernel_taps[offset] * padded[offset:offset + signal.shape[0]]
    return result

def feed_forward(rows_in, gain_vec, shift_vec, weight_in, weight_out):
    normed = low(norm_rows(rows_in, gain_vec, shift_vec))
    pre_act = low_back(matmul(normed, weight_in))
    hidden = low(jax.nn.silu(pre_act))
    return low_back(matmul(hidden, weight_out))

def layer(rows_in, params, live_mask):
    first_gain, first_shift, first_up, first_down, attn_gain, attn_shift, w_query, w_key, w_value, w_pos, bias_content, bias_position, attn_out, cgmlp_gain, cgmlp_shift, cgmlp_up, gate_gain, gate_shift, gate_taps, cgmlp_down, merge_taps, merge_proj, second_gain, second_shift, second_up, second_down, final_gain, final_shift = params
    frames = rows_in.shape[0]
    head_count = bias_content.shape[0]
    head_size = bias_content.shape[1]
    state = rows_in + 0.5 * feed_forward(rows_in, first_gain, first_shift, first_up, first_down)
    attn_in = low(norm_rows(state, attn_gain, attn_shift))
    queries = low_back(matmul(attn_in, w_query)).reshape(frames, head_count, head_size)
    keys_all = low(low_back(matmul(attn_in, w_key))).reshape(frames, head_count, head_size)
    values = low(low_back(matmul(attn_in, w_value))).reshape(frames, head_count, head_size)
    query_content = low(queries + bias_content[None])
    query_position = low(queries + bias_position[None])
    pos_table = low(position_table(frames, rows_in.shape[1]))
    pos_proj = low(low_back(matmul(pos_table, w_pos))).reshape(2 * frames - 1, head_count, head_size)
    content = jnp.einsum('ihe,jhe->hij', query_content, keys_all, precision=highest)
    relative = shift_relative(jnp.einsum('ihe,rhe->hir', query_position, pos_proj, precision=highest), frames, frames)
    scores = low_back((content + relative) * head_size ** (-0.5))
    scores = jnp.where(live_mask[None, None, :] > 0, scores, -1e+30)
    softmax_w = jax.nn.softmax(scores, axis=-1)
    attended = low(low_back(jnp.einsum('hij,jhe->ihe', low(softmax_w), values, precision=highest)))
    attended = attended.reshape(frames, head_count * head_size)
    branch_attn = low_back(matmul(attended, attn_out))
    cg_in = low(norm_rows(state, cgmlp_gain, cgmlp_shift))
    up_proj = low_back(matmul(cg_in, cgmlp_up.reshape(cgmlp_up.shape[0], -1))).reshape(frames, 2, -1)
    gelu_out = jax.nn.gelu(up_proj, approximate=False)
    gate_norm = norm_rows(gelu_out[:, 1], gate_gain, gate_shift) * live_mask[:, None]
    gate_out = low(gelu_out[:, 0] * depthwise(gate_norm, gate_taps))
    branch_gate = low_back(matmul(gate_out, cgmlp_down))
    joined = jnp.concatenate([branch_attn, branch_gate], axis=1)
    mixed = low(joined + depthwise(joined * live_mask[:, None], merge_taps))
    state = state + low_back(matmul(mixed, merge_proj))
    state = state + 0.5 * feed_forward(state, second_gain, second_shift, second_up, second_down)
    return norm_rows(state, final_gain, final_shift)

def reference(features, lengths, first_gain, first_shift, first_up, first_down, attn_gain, attn_shift, w_query, w_key, w_value, w_pos, bias_content, bias_position, attn_out, cgmlp_gain, cgmlp_shift, cgmlp_up, gate_gain, gate_shift, gate_taps, cgmlp_down, merge_taps, merge_proj, second_gain, second_shift, second_up, second_down, final_gain, final_shift, cotangent):
    params = tuple((array_in.astype(jnp.float32) for array_in in (first_gain, first_shift, first_up, first_down, attn_gain, attn_shift, w_query, w_key, w_value, w_pos, bias_content, bias_position, attn_out, cgmlp_gain, cgmlp_shift, cgmlp_up, gate_gain, gate_shift, gate_taps, cgmlp_down, merge_taps, merge_proj, second_gain, second_shift, second_up, second_down, final_gain, final_shift)))
    inputs = features.astype(jnp.float32).reshape(UTTS, LEN, D)
    cotangents = cotangent.astype(jnp.float32).reshape(UTTS, LEN, D)

    def one_utterance(carried, packed):
        rows_in, cot_rows, length_one = packed
        live_mask = (jnp.arange(LEN, dtype=jnp.int32) < length_one).astype(jnp.float32)
        encoded_rows, pullback = jax.vjp(lambda first_arg, second_arg: layer(first_arg, second_arg, live_mask), rows_in, params)
        grad_rows, grad_params = pullback(cot_rows)
        summed = jax.tree.map(lambda left_op, right_op: left_op + right_op, carried, grad_params)
        return (summed, (encoded_rows, grad_rows))
    zeros_init = jax.tree.map(jnp.zeros_like, params)
    grad_sums, (encoded, grad_inputs) = lax.scan(one_utterance, zeros_init, (inputs, cotangents, lengths))
    return (encoded.reshape(TOKENS, D), grad_inputs.reshape(TOKENS, D), grad_sums[0], grad_sums[1], grad_sums[2], grad_sums[3], grad_sums[4], grad_sums[5], grad_sums[6], grad_sums[7], grad_sums[8], grad_sums[9], grad_sums[10], grad_sums[11], grad_sums[12], grad_sums[13], grad_sums[14], grad_sums[15], grad_sums[16], grad_sums[17], grad_sums[18], grad_sums[19], grad_sums[20], grad_sums[21], grad_sums[22], grad_sums[23], grad_sums[24], grad_sums[25], grad_sums[26], grad_sums[27])
```

```python
import math

import jax
import jax.numpy as jnp
from jax import lax
from jax.experimental import pallas as pl
from jax.experimental.pallas import tpu as pltpu
from jax.sharding import Mesh, PartitionSpec as P

GATE = 1536
KERNEL = 31
D = 512
ROWS = 320
HALO = 16
GROUP = 4
EPS = 1e-05
F32 = jnp.float32
BF16 = jnp.bfloat16
MESH = pl.DeviceIdType.MESH
ANY = pl.BlockSpec(memory_space=pl.ANY)
VM = pl.BlockSpec(memory_space=pltpu.VMEM)


def product(a, b):
    return jnp.dot(a, b, preferred_element_type=F32)


def contract_rows(a, b):
    return lax.dot_general(a, b, (((0,), (0,)), ((), ())), preferred_element_type=F32)


def times_transpose(a, b):
    return lax.dot_general(a, b, (((1,), (1,)), ((), ())), preferred_element_type=F32)


def unit_norm(rows):
    center = rows - jnp.mean(rows, -1, keepdims=True)
    inverse = lax.rsqrt(jnp.mean(center * center, -1, keepdims=True) + EPS)
    return center * inverse, inverse


def norm_back(scaled, unit, inverse):
    inner = (
        scaled
        - jnp.mean(scaled, -1, keepdims=True)
        - unit * jnp.mean(scaled * unit, -1, keepdims=True)
    )
    return inner * inverse


def params(cid, vmem=48, **more):
    return pltpu.CompilerParams(
        collective_id=cid, has_side_effects=True, vmem_limit_bytes=vmem * 2**20, **more
    )


def ring():
    me = lax.axis_index("y")
    return me, lax.rem(me + 1, GROUP), lax.rem(me + GROUP - 1, GROUP), lax.rem(me + 2, GROUP)


def to_y(where):
    return dict(device_id={"y": where}, device_id_type=MESH)


def greet_ring(offsets):
    me = lax.axis_index("y")
    barrier = pltpu.get_barrier_semaphore()
    for off in offsets:
        pl.semaphore_signal(barrier, inc=1, **to_y(lax.rem(me + off, GROUP)))
    pl.semaphore_wait(barrier, len(offsets))


def gather_weights(shards, kinds, cid):
    count = len(shards)

    def kernel(*refs):
        srcs, dsts = refs[:count], refs[count : 2 * count]
        local_sem, send, recv = refs[2 * count :]
        me, up, down, _ = ring()
        across = lax.rem(me + 2, GROUP)
        core = lax.axis_index("core")
        barrier = pltpu.get_barrier_semaphore()
        pair = dict(device_id={"core": 1 - core}, device_id_type=MESH)
        pl.semaphore_signal(barrier, inc=1, **to_y(up))
        pl.semaphore_signal(barrier, inc=1, **to_y(down))
        pl.semaphore_signal(barrier, inc=1, **pair)
        pl.semaphore_wait(barrier, 3)

        def part(i, owner, start, size):
            rows, cols = shards[i].shape
            if kinds[i] == "rows":
                return dsts[i].at[pl.ds(owner * rows + start, size), :]
            return dsts[i].at[pl.ds(start, size), pl.ds(owner * cols, cols)]

        def half(i, owner):
            size = shards[i].shape[0] // 2
            return part(i, owner, core * size, size)

        def quarter(i, owner, q):
            size = shards[i].shape[0] // 4
            return part(i, owner, core * size * 2 + q * size, size)

        def remote(src, dst, i, k, where):
            return pltpu.make_async_remote_copy(
                src_ref=src, dst_ref=dst, send_sem=send.at[i, k], recv_sem=recv.at[i, k], **where
            )

        started = []
        first = []
        for i in range(count):
            size = shards[i].shape[0] // 2
            mine = srcs[i].at[pl.ds(core * size, size), :]
            a = remote(mine, half(i, me), i, 0, to_y(up))
            b = remote(mine, half(i, me), i, 1, to_y(down))
            a.start()
            b.start()
            first.append((a, b))
        locals_ = []
        for i in range(count):
            own = pltpu.make_async_copy(
                srcs[i], part(i, me, 0, shards[i].shape[0]), local_sem.at[i]
            )
            own.start()
            locals_.append(own)
        second = []
        for i in range(count):
            a, b = first[i]
            a.wait_recv()
            qa = remote(quarter(i, down, 0), quarter(i, down, 0), i, 2, to_y(up))
            qa.start()
            pa = remote(half(i, down), half(i, down), i, 4, pair)
            pa.start()
            b.wait_recv()
            qb = remote(quarter(i, up, 1), quarter(i, up, 1), i, 3, to_y(down))
            qb.start()
            pb = remote(half(i, up), half(i, up), i, 5, pair)
            pb.start()
            second.append((qa, qb))
            started += [pa, pb]
        for i in range(count):
            qa, qb = second[i]
            qa.wait_recv()
            qb.wait_recv()
            pc = remote(half(i, across), half(i, across), i, 6, pair)
            pc.start()
            started.append(pc)
        for i in range(count):
            for c in first[i] + second[i]:
                c.wait_send()
            locals_[i].wait()
        for c in started:
            c.wait()

    def full(shard, kind):
        rows, cols = shard.shape
        shape = (GROUP * rows, cols) if kind == "rows" else (rows, GROUP * cols)
        return jax.ShapeDtypeStruct(shape, shard.dtype)

    return pl.pallas_call(
        kernel,
        out_shape=[full(s, k) for s, k in zip(shards, kinds)],
        in_specs=[ANY] * count,
        out_specs=[ANY] * count,
        scratch_shapes=[
            pltpu.SemaphoreType.DMA((count,)),
            pltpu.SemaphoreType.DMA((count, 7)),
            pltpu.SemaphoreType.DMA((count, 7)),
        ],
        compiler_params=params(cid),
        name="gather_weights",
    )(*shards)


def split_copies(src, dst, send, recv, local_sem, to_heads):
    me = lax.axis_index("y")
    width = src.shape[1] // GROUP if to_heads else src.shape[1]

    def views(peer):
        if to_heads:
            return (
                src.at[:, pl.ds(pl.multiple_of(peer * width, width), width)],
                dst.at[pl.ds(pl.multiple_of(me * ROWS, ROWS), ROWS), :],
            )
        return (
            src.at[pl.ds(pl.multiple_of(peer * ROWS, ROWS), ROWS), :],
            dst.at[:, pl.ds(pl.multiple_of(me * width, width), width)],
        )

    copies = []
    for off in (2, 1, 3):
        peer = lax.rem(me + off, GROUP)
        s, d = views(peer)
        c = pltpu.make_async_remote_copy(
            src_ref=s, dst_ref=d, send_sem=send.at[off], recv_sem=recv.at[off], **to_y(peer)
        )
        c.start()
        copies.append(c)
    s, d = views(me)
    own = pltpu.make_async_copy(s, d, local_sem)
    own.start()
    copies.append(own)
    return copies


def exchange(x, to_heads, cid):
    rows, cols = x.shape
    shape = (rows * GROUP, cols // GROUP) if to_heads else (rows // GROUP, cols * GROUP)

    def kernel(x_ref, o_ref, send, recv, local_sem):
        greet_ring((1, 2, 3))
        for c in split_copies(x_ref, o_ref, send, recv, local_sem, to_heads):
            c.wait()

    return pl.pallas_call(
        kernel,
        out_shape=jax.ShapeDtypeStruct(shape, x.dtype),
        in_specs=[ANY],
        out_specs=ANY,
        scratch_shapes=[
            pltpu.SemaphoreType.DMA((GROUP,)),
            pltpu.SemaphoreType.DMA((GROUP,)),
            pltpu.SemaphoreType.DMA,
        ],
        compiler_params=params(cid),
        name="exchange",
    )(x)


def start_halo(edges, prev, nxt, send, recv):
    _, up, down, _ = ring()
    a = pltpu.make_async_remote_copy(
        src_ref=edges.at[1], dst_ref=prev, send_sem=send.at[0], recv_sem=recv.at[0], **to_y(up)
    )
    b = pltpu.make_async_remote_copy(
        src_ref=edges.at[0], dst_ref=nxt, send_sem=send.at[1], recv_sem=recv.at[1], **to_y(down)
    )
    a.start()
    b.start()
    return a, b


def lanes(b):
    return pl.ds(pl.multiple_of(b * 128, 128), 128)


CHUNK = 64


def conv_block(pad, taps, b, flip):
    weights = [taps[pl.ds(KERNEL - 1 - o if flip else o, 1), lanes(b)] for o in range(KERNEL)]
    for r in range(0, ROWS, CHUNK):
        total = None
        for o in range(KERNEL):
            term = weights[o] * pad[b, pl.ds(r + o + 1, CHUNK), :]
            total = term if total is None else total + term
        yield r, total


def taps_block(pad, g_pad, b, out):
    sums = [None] * KERNEL
    for r in range(0, ROWS, CHUNK):
        g = g_pad[b, pl.ds(HALO + r, CHUNK), :]
        for o in range(KERNEL):
            term = g * pad[b, pl.ds(r + o + 1, CHUNK), :]
            term = jnp.sum(term.reshape(CHUNK // 8, 8, 128), 0)
            sums[o] = term if sums[o] is None else sums[o] + term
    for o in range(KERNEL):
        out[pl.ds(o, 1), lanes(b)] = jnp.sum(sums[o], 0, keepdims=True)


def fill_middle(x_ref, pad, blocks):
    @pl.loop(0, blocks)
    def _(b):
        pad[b, pl.ds(HALO, ROWS), :] = x_ref[:, lanes(b)].astype(F32)


def fill_ends(prev, nxt, pad, blocks):
    me = lax.axis_index("y")
    has_prev = jnp.where(me > 0, 1.0, 0.0)
    has_next = jnp.where(me < GROUP - 1, 1.0, 0.0)

    @pl.loop(0, blocks)
    def _(b):
        pad[b, pl.ds(0, HALO), :] = prev[:, lanes(b)].astype(F32) * has_prev
        pad[b, pl.ds(HALO + ROWS, HALO), :] = nxt[:, lanes(b)].astype(F32) * has_next


def set_edges(x_ref, edges):
    edges[0] = x_ref[pl.ds(0, HALO), :].astype(BF16)
    edges[1] = x_ref[pl.ds(ROWS - HALO, HALO), :].astype(BF16)


def conv_forward(x, taps, cid, heads_in=None):
    cols = x.shape[1]
    blocks = cols // 128
    extra = heads_in is not None

    def kernel(*refs):
        if extra:
            x_ref, t_ref, h_ref, o_ref, prev, nxt, ho_ref = refs[:7]
            pad, edges, hs, hr, ss, sr, sl = refs[7:]
        else:
            x_ref, t_ref, o_ref, prev, nxt = refs[:5]
            pad, edges, hs, hr = refs[5:]
        greet_ring((1, 2, 3) if extra else (1, 3))
        set_edges(x_ref, edges)
        a, b = start_halo(edges, prev, nxt, hs, hr)
        waits = split_copies(h_ref, ho_ref, ss, sr, sl, True) if extra else []
        fill_middle(x_ref, pad, blocks)
        a.wait()
        b.wait()
        fill_ends(prev, nxt, pad, blocks)

        @pl.loop(0, blocks)
        def _(blk):
            for r, value in conv_block(pad, t_ref, blk, False):
                o_ref[pl.ds(r, CHUNK), lanes(blk)] = value

        for c in waits:
            c.wait()

    edge = jax.ShapeDtypeStruct((HALO, cols), BF16)
    outs = [jax.ShapeDtypeStruct((ROWS, cols), F32), edge, edge]
    ins = [x, taps]
    scratch = [
        pltpu.VMEM((blocks, ROWS + 2 * HALO, 128), F32),
        pltpu.VMEM((2, HALO, cols), BF16),
        pltpu.SemaphoreType.DMA((2,)),
        pltpu.SemaphoreType.DMA((2,)),
    ]
    in_specs, out_specs = [VM, VM], [VM, VM, VM]
    if extra:
        ins.append(heads_in)
        in_specs.append(ANY)
        outs.append(
            jax.ShapeDtypeStruct((ROWS * GROUP, heads_in.shape[1] // GROUP), heads_in.dtype)
        )
        out_specs.append(ANY)
        scratch += [
            pltpu.SemaphoreType.DMA((GROUP,)),
            pltpu.SemaphoreType.DMA((GROUP,)),
            pltpu.SemaphoreType.DMA,
        ]
    return pl.pallas_call(
        kernel,
        out_shape=outs,
        in_specs=in_specs,
        out_specs=out_specs,
        scratch_shapes=scratch,
        compiler_params=params(cid),
        name="conv_forward",
    )(*ins)


def conv_backward(g, x, x_prev, x_next, taps, cid, heads_in=None):
    cols = g.shape[1]
    blocks = cols // 128
    extra = heads_in is not None

    def kernel(*refs):
        g_ref, x_ref, xp_ref, xn_ref, t_ref = refs[:5]
        if extra:
            h_ref, o_ref, tg_ref, ho_ref = refs[5:9]
            g_pad, pad, edges, prev, nxt, hs, hr, ss, sr, sl = refs[9:]
        else:
            o_ref, tg_ref = refs[5:7]
            g_pad, pad, edges, prev, nxt, hs, hr = refs[7:]
        greet_ring((1, 2, 3) if extra else (1, 3))
        set_edges(g_ref, edges)
        a, b = start_halo(edges, prev, nxt, hs, hr)
        waits = split_copies(h_ref, ho_ref, ss, sr, sl, True) if extra else []
        fill_middle(g_ref, g_pad, blocks)
        fill_middle(x_ref, pad, blocks)
        fill_ends(xp_ref, xn_ref, pad, blocks)
        tg_ref[pl.ds(24, 8), :] = jnp.zeros((8, cols), F32)

        @pl.loop(0, blocks)
        def _(blk):
            taps_block(pad, g_pad, blk, tg_ref)

        a.wait()
        b.wait()
        fill_ends(prev, nxt, g_pad, blocks)

        @pl.loop(0, blocks)
        def _(blk):
            for r, value in conv_block(g_pad, t_ref, blk, True):
                o_ref[pl.ds(r, CHUNK), lanes(blk)] = value

        for c in waits:
            c.wait()

    outs = [jax.ShapeDtypeStruct((ROWS, cols), F32), jax.ShapeDtypeStruct((32, cols), F32)]
    ins = [g, x, x_prev, x_next, taps]
    scratch = [
        pltpu.VMEM((blocks, ROWS + 2 * HALO, 128), F32),
        pltpu.VMEM((blocks, ROWS + 2 * HALO, 128), F32),
        pltpu.VMEM((2, HALO, cols), BF16),
        pltpu.VMEM((HALO, cols), BF16),
        pltpu.VMEM((HALO, cols), BF16),
        pltpu.SemaphoreType.DMA((2,)),
        pltpu.SemaphoreType.DMA((2,)),
    ]
    in_specs, out_specs = [VM] * 5, [VM, VM]
    if extra:
        ins.append(heads_in)
        in_specs.append(ANY)
        outs.append(
            jax.ShapeDtypeStruct((ROWS * GROUP, heads_in.shape[1] // GROUP), heads_in.dtype)
        )
        out_specs.append(ANY)
        scratch += [
            pltpu.SemaphoreType.DMA((GROUP,)),
            pltpu.SemaphoreType.DMA((GROUP,)),
            pltpu.SemaphoreType.DMA,
        ]
    return pl.pallas_call(
        kernel,
        out_shape=outs,
        in_specs=in_specs,
        out_specs=out_specs,
        scratch_shapes=scratch,
        compiler_params=params(cid),
        name="conv_backward",
    )(*ins)


def position_factors(frames, width):
    frequency = jnp.exp(
        jnp.arange(width // 2, dtype=jnp.int32).astype(F32) * (-2.0 * math.log(10000.0) / width)
    )
    coarse = (32.0 * jnp.arange(frames // 32, dtype=jnp.int32).astype(F32))[:, None] * frequency
    fine = jnp.arange(32, dtype=jnp.int32).astype(F32)[:, None] * frequency
    sa, ca = jnp.sin(coarse)[:, None], jnp.cos(coarse)[:, None]
    sb, cb = jnp.sin(fine)[None], jnp.cos(fine)[None]
    sin = (sa * cb + ca * sb).reshape(frames, width // 2)
    cos = (ca * cb - sa * sb).reshape(frames, width // 2)
    return sin, cos


def head_mask(h):
    column = lax.broadcasted_iota(jnp.int32, (1, 128), 1)
    return jnp.where((column >= 64 * h) & (column < 64 * h + 64), 1.0, 0.0)


def rotated(query, sin, cos, w_pos):
    z = times_transpose(query, w_pos)
    zs, zc = z[:, : D // 2], z[:, D // 2 :]
    return jnp.concatenate([zc * sin - zs * cos, zs * sin + zc * cos], axis=1).astype(BF16)


def attention_forward(qkv, w_pos, biases, mask, table, sin, cos):
    frames = qkv.shape[0]

    def kernel(q_ref, k_ref, v_ref, wp_ref, b_ref, m_ref, t_ref, s_ref, c_ref, o_ref, p_ref):
        query = q_ref[...].astype(F32)
        total = jnp.zeros((ROWS, 128), F32)
        for h in range(2):
            keep = head_mask(h)
            content = ((query + b_ref[pl.ds(0, 1), :]) * (0.125 * keep)).astype(BF16)
            position = ((query + b_ref[pl.ds(1, 1), :]) * (0.125 * keep)).astype(BF16)
            turned = rotated(position, s_ref[...], c_ref[...], wp_ref[...])
            scores = times_transpose(turned, t_ref[...]) + times_transpose(content, k_ref[...])
            scores = scores + m_ref[...]
            top = jnp.max(scores, -1, keepdims=True)
            weights = jnp.exp(scores - top)
            weights = (weights * (1.0 / jnp.sum(weights, -1, keepdims=True))).astype(BF16)
            p_ref[h] = weights
            total = total + product(weights, v_ref[...]) * keep
        o_ref[...] = total.astype(BF16)

    def whole(shape):
        return pl.BlockSpec(shape, lambda i: (0,) * len(shape))

    return pl.pallas_call(
        kernel,
        grid=(frames // ROWS,),
        in_specs=[
            pl.BlockSpec((ROWS, 128), lambda i: (i, 0)),
            pl.BlockSpec((frames, 128), lambda i: (0, 1)),
            pl.BlockSpec((frames, 128), lambda i: (0, 2)),
            whole((D, 128)),
            whole((8, 128)),
            whole((1, frames)),
            whole((frames, D)),
            pl.BlockSpec((ROWS, D // 2), lambda i: (i, 0)),
            pl.BlockSpec((ROWS, D // 2), lambda i: (i, 0)),
        ],
        out_specs=[
            pl.BlockSpec((ROWS, 128), lambda i: (i, 0)),
            pl.BlockSpec((2, ROWS, frames), lambda i: (0, i, 0)),
        ],
        out_shape=[
            jax.ShapeDtypeStruct((frames, 128), BF16),
            jax.ShapeDtypeStruct((2, frames, frames), BF16),
        ],
        compiler_params=pltpu.CompilerParams(
            dimension_semantics=("arbitrary",), vmem_limit_bytes=48 * 2**20
        ),
        name="attention_forward",
    )(qkv, qkv, qkv, w_pos, biases, mask, table, sin, cos)


def attention_backward(qkv, weights, attended, g_attended, w_pos, biases, table, sin, cos):
    frames = qkv.shape[0]
    steps = frames // ROWS

    def kernel(
        q_ref, k_ref, v_ref, p_ref, a_ref, ga_ref, wp_ref, b_ref, t_ref, s_ref, c_ref,
        gq_ref, gk_ref, gv_ref, gw_ref, gb_ref, gk_acc, gv_acc,
    ):
        step = pl.program_id(0)

        @pl.when(step == 0)
        def _():
            gk_acc[...] = jnp.zeros_like(gk_acc)
            gv_acc[...] = jnp.zeros_like(gv_acc)
            gw_ref[...] = jnp.zeros_like(gw_ref)
            gb_ref[...] = jnp.zeros_like(gb_ref)

        query = q_ref[...].astype(F32)
        g_out = ga_ref[...]
        dots = g_out.astype(F32) * a_ref[...].astype(F32)
        sin_, cos_ = s_ref[...], c_ref[...]
        g_content = jnp.zeros((ROWS, 128), F32)
        g_position = jnp.zeros((ROWS, 128), F32)
        for h in range(2):
            keep = head_mask(h)
            content = ((query + b_ref[pl.ds(0, 1), :]) * (0.125 * keep)).astype(BF16)
            position = ((query + b_ref[pl.ds(1, 1), :]) * (0.125 * keep)).astype(BF16)
            g_head = (g_out.astype(F32) * keep).astype(BF16)
            p = p_ref[h]
            g_weights = times_transpose(g_head, v_ref[...])
            inner = jnp.sum(dots * keep, -1, keepdims=True)
            g_scores = (p.astype(F32) * (g_weights - inner)).astype(BF16)
            gv_acc[...] += contract_rows(g_head, p)
            gk_acc[...] += contract_rows(content, g_scores)
            g_content = g_content + product(g_scores, k_ref[...]) * keep
            turned = product(g_scores, t_ref[...])
            ts, tc = turned[:, : D // 2], turned[:, D // 2 :]
            g_z = jnp.concatenate([tc * sin_ - ts * cos_, ts * sin_ + tc * cos_], axis=1)
            g_z = g_z.astype(BF16)
            g_position = g_position + product(g_z, wp_ref[...]) * keep
            gw_ref[...] += contract_rows(g_z, position)
        g_content = g_content * 0.125
        g_position = g_position * 0.125
        gq_ref[...] = (g_content + g_position).astype(BF16)
        gb_ref[pl.ds(0, 1), :] += jnp.sum(g_content, 0, keepdims=True)
        gb_ref[pl.ds(1, 1), :] += jnp.sum(g_position, 0, keepdims=True)

        @pl.when(step == steps - 1)
        def _():
            gk_ref[...] = gk_acc[...].T.astype(BF16)
            gv_ref[...] = gv_acc[...].T.astype(BF16)

    def whole(shape):
        return pl.BlockSpec(shape, lambda i: (0,) * len(shape))

    rows = pl.BlockSpec((ROWS, 128), lambda i: (i, 0))
    return pl.pallas_call(
        kernel,
        grid=(steps,),
        in_specs=[
            rows,
            pl.BlockSpec((frames, 128), lambda i: (0, 1)),
            pl.BlockSpec((frames, 128), lambda i: (0, 2)),
            pl.BlockSpec((2, ROWS, frames), lambda i: (0, i, 0)),
            rows,
            rows,
            whole((D, 128)),
            whole((8, 128)),
            whole((frames, D)),
            pl.BlockSpec((ROWS, D // 2), lambda i: (i, 0)),
            pl.BlockSpec((ROWS, D // 2), lambda i: (i, 0)),
        ],
        out_specs=[rows, whole((frames, 128)), whole((frames, 128)), whole((D, 128)), whole((8, 128))],
        out_shape=[
            jax.ShapeDtypeStruct((frames, 128), BF16),
            jax.ShapeDtypeStruct((frames, 128), BF16),
            jax.ShapeDtypeStruct((frames, 128), BF16),
            jax.ShapeDtypeStruct((D, 128), F32),
            jax.ShapeDtypeStruct((8, 128), F32),
        ],
        scratch_shapes=[pltpu.VMEM((128, frames), F32), pltpu.VMEM((128, frames), F32)],
        compiler_params=pltpu.CompilerParams(
            dimension_semantics=("arbitrary",), vmem_limit_bytes=48 * 2**20
        ),
        name="attention_backward",
    )(qkv, qkv, qkv, weights, attended, g_attended, w_pos, biases, table, sin, cos)


def local(
    features,
    lengths,
    first_gain,
    first_shift,
    first_up,
    first_down,
    attn_gain,
    attn_shift,
    w_query,
    w_key,
    w_value,
    w_pos,
    bias_content,
    bias_position,
    attn_out,
    cgmlp_gain,
    cgmlp_shift,
    cgmlp_up,
    gate_gain,
    gate_shift,
    gate_taps,
    cgmlp_down,
    merge_taps,
    merge_proj,
    second_gain,
    second_shift,
    second_up,
    second_down,
    final_gain,
    final_shift,
    cotangent,
):
    frames = ROWS * GROUP
    channels = gate_gain.shape[0]
    me = lax.axis_index("y")
    length = lengths[0]
    live = (jnp.arange(ROWS, dtype=jnp.int32) + me * ROWS < length).astype(F32)[:, None]
    mask = jnp.where(jnp.arange(frames, dtype=jnp.int32) < length, 0.0, -1e30)[None].astype(F32)
    vec = lambda v: v.astype(F32)[None]
    sin, cos = position_factors(frames, D)
    table = jnp.concatenate([sin, cos], axis=1).astype(BF16)
    biases = jnp.concatenate(
        [
            bias_content.astype(F32).reshape(1, 128),
            bias_position.astype(F32).reshape(1, 128),
            jnp.zeros((6, 128), F32),
        ]
    )
    small = jnp.concatenate(
        [gate_taps, gate_gain[None], gate_shift[None], jnp.zeros((31, channels), BF16)]
    )
    wide = jnp.concatenate([w_query, w_key, w_value], axis=1)
    halves = cgmlp_up[:, 0], cgmlp_up[:, 1]
    (up1, down1, qkv_w, cg0, cg1, small_all, out_w, cg_down, up2, down2) = gather_weights(
        (
            first_up, first_down, wide, halves[0], halves[1], small, attn_out, cgmlp_down,
            second_up, second_down,
        ),
        ("cols", "rows", "cols", "cols", "cols", "cols", "rows", "rows", "cols", "rows"),
        0,
    )
    small_f = small_all.astype(F32)
    gate_taps_f = small_f[:32]
    gate_gain_f, gate_shift_f = small_f[31:32], small_f[32:33]
    merge_taps_f = jnp.pad(merge_taps.astype(F32), ((0, 1), (0, 0)))

    start = features.astype(F32)
    u1, inv1 = unit_norm(start)
    in1 = (u1 * vec(first_gain) + vec(first_shift)).astype(BF16)
    act1 = product(in1, up1)
    hid1 = (act1 * jax.nn.sigmoid(act1)).astype(BF16)
    middle = start + 0.5 * product(hid1, down1)
    u2, inv2 = unit_norm(middle)
    attn_in = (u2 * vec(attn_gain) + vec(attn_shift)).astype(BF16)
    cg_in = (u2 * vec(cgmlp_gain) + vec(cgmlp_shift)).astype(BF16)
    qkv_rows = product(attn_in, qkv_w).astype(BF16)
    c0 = product(cg_in, cg0)
    c1 = product(cg_in, cg1)
    root = 1.0 / math.sqrt(2.0)
    phi0 = 0.5 * (1.0 + lax.erf(c0 * root))
    phi1 = 0.5 * (1.0 + lax.erf(c1 * root))
    half0 = c0 * phi0
    ug, invg = unit_norm(c1 * phi1)
    gate_norm = (ug * gate_gain_f + gate_shift_f) * live
    gate_conv, gn_prev, gn_next, qkv = conv_forward(gate_norm, gate_taps_f, 1, qkv_rows)
    gate_out = (half0 * gate_conv).astype(BF16)
    attended, weights = attention_forward(qkv, w_pos, biases, mask, table, sin, cos)
    attended_rows = exchange(attended, False, 2)
    joined = jnp.concatenate([product(attended_rows, out_w), product(gate_out, cg_down)], axis=1)
    joined_live = joined * live
    merge_conv, jl_prev, jl_next = conv_forward(joined_live, merge_taps_f, 3)
    mixed = (joined + merge_conv).astype(BF16)
    merged = middle + product(mixed, merge_proj)
    u3, inv3 = unit_norm(merged)
    in2 = (u3 * vec(second_gain) + vec(second_shift)).astype(BF16)
    act2 = product(in2, up2)
    sig2 = jax.nn.sigmoid(act2)
    hid2 = (act2 * sig2).astype(BF16)
    last = merged + 0.5 * product(hid2, down2)
    u4, inv4 = unit_norm(last)
    encoded = u4 * vec(final_gain) + vec(final_shift)

    cot = cotangent.astype(F32)
    g_final_gain = jnp.sum(cot * u4, 0)
    g_final_shift = jnp.sum(cot, 0)
    g_last = norm_back(cot * vec(final_gain), u4, inv4)
    gy2 = (0.5 * g_last).astype(BF16)
    g_down2 = contract_rows(hid2, gy2)
    g_act2 = (times_transpose(gy2, down2) * sig2 * (1.0 + act2 * (1.0 - sig2))).astype(BF16)
    g_up2 = contract_rows(in2, g_act2)
    g_in2 = times_transpose(g_act2, up2)
    g_second_gain = jnp.sum(g_in2 * u3, 0)
    g_second_shift = jnp.sum(g_in2, 0)
    g_merged = g_last + norm_back(g_in2 * vec(second_gain), u3, inv3)
    gm = g_merged.astype(BF16)
    g_merge_proj = contract_rows(mixed, gm)
    gx = times_transpose(gm, merge_proj)
    merge_back, g_merge_taps = conv_backward(gx, joined_live, jl_prev, jl_next, merge_taps_f, 4)
    g_joined = (gx + live * merge_back).astype(BF16)
    ga, gb = g_joined[:, :D], g_joined[:, D:]
    g_attn_out = contract_rows(attended_rows, ga)
    g_attended_rows = times_transpose(ga, out_w).astype(BF16)
    g_cg_down = contract_rows(gate_out, gb)
    gg = times_transpose(gb, cg_down)
    g_conv = gg * half0
    g_norm_raw, g_gate_taps, g_attended = conv_backward(
        g_conv, gate_norm, gn_prev, gn_next, gate_taps_f, 5, g_attended_rows
    )
    gq, gk, gv, g_w_pos, g_bias = attention_backward(
        qkv, weights, attended, g_attended, w_pos, biases, table, sin, cos
    )
    g_qkv = exchange(jnp.concatenate([gq, gk, gv], axis=1), False, 6)
    g_gate_norm = g_norm_raw * live
    g_gate_gain = jnp.sum(g_gate_norm * ug, 0)
    g_gate_shift = jnp.sum(g_gate_norm, 0)
    g_half1 = norm_back(g_gate_norm * gate_gain_f, ug, invg)
    density = 1.0 / math.sqrt(2.0 * math.pi)
    g_c0 = (gg * gate_conv * (phi0 + c0 * (density * jnp.exp(-0.5 * c0 * c0)))).astype(BF16)
    g_c1 = (g_half1 * (phi1 + c1 * (density * jnp.exp(-0.5 * c1 * c1)))).astype(BF16)
    g_cg0 = contract_rows(cg_in, g_c0)
    g_cg1 = contract_rows(cg_in, g_c1)
    g_cg_in = times_transpose(g_c0, cg0) + times_transpose(g_c1, cg1)
    g_attn_in = times_transpose(g_qkv, qkv_w)
    g_wide = contract_rows(attn_in, g_qkv)
    g_attn_gain = jnp.sum(g_attn_in * u2, 0)
    g_attn_shift = jnp.sum(g_attn_in, 0)
    g_cgmlp_gain = jnp.sum(g_cg_in * u2, 0)
    g_cgmlp_shift = jnp.sum(g_cg_in, 0)
    g_middle = g_merged + norm_back(
        g_attn_in * vec(attn_gain) + g_cg_in * vec(cgmlp_gain), u2, inv2
    )
    gy1 = (0.5 * g_middle).astype(BF16)
    sig1 = jax.nn.sigmoid(act1)
    g_down1 = contract_rows(hid1, gy1)
    g_act1 = (times_transpose(gy1, down1) * sig1 * (1.0 + act1 * (1.0 - sig1))).astype(BF16)
    g_up1 = contract_rows(in1, g_act1)
    g_in1 = times_transpose(g_act1, up1)
    g_first_gain = jnp.sum(g_in1 * u1, 0)
    g_first_shift = jnp.sum(g_in1, 0)
    g_features = g_middle + norm_back(g_in1 * vec(first_gain), u1, inv1)

    every = ("z", "x", "core", "y")
    groups = ("z", "x", "core")

    def scatter(a, dim):
        return lax.psum_scatter(a.astype(BF16), "y", scatter_dimension=dim, tiled=True)

    g_small = jnp.concatenate([g_gate_taps[:31], g_gate_gain[None], g_gate_shift[None]])
    owned = (
        scatter(g_up1, 1),
        scatter(g_down1, 0),
        scatter(g_wide, 1),
        scatter(g_cg0, 1),
        scatter(g_cg1, 1),
        scatter(g_small, 1),
        scatter(g_attn_out, 0),
        scatter(g_cg_down, 0),
        scatter(g_up2, 1),
        scatter(g_down2, 0),
        g_w_pos.astype(BF16),
        g_bias.astype(BF16),
    )
    owned = [a.astype(F32) for a in lax.psum(owned, groups)]
    (d_up1, d_down1, d_wide, d_cg0, d_cg1, d_small, d_out, d_cg_down, d_up2, d_down2, d_pos, d_bias) = owned
    shared = lax.psum(
        (
            g_first_gain, g_first_shift, g_attn_gain, g_attn_shift, g_cgmlp_gain, g_cgmlp_shift,
            g_merge_taps[:31], g_merge_proj, g_second_gain, g_second_shift, g_final_gain,
            g_final_shift,
        ),
        every,
    )
    return (
        encoded,
        g_features,
        shared[0],
        shared[1],
        d_up1,
        d_down1,
        shared[2],
        shared[3],
        d_wide[:, :128],
        d_wide[:, 128:256],
        d_wide[:, 256:],
        d_pos,
        d_bias[0].reshape(2, 64),
        d_bias[1].reshape(2, 64),
        d_out,
        shared[4],
        shared[5],
        jnp.stack([d_cg0, d_cg1], axis=1),
        d_small[31],
        d_small[32],
        d_small[:31],
        d_cg_down,
        shared[6],
        shared[7],
        shared[8],
        shared[9],
        d_up2,
        d_down2,
        shared[10],
        shared[11],
    )


def solution(mesh):
    devices = mesh.devices.reshape(4, 4, 2, GROUP)
    fine = Mesh(devices, ("z", "x", "core", "y"))
    rows = P(("z", "x", "core", "y"), None)
    column, row = P(None, "y"), P("y", None)
    placed = (
        rows,
        P(("z", "x", "core")),
        P(),
        P(),
        column,
        row,
        P(),
        P(),
        column,
        column,
        column,
        column,
        row,
        row,
        row,
        P(),
        P(),
        P(None, None, "y"),
        P("y"),
        P("y"),
        column,
        row,
        P(),
        P(),
        P(),
        P(),
        column,
        row,
        P(),
        P(),
        rows,
    )
    return jax.shard_map(
        local,
        mesh=fine,
        in_specs=placed,
        out_specs=(rows,) + (rows,) + placed[2:30],
        check_vma=False,
    )
```

```python
import math

import jax
import jax.numpy as jnp
from jax import lax
from jax.experimental import pallas as pl
from jax.experimental.pallas import tpu as pltpu
from jax.sharding import Mesh, PartitionSpec as P

GATE = 1536
KERNEL = 31
D = 512
ROWS = 320
HALO = 16
GROUP = 4
EPS = 1e-05
F32 = jnp.float32
BF16 = jnp.bfloat16
MESH = pl.DeviceIdType.MESH
ANY = pl.BlockSpec(memory_space=pl.ANY)
VM = pl.BlockSpec(memory_space=pltpu.VMEM)


def product(a, b):
    return jnp.dot(a, b, preferred_element_type=F32)


def contract_rows(a, b):
    return lax.dot_general(a, b, (((0,), (0,)), ((), ())), preferred_element_type=F32)


def times_transpose(a, b):
    return lax.dot_general(a, b, (((1,), (1,)), ((), ())), preferred_element_type=F32)


def unit_norm(rows):
    center = rows - jnp.mean(rows, -1, keepdims=True)
    inverse = lax.rsqrt(jnp.mean(center * center, -1, keepdims=True) + EPS)
    return center * inverse, inverse


def norm_back(scaled, unit, inverse):
    inner = (
        scaled
        - jnp.mean(scaled, -1, keepdims=True)
        - unit * jnp.mean(scaled * unit, -1, keepdims=True)
    )
    return inner * inverse


def params(cid, vmem=48, **more):
    return pltpu.CompilerParams(
        collective_id=cid, has_side_effects=True, vmem_limit_bytes=vmem * 2**20, **more
    )


def ring():
    me = lax.axis_index("y")
    return me, lax.rem(me + 1, GROUP), lax.rem(me + GROUP - 1, GROUP), lax.rem(me + 2, GROUP)


def to_y(where):
    return dict(device_id={"y": where}, device_id_type=MESH)


def greet_ring(offsets):
    me = lax.axis_index("y")
    barrier = pltpu.get_barrier_semaphore()
    for off in offsets:
        pl.semaphore_signal(barrier, inc=1, **to_y(lax.rem(me + off, GROUP)))
    pl.semaphore_wait(barrier, len(offsets))


def gather_weights(shards, kinds, cid):
    count = len(shards)

    def kernel(*refs):
        srcs, dsts = refs[:count], refs[count : 2 * count]
        local_sem, send, recv = refs[2 * count :]
        me, up, down, _ = ring()
        across = lax.rem(me + 2, GROUP)
        core = lax.axis_index("core")
        barrier = pltpu.get_barrier_semaphore()
        pair = dict(device_id={"core": 1 - core}, device_id_type=MESH)
        pl.semaphore_signal(barrier, inc=1, **to_y(up))
        pl.semaphore_signal(barrier, inc=1, **to_y(down))
        pl.semaphore_signal(barrier, inc=1, **pair)
        pl.semaphore_wait(barrier, 3)

        def part(i, owner, start, size):
            rows, cols = shards[i].shape
            if kinds[i] == "rows":
                return dsts[i].at[pl.ds(owner * rows + start, size), :]
            return dsts[i].at[pl.ds(start, size), pl.ds(owner * cols, cols)]

        def half(i, owner):
            size = shards[i].shape[0] // 2
            return part(i, owner, core * size, size)

        def quarter(i, owner, q):
            size = shards[i].shape[0] // 4
            return part(i, owner, core * size * 2 + q * size, size)

        def remote(src, dst, i, k, where):
            return pltpu.make_async_remote_copy(
                src_ref=src, dst_ref=dst, send_sem=send.at[i, k], recv_sem=recv.at[i, k], **where
            )

        started = []
        first = []
        for i in range(count):
            size = shards[i].shape[0] // 2
            mine = srcs[i].at[pl.ds(core * size, size), :]
            a = remote(mine, half(i, me), i, 0, to_y(up))
            b = remote(mine, half(i, me), i, 1, to_y(down))
            a.start()
            b.start()
            first.append((a, b))
        locals_ = []
        for i in range(count):
            own = pltpu.make_async_copy(
                srcs[i], part(i, me, 0, shards[i].shape[0]), local_sem.at[i]
            )
            own.start()
            locals_.append(own)
        second = []
        for i in range(count):
            a, b = first[i]
            a.wait_recv()
            qa = remote(quarter(i, down, 0), quarter(i, down, 0), i, 2, to_y(up))
            qa.start()
            pa = remote(half(i, down), half(i, down), i, 4, pair)
            pa.start()
            b.wait_recv()
            qb = remote(quarter(i, up, 1), quarter(i, up, 1), i, 3, to_y(down))
            qb.start()
            pb = remote(half(i, up), half(i, up), i, 5, pair)
            pb.start()
            second.append((qa, qb))
            started += [pa, pb]
        for i in range(count):
            qa, qb = second[i]
            qa.wait_recv()
            qb.wait_recv()
            pc = remote(half(i, across), half(i, across), i, 6, pair)
            pc.start()
            started.append(pc)
        for i in range(count):
            for c in first[i] + second[i]:
                c.wait_send()
            locals_[i].wait()
        for c in started:
            c.wait()

    def full(shard, kind):
        rows, cols = shard.shape
        shape = (GROUP * rows, cols) if kind == "rows" else (rows, GROUP * cols)
        return jax.ShapeDtypeStruct(shape, shard.dtype)

    return pl.pallas_call(
        kernel,
        out_shape=[full(s, k) for s, k in zip(shards, kinds)],
        in_specs=[ANY] * count,
        out_specs=[ANY] * count,
        scratch_shapes=[
            pltpu.SemaphoreType.DMA((count,)),
            pltpu.SemaphoreType.DMA((count, 7)),
            pltpu.SemaphoreType.DMA((count, 7)),
        ],
        compiler_params=params(cid),
        name="gather_weights",
    )(*shards)


def split_copies(src, dst, send, recv, local_sem, to_heads):
    me = lax.axis_index("y")
    width = src.shape[1] // GROUP if to_heads else src.shape[1]

    def views(peer):
        if to_heads:
            return (
                src.at[:, pl.ds(pl.multiple_of(peer * width, width), width)],
                dst.at[pl.ds(pl.multiple_of(me * ROWS, ROWS), ROWS), :],
            )
        return (
            src.at[pl.ds(pl.multiple_of(peer * ROWS, ROWS), ROWS), :],
            dst.at[:, pl.ds(pl.multiple_of(me * width, width), width)],
        )

    copies = []
    for off in (2, 1, 3):
        peer = lax.rem(me + off, GROUP)
        s, d = views(peer)
        c = pltpu.make_async_remote_copy(
            src_ref=s, dst_ref=d, send_sem=send.at[off], recv_sem=recv.at[off], **to_y(peer)
        )
        c.start()
        copies.append(c)
    s, d = views(me)
    own = pltpu.make_async_copy(s, d, local_sem)
    own.start()
    copies.append(own)
    return copies


def exchange(x, to_heads, cid):
    rows, cols = x.shape
    shape = (rows * GROUP, cols // GROUP) if to_heads else (rows // GROUP, cols * GROUP)

    def kernel(x_ref, o_ref, send, recv, local_sem):
        greet_ring((1, 2, 3))
        for c in split_copies(x_ref, o_ref, send, recv, local_sem, to_heads):
            c.wait()

    return pl.pallas_call(
        kernel,
        out_shape=jax.ShapeDtypeStruct(shape, x.dtype),
        in_specs=[ANY],
        out_specs=ANY,
        scratch_shapes=[
            pltpu.SemaphoreType.DMA((GROUP,)),
            pltpu.SemaphoreType.DMA((GROUP,)),
            pltpu.SemaphoreType.DMA,
        ],
        compiler_params=params(cid),
        name="exchange",
    )(x)


def start_halo(edges, prev, nxt, send, recv):
    _, up, down, _ = ring()
    a = pltpu.make_async_remote_copy(
        src_ref=edges.at[1], dst_ref=prev, send_sem=send.at[0], recv_sem=recv.at[0], **to_y(up)
    )
    b = pltpu.make_async_remote_copy(
        src_ref=edges.at[0], dst_ref=nxt, send_sem=send.at[1], recv_sem=recv.at[1], **to_y(down)
    )
    a.start()
    b.start()
    return a, b


def lanes(b):
    return pl.ds(pl.multiple_of(b * 128, 128), 128)


CHUNK = 64


def conv_block(pad, taps, b, flip):
    weights = [taps[pl.ds(KERNEL - 1 - o if flip else o, 1), lanes(b)] for o in range(KERNEL)]
    for r in range(0, ROWS, CHUNK):
        total = None
        for o in range(KERNEL):
            term = weights[o] * pad[b, pl.ds(r + o + 1, CHUNK), :]
            total = term if total is None else total + term
        yield r, total


def taps_block(pad, g_pad, b, out):
    sums = [None] * KERNEL
    for r in range(0, ROWS, CHUNK):
        g = g_pad[b, pl.ds(HALO + r, CHUNK), :]
        for o in range(KERNEL):
            term = g * pad[b, pl.ds(r + o + 1, CHUNK), :]
            term = jnp.sum(term.reshape(CHUNK // 8, 8, 128), 0)
            sums[o] = term if sums[o] is None else sums[o] + term
    for o in range(KERNEL):
        out[pl.ds(o, 1), lanes(b)] = jnp.sum(sums[o], 0, keepdims=True)


def fill_middle(x_ref, pad, blocks):
    @pl.loop(0, blocks)
    def _(b):
        pad[b, pl.ds(HALO, ROWS), :] = x_ref[:, lanes(b)].astype(F32)


def fill_ends(prev, nxt, pad, blocks):
    me = lax.axis_index("y")
    has_prev = jnp.where(me > 0, 1.0, 0.0)
    has_next = jnp.where(me < GROUP - 1, 1.0, 0.0)

    @pl.loop(0, blocks)
    def _(b):
        pad[b, pl.ds(0, HALO), :] = prev[:, lanes(b)].astype(F32) * has_prev
        pad[b, pl.ds(HALO + ROWS, HALO), :] = nxt[:, lanes(b)].astype(F32) * has_next


def set_edges(x_ref, edges):
    edges[0] = x_ref[pl.ds(0, HALO), :].astype(BF16)
    edges[1] = x_ref[pl.ds(ROWS - HALO, HALO), :].astype(BF16)


def conv_forward(x, taps, cid, heads_in=None):
    cols = x.shape[1]
    blocks = cols // 128
    extra = heads_in is not None

    def kernel(*refs):
        if extra:
            x_ref, t_ref, h_ref, o_ref, prev, nxt, ho_ref = refs[:7]
            pad, edges, hs, hr, ss, sr, sl = refs[7:]
        else:
            x_ref, t_ref, o_ref, prev, nxt = refs[:5]
            pad, edges, hs, hr = refs[5:]
        greet_ring((1, 2, 3) if extra else (1, 3))
        set_edges(x_ref, edges)
        a, b = start_halo(edges, prev, nxt, hs, hr)
        waits = split_copies(h_ref, ho_ref, ss, sr, sl, True) if extra else []
        fill_middle(x_ref, pad, blocks)
        a.wait()
        b.wait()
        fill_ends(prev, nxt, pad, blocks)

        @pl.loop(0, blocks)
        def _(blk):
            for r, value in conv_block(pad, t_ref, blk, False):
                o_ref[pl.ds(r, CHUNK), lanes(blk)] = value

        for c in waits:
            c.wait()

    edge = jax.ShapeDtypeStruct((HALO, cols), BF16)
    outs = [jax.ShapeDtypeStruct((ROWS, cols), F32), edge, edge]
    ins = [x, taps]
    scratch = [
        pltpu.VMEM((blocks, ROWS + 2 * HALO, 128), F32),
        pltpu.VMEM((2, HALO, cols), BF16),
        pltpu.SemaphoreType.DMA((2,)),
        pltpu.SemaphoreType.DMA((2,)),
    ]
    in_specs, out_specs = [VM, VM], [VM, VM, VM]
    if extra:
        ins.append(heads_in)
        in_specs.append(ANY)
        outs.append(
            jax.ShapeDtypeStruct((ROWS * GROUP, heads_in.shape[1] // GROUP), heads_in.dtype)
        )
        out_specs.append(ANY)
        scratch += [
            pltpu.SemaphoreType.DMA((GROUP,)),
            pltpu.SemaphoreType.DMA((GROUP,)),
            pltpu.SemaphoreType.DMA,
        ]
    return pl.pallas_call(
        kernel,
        out_shape=outs,
        in_specs=in_specs,
        out_specs=out_specs,
        scratch_shapes=scratch,
        compiler_params=params(cid),
        name="conv_forward",
    )(*ins)


def conv_backward(g, x, x_prev, x_next, taps, cid, heads_in=None):
    cols = g.shape[1]
    blocks = cols // 128
    extra = heads_in is not None

    def kernel(*refs):
        g_ref, x_ref, xp_ref, xn_ref, t_ref = refs[:5]
        if extra:
            h_ref, o_ref, tg_ref, ho_ref = refs[5:9]
            g_pad, pad, edges, prev, nxt, hs, hr, ss, sr, sl = refs[9:]
        else:
            o_ref, tg_ref = refs[5:7]
            g_pad, pad, edges, prev, nxt, hs, hr = refs[7:]
        greet_ring((1, 2, 3) if extra else (1, 3))
        set_edges(g_ref, edges)
        a, b = start_halo(edges, prev, nxt, hs, hr)
        waits = split_copies(h_ref, ho_ref, ss, sr, sl, True) if extra else []
        fill_middle(g_ref, g_pad, blocks)
        fill_middle(x_ref, pad, blocks)
        fill_ends(xp_ref, xn_ref, pad, blocks)
        tg_ref[pl.ds(24, 8), :] = jnp.zeros((8, cols), F32)

        @pl.loop(0, blocks)
        def _(blk):
            taps_block(pad, g_pad, blk, tg_ref)

        a.wait()
        b.wait()
        fill_ends(prev, nxt, g_pad, blocks)

        @pl.loop(0, blocks)
        def _(blk):
            for r, value in conv_block(g_pad, t_ref, blk, True):
                o_ref[pl.ds(r, CHUNK), lanes(blk)] = value

        for c in waits:
            c.wait()

    outs = [jax.ShapeDtypeStruct((ROWS, cols), F32), jax.ShapeDtypeStruct((32, cols), F32)]
    ins = [g, x, x_prev, x_next, taps]
    scratch = [
        pltpu.VMEM((blocks, ROWS + 2 * HALO, 128), F32),
        pltpu.VMEM((blocks, ROWS + 2 * HALO, 128), F32),
        pltpu.VMEM((2, HALO, cols), BF16),
        pltpu.VMEM((HALO, cols), BF16),
        pltpu.VMEM((HALO, cols), BF16),
        pltpu.SemaphoreType.DMA((2,)),
        pltpu.SemaphoreType.DMA((2,)),
    ]
    in_specs, out_specs = [VM] * 5, [VM, VM]
    if extra:
        ins.append(heads_in)
        in_specs.append(ANY)
        outs.append(
            jax.ShapeDtypeStruct((ROWS * GROUP, heads_in.shape[1] // GROUP), heads_in.dtype)
        )
        out_specs.append(ANY)
        scratch += [
            pltpu.SemaphoreType.DMA((GROUP,)),
            pltpu.SemaphoreType.DMA((GROUP,)),
            pltpu.SemaphoreType.DMA,
        ]
    return pl.pallas_call(
        kernel,
        out_shape=outs,
        in_specs=in_specs,
        out_specs=out_specs,
        scratch_shapes=scratch,
        compiler_params=params(cid),
        name="conv_backward",
    )(*ins)


def position_factors(frames, width):
    frequency = jnp.exp(
        jnp.arange(width // 2, dtype=jnp.int32).astype(F32) * (-2.0 * math.log(10000.0) / width)
    )
    coarse = (32.0 * jnp.arange(frames // 32, dtype=jnp.int32).astype(F32))[:, None] * frequency
    fine = jnp.arange(32, dtype=jnp.int32).astype(F32)[:, None] * frequency
    sa, ca = jnp.sin(coarse)[:, None], jnp.cos(coarse)[:, None]
    sb, cb = jnp.sin(fine)[None], jnp.cos(fine)[None]
    sin = (sa * cb + ca * sb).reshape(frames, width // 2)
    cos = (ca * cb - sa * sb).reshape(frames, width // 2)
    return sin, cos


def head_mask(h):
    column = lax.broadcasted_iota(jnp.int32, (1, 128), 1)
    return jnp.where((column >= 64 * h) & (column < 64 * h + 64), 1.0, 0.0)


def rotated(query, sin, cos, w_pos):
    z = times_transpose(query, w_pos)
    zs, zc = z[:, : D // 2], z[:, D // 2 :]
    return jnp.concatenate([zc * sin - zs * cos, zs * sin + zc * cos], axis=1).astype(BF16)


def attention_forward(qkv, w_pos, biases, mask, table, sin, cos):
    frames = qkv.shape[0]

    def kernel(q_ref, k_ref, v_ref, wp_ref, b_ref, m_ref, t_ref, s_ref, c_ref, o_ref, p_ref):
        query = q_ref[...].astype(F32)
        total = jnp.zeros((ROWS, 128), F32)
        for h in range(2):
            keep = head_mask(h)
            content = ((query + b_ref[pl.ds(0, 1), :]) * (0.125 * keep)).astype(BF16)
            position = ((query + b_ref[pl.ds(1, 1), :]) * (0.125 * keep)).astype(BF16)
            turned = rotated(position, s_ref[...], c_ref[...], wp_ref[...])
            scores = times_transpose(turned, t_ref[...]) + times_transpose(content, k_ref[...])
            scores = scores + m_ref[...]
            top = jnp.max(scores, -1, keepdims=True)
            weights = jnp.exp(scores - top)
            weights = (weights * (1.0 / jnp.sum(weights, -1, keepdims=True))).astype(BF16)
            p_ref[h] = weights
            total = total + product(weights, v_ref[...]) * keep
        o_ref[...] = total.astype(BF16)

    def whole(shape):
        return pl.BlockSpec(shape, lambda i: (0,) * len(shape))

    return pl.pallas_call(
        kernel,
        grid=(frames // ROWS,),
        in_specs=[
            pl.BlockSpec((ROWS, 128), lambda i: (i, 0)),
            pl.BlockSpec((frames, 128), lambda i: (0, 1)),
            pl.BlockSpec((frames, 128), lambda i: (0, 2)),
            whole((D, 128)),
            whole((8, 128)),
            whole((1, frames)),
            whole((frames, D)),
            pl.BlockSpec((ROWS, D // 2), lambda i: (i, 0)),
            pl.BlockSpec((ROWS, D // 2), lambda i: (i, 0)),
        ],
        out_specs=[
            pl.BlockSpec((ROWS, 128), lambda i: (i, 0)),
            pl.BlockSpec((2, ROWS, frames), lambda i: (0, i, 0)),
        ],
        out_shape=[
            jax.ShapeDtypeStruct((frames, 128), BF16),
            jax.ShapeDtypeStruct((2, frames, frames), BF16),
        ],
        compiler_params=pltpu.CompilerParams(
            dimension_semantics=("arbitrary",), vmem_limit_bytes=48 * 2**20
        ),
        name="attention_forward",
    )(qkv, qkv, qkv, w_pos, biases, mask, table, sin, cos)


def attention_backward(qkv, weights, attended, g_attended, w_pos, biases, table, sin, cos):
    frames = qkv.shape[0]
    steps = frames // ROWS

    def kernel(
        q_ref, k_ref, v_ref, p_ref, a_ref, ga_ref, wp_ref, b_ref, t_ref, s_ref, c_ref,
        gq_ref, gk_ref, gv_ref, gw_ref, gb_ref, gk_acc, gv_acc,
    ):
        step = pl.program_id(0)

        @pl.when(step == 0)
        def _():
            gk_acc[...] = jnp.zeros_like(gk_acc)
            gv_acc[...] = jnp.zeros_like(gv_acc)
            gw_ref[...] = jnp.zeros_like(gw_ref)
            gb_ref[...] = jnp.zeros_like(gb_ref)

        query = q_ref[...].astype(F32)
        g_out = ga_ref[...]
        dots = g_out.astype(F32) * a_ref[...].astype(F32)
        sin_, cos_ = s_ref[...], c_ref[...]
        g_content = jnp.zeros((ROWS, 128), F32)
        g_position = jnp.zeros((ROWS, 128), F32)
        for h in range(2):
            keep = head_mask(h)
            content = ((query + b_ref[pl.ds(0, 1), :]) * (0.125 * keep)).astype(BF16)
            position = ((query + b_ref[pl.ds(1, 1), :]) * (0.125 * keep)).astype(BF16)
            g_head = (g_out.astype(F32) * keep).astype(BF16)
            p = p_ref[h]
            g_weights = times_transpose(g_head, v_ref[...])
            inner = jnp.sum(dots * keep, -1, keepdims=True)
            g_scores = (p.astype(F32) * (g_weights - inner)).astype(BF16)
            gv_acc[...] += contract_rows(g_head, p)
            gk_acc[...] += contract_rows(content, g_scores)
            g_content = g_content + product(g_scores, k_ref[...]) * keep
            turned = product(g_scores, t_ref[...])
            ts, tc = turned[:, : D // 2], turned[:, D // 2 :]
            g_z = jnp.concatenate([tc * sin_ - ts * cos_, ts * sin_ + tc * cos_], axis=1)
            g_z = g_z.astype(BF16)
            g_position = g_position + product(g_z, wp_ref[...]) * keep
            gw_ref[...] += contract_rows(g_z, position)
        g_content = g_content * 0.125
        g_position = g_position * 0.125
        gq_ref[...] = (g_content + g_position).astype(BF16)
        gb_ref[pl.ds(0, 1), :] += jnp.sum(g_content, 0, keepdims=True)
        gb_ref[pl.ds(1, 1), :] += jnp.sum(g_position, 0, keepdims=True)

        @pl.when(step == steps - 1)
        def _():
            gk_ref[...] = gk_acc[...].T.astype(BF16)
            gv_ref[...] = gv_acc[...].T.astype(BF16)

    def whole(shape):
        return pl.BlockSpec(shape, lambda i: (0,) * len(shape))

    rows = pl.BlockSpec((ROWS, 128), lambda i: (i, 0))
    return pl.pallas_call(
        kernel,
        grid=(steps,),
        in_specs=[
            rows,
            pl.BlockSpec((frames, 128), lambda i: (0, 1)),
            pl.BlockSpec((frames, 128), lambda i: (0, 2)),
            pl.BlockSpec((2, ROWS, frames), lambda i: (0, i, 0)),
            rows,
            rows,
            whole((D, 128)),
            whole((8, 128)),
            whole((frames, D)),
            pl.BlockSpec((ROWS, D // 2), lambda i: (i, 0)),
            pl.BlockSpec((ROWS, D // 2), lambda i: (i, 0)),
        ],
        out_specs=[rows, whole((frames, 128)), whole((frames, 128)), whole((D, 128)), whole((8, 128))],
        out_shape=[
            jax.ShapeDtypeStruct((frames, 128), BF16),
            jax.ShapeDtypeStruct((frames, 128), BF16),
            jax.ShapeDtypeStruct((frames, 128), BF16),
            jax.ShapeDtypeStruct((D, 128), F32),
            jax.ShapeDtypeStruct((8, 128), F32),
        ],
        scratch_shapes=[pltpu.VMEM((128, frames), F32), pltpu.VMEM((128, frames), F32)],
        compiler_params=pltpu.CompilerParams(
            dimension_semantics=("arbitrary",), vmem_limit_bytes=48 * 2**20
        ),
        name="attention_backward",
    )(qkv, qkv, qkv, weights, attended, g_attended, w_pos, biases, table, sin, cos)


class Reduction:
    def __init__(self, arrays, kinds, parts, shared_rows=0):
        self.kinds = kinds
        self.halves = []
        self.offsets = []
        at = 0
        for a, kind in zip(arrays, kinds):
            rows, cols = a.shape
            h, c = (rows // 8, cols) if kind == "rows" else (rows // 2, cols // 4)
            self.halves.append((h, c))
            self.offsets.append(at)
            at += h * c // D
        self.used = at
        self.parts = parts
        self.rows = sum(parts)
        self.shared = shared_rows
        count = len(arrays)
        n_a = parts[0]
        n_b = parts[2]
        self.scratch = []
        for (h, c), kind in zip(self.halves, kinds):
            shape = (4, h, c) if kind == "rows" else (h, 4 * c)
            self.scratch += [pltpu.VMEM(shape, BF16)] * 2
        self.scratch += [
            pltpu.VMEM((4, self.rows, D), BF16),
            pltpu.VMEM((2, 3, n_a, D), BF16),
            pltpu.VMEM((2, n_a, D), BF16),
            pltpu.VMEM((3, n_a // 4, D), BF16),
            pltpu.VMEM((n_a // 4, D), BF16),
            pltpu.VMEM((3, n_a, 128), BF16),
            pltpu.VMEM((n_a, 128), BF16),
            pltpu.VMEM((2, 3, n_a // 4, 128), BF16),
            pltpu.VMEM((3, 4, n_b // 4, D), BF16),
            pltpu.VMEM((4, n_b // 4, D), BF16),
            pltpu.VMEM((3, 4, n_b, 128), BF16),
            pltpu.VMEM((4, n_b, 128), BF16),
            pltpu.VMEM((2, 3, 4, n_b // 4, 128), BF16),
            pltpu.VMEM((2, 4, n_b // 4, 128), BF16),
            pltpu.VMEM((2, 3, n_b // 4, 128), BF16),
            pltpu.SemaphoreType.DMA((count, 4)),
            pltpu.SemaphoreType.DMA((count, 4)),
            pltpu.SemaphoreType.DMA((count, 4)),
            pltpu.SemaphoreType.DMA((24, 3)),
            pltpu.SemaphoreType.DMA((24, 3)),
        ]
        self.outs = [jax.ShapeDtypeStruct((2, self.rows, D), BF16)]
        if shared_rows:
            self.outs.append(jax.ShapeDtypeStruct((4, 2, shared_rows, D), BF16))

    def greet(self):
        barrier = pltpu.get_barrier_semaphore()
        for axis in ("x", "y", "z"):
            me = lax.axis_index(axis)
            for off in (1, 2, 3):
                where = {axis: lax.rem(me + off, 4)}
                pl.semaphore_signal(barrier, inc=1, device_id=where, device_id_type=MESH)
        where = {"core": 1 - lax.axis_index("core")}
        pl.semaphore_signal(barrier, inc=1, device_id=where, device_id_type=MESH)
        pl.semaphore_wait(barrier, 10)

    def run(self, ins, outs, scratch):
        count = len(ins)
        own, other = scratch[0 : 2 * count : 2], scratch[1 : 2 * count : 2]
        (packed, ya, ta, xa1, ta1, za2, ta2, la, xb, tb, zc, tc, l2, t2, l3) = scratch[2 * count : 2 * count + 15]
        s_loc, s_send, s_recv, g_send, g_recv = scratch[2 * count + 15 :]
        out = outs[0]
        core, x, y, z = (lax.axis_index(a) for a in ("core", "x", "y", "z"))
        mine = {"x": x, "y": y, "z": z}
        group = [0]

        def send_all(axis, src, dst):
            g = group[0]
            group[0] += 1
            copies = []
            for off in (2, 1, 3):
                peer = lax.rem(mine[axis] + off, 4)
                c = pltpu.make_async_remote_copy(
                    src_ref=src(peer),
                    dst_ref=dst(off - 1),
                    send_sem=g_send.at[g, off - 1],
                    recv_sem=g_recv.at[g, off - 1],
                    device_id={axis: peer},
                    device_id_type=MESH,
                )
                c.start()
                copies.append(c)
            return copies

        def wait(copies):
            for c in copies:
                c.wait()

        def add(dest, terms, rows, lead=None):
            step = 32 if rows % 32 == 0 else 16

            @pl.loop(0, rows, step=step)
            def _(r):
                at = pl.ds(pl.multiple_of(r, step), step)
                for b in range(lead or 1):
                    key = (b, at) if lead else (at,)
                    total = terms[0][key].astype(F32)
                    for t in terms[1:]:
                        total = total + t[key].astype(F32)
                    dest[key] = total.astype(BF16)

        pair = dict(device_id={"core": 1 - core}, device_id_type=MESH)
        copies, locals_ = [], []
        for i in range(count):
            h, c = self.halves[i]
            if self.kinds[i] == "rows":
                for b in range(4):
                    r = pltpu.make_async_remote_copy(
                        src_ref=ins[i].at[pl.ds(b * 2 * h + (1 - core) * h, h), :],
                        dst_ref=other[i].at[b],
                        send_sem=s_send.at[i, b],
                        recv_sem=s_recv.at[i, b],
                        **pair,
                    )
                    l = pltpu.make_async_copy(
                        ins[i].at[pl.ds(b * 2 * h + core * h, h), :], own[i].at[b], s_loc.at[i, b]
                    )
                    r.start()
                    l.start()
                    copies.append((i, r))
                    locals_.append((i, l))
            else:
                r = pltpu.make_async_remote_copy(
                    src_ref=ins[i].at[pl.ds((1 - core) * h, h), :],
                    dst_ref=other[i],
                    send_sem=s_send.at[i, 0],
                    recv_sem=s_recv.at[i, 0],
                    **pair,
                )
                l = pltpu.make_async_copy(
                    ins[i].at[pl.ds(core * h, h), :], own[i], s_loc.at[i, 0]
                )
                r.start()
                l.start()
                copies.append((i, r))
                locals_.append((i, l))
        yield
        if self.rows > self.used:
            gap = self.rows - self.used
            for b in range(4):
                packed[b, pl.ds(self.used, gap), :] = jnp.zeros((gap, D), BF16)
        for i in range(count):
            for j, c in copies + locals_:
                if j == i:
                    c.wait()
            h, c = self.halves[i]
            at = self.offsets[i]
            tiles = c // 128
            if self.kinds[i] == "rows":

                @pl.loop(0, h, step=16)
                def _(r):
                    row = pl.ds(pl.multiple_of(r, 16), 16)
                    to = pl.ds(pl.multiple_of(at + r, 16), 16)
                    for b in range(4):
                        packed[b, to, :] = own[i][b, row, :] + other[i][b, row, :]

            elif tiles == 4:

                @pl.loop(0, h, step=16)
                def _(r):
                    row = pl.ds(pl.multiple_of(r, 16), 16)
                    to = pl.ds(pl.multiple_of(at + r, 16), 16)
                    for b in range(4):
                        col = pl.ds(b * D, D)
                        packed[b, to, :] = own[i][row, col] + other[i][row, col]

            else:
                q = h // 4
                for g in range(4):
                    for t in range(tiles):
                        k = g * tiles + t
                        for b in range(4):
                            row, col = pl.ds(g * q, q), pl.ds(b * c + t * 128, 128)
                            to, lane = pl.ds(at + k // 4 * q, q), pl.ds(k % 4 * 128, 128)
                            packed[b, to, lane] = own[i][row, col] + other[i][row, col]

        n1, n2, n3, n4 = self.parts
        o1, o2, o3, o4 = 0, n1, n1 + n2, n1 + n2 + n3

        def lane(i):
            return pl.ds(pl.multiple_of(i * 128, 128), 128)

        def quarter(start, n, i):
            q = n // 4
            return pl.ds(pl.multiple_of(start + i * q, 16), q)

        a1 = send_all("y", lambda p: packed.at[p, pl.ds(o1, n1), :], lambda s: ya.at[0, s])
        a2 = send_all("y", lambda p: packed.at[p, pl.ds(o2, n2), :], lambda s: ya.at[1, s])
        b1 = send_all("x", lambda p: packed.at[:, quarter(o3, n3, p), :], lambda s: xb.at[s])
        c1 = send_all("z", lambda p: packed.at[:, pl.ds(o4, n4), lane(p)], lambda s: zc.at[s])
        yield
        wait(a1)
        add(ta.at[0], [packed.at[y, pl.ds(o1, n1)]] + [ya.at[0, s] for s in range(3)], n1)
        a1 = send_all("x", lambda p: ta.at[0, quarter(0, n1, p), :], lambda s: xa1.at[s])
        wait(a2)
        add(ta.at[1], [packed.at[y, pl.ds(o2, n2)]] + [ya.at[1, s] for s in range(3)], n2)
        a2 = send_all("z", lambda p: ta.at[1, :, lane(p)], lambda s: za2.at[s])
        wait(b1)
        add(tb, [packed.at[:, quarter(o3, n3, x), :]] + [xb.at[s] for s in range(3)], n3 // 4, 4)
        b1 = send_all("z", lambda p: tb.at[:, :, lane(p)], lambda s: l2.at[0, s])
        wait(c1)
        add(tc, [packed.at[:, pl.ds(o4, n4), lane(z)]] + [zc.at[s] for s in range(3)], n4, 4)
        c1 = send_all("x", lambda p: tc.at[:, quarter(0, n4, p), :], lambda s: l2.at[1, s])
        yield
        wait(a1)
        add(ta1, [ta.at[0, quarter(0, n1, x), :]] + [xa1.at[s] for s in range(3)], n1 // 4)
        a1 = send_all("z", lambda p: ta1.at[:, lane(p)], lambda s: la.at[0, s])
        wait(a2)
        add(ta2, [ta.at[1, :, lane(z)]] + [za2.at[s] for s in range(3)], n2)
        a2 = send_all("x", lambda p: ta2.at[quarter(0, n2, p), :], lambda s: la.at[1, s])
        wait(b1)
        add(t2.at[0], [tb.at[:, :, lane(z)]] + [l2.at[0, s] for s in range(3)], n3 // 4, 4)
        b1 = send_all("y", lambda p: t2.at[0, p], lambda s: l3.at[0, s])
        wait(c1)
        add(t2.at[1], [tc.at[:, quarter(0, n4, x), :]] + [l2.at[1, s] for s in range(3)], n4 // 4, 4)
        c1 = send_all("y", lambda p: t2.at[1, p], lambda s: l3.at[1, s])
        yield
        starts = (o1, o2, o3, o4)
        final = [
            (a1, ta1.at[:, lane(z)], la.at[0]),
            (a2, ta2.at[quarter(0, n2, x), :], la.at[1]),
            (b1, t2.at[0, y], l3.at[0]),
            (c1, t2.at[1, y], l3.at[1]),
        ]
        back = []
        for k in range(4):
            copies, base, rest = final[k]
            wait(copies)
            piece = out.at[core, quarter(starts[k], self.parts[k], x), lane(z)]
            add(piece, [base] + [rest.at[s] for s in range(3)], self.parts[k] // 4)
            back.append(send_all("z" if k % 2 == 0 else "x", lambda p: piece, lambda s: piece))
        yield
        for k in range(4):
            wait(back[k])
            if k % 2 == 0:
                piece = out.at[core, quarter(starts[k], self.parts[k], x), :]
                back[k] = send_all("x", lambda p: piece, lambda s: piece)
            else:
                piece = out.at[core, pl.ds(starts[k], self.parts[k]), lane(z)]
                back[k] = send_all("z", lambda p: piece, lambda s: piece)
        yield
        for k in range(4):
            wait(back[k])
        last = pltpu.make_async_remote_copy(
            src_ref=out.at[core],
            dst_ref=out.at[core],
            send_sem=g_send.at[22, 0],
            recv_sem=g_recv.at[22, 0],
            **pair,
        )
        last.start()
        if self.shared:
            every = outs[1]
            start = self.used - self.shared
            every[y, core] = out[core, pl.ds(start, self.shared), :]
            wait(send_all("y", lambda p: every.at[y, core], lambda s: every.at[y, core]))
            more = pltpu.make_async_remote_copy(
                src_ref=every.at[:, core],
                dst_ref=every.at[:, core],
                send_sem=g_send.at[23, 0],
                recv_sem=g_recv.at[23, 0],
                **pair,
            )
            more.start()
            more.wait()
        last.wait()

    def shard(self, out, i):
        h, c = self.halves[i]
        n = h * c // D
        a = out[:, self.offsets[i] : self.offsets[i] + n].astype(F32)
        tiles = c // 128
        if tiles != 4:
            q = h // 4
            a = a.reshape(2, tiles, q, 4, 128).transpose(0, 1, 3, 2, 4)
            a = a.reshape(2, 4, tiles, q, 128).transpose(0, 1, 3, 2, 4)
        return a.reshape(2 * h, c)


def reduce_gradients(arrays, kinds, parts, shared_rows, cid):
    plan = Reduction(arrays, kinds, parts, shared_rows)
    count = len(arrays)

    def kernel(*refs):
        outs = refs[count : count + len(plan.outs)]
        plan.greet()
        for _ in plan.run(refs[:count], outs, refs[count + len(plan.outs) :]):
            pass

    outs = pl.pallas_call(
        kernel,
        out_shape=plan.outs,
        in_specs=[ANY] * count,
        out_specs=[VM] * len(plan.outs),
        scratch_shapes=plan.scratch,
        compiler_params=params(cid, 56),
        name="reduce_gradients",
    )(*arrays)
    return plan, outs


def local(
    features,
    lengths,
    first_gain,
    first_shift,
    first_up,
    first_down,
    attn_gain,
    attn_shift,
    w_query,
    w_key,
    w_value,
    w_pos,
    bias_content,
    bias_position,
    attn_out,
    cgmlp_gain,
    cgmlp_shift,
    cgmlp_up,
    gate_gain,
    gate_shift,
    gate_taps,
    cgmlp_down,
    merge_taps,
    merge_proj,
    second_gain,
    second_shift,
    second_up,
    second_down,
    final_gain,
    final_shift,
    cotangent,
):
    frames = ROWS * GROUP
    channels = gate_gain.shape[0]
    me = lax.axis_index("y")
    length = lengths[0]
    live = (jnp.arange(ROWS, dtype=jnp.int32) + me * ROWS < length).astype(F32)[:, None]
    mask = jnp.where(jnp.arange(frames, dtype=jnp.int32) < length, 0.0, -1e30)[None].astype(F32)
    vec = lambda v: v.astype(F32)[None]
    sin, cos = position_factors(frames, D)
    table = jnp.concatenate([sin, cos], axis=1).astype(BF16)
    biases = jnp.concatenate(
        [
            bias_content.astype(F32).reshape(1, 128),
            bias_position.astype(F32).reshape(1, 128),
            jnp.zeros((6, 128), F32),
        ]
    )
    small = jnp.concatenate(
        [gate_taps, gate_gain[None], gate_shift[None], jnp.zeros((31, channels), BF16)]
    )
    wide = jnp.concatenate([w_query, w_key, w_value], axis=1)
    halves = cgmlp_up[:, 0], cgmlp_up[:, 1]
    (up1, down1, qkv_w, cg0, cg1, small_all, out_w, cg_down, up2, down2) = gather_weights(
        (
            first_up, first_down, wide, halves[0], halves[1], small, attn_out, cgmlp_down,
            second_up, second_down,
        ),
        ("cols", "rows", "cols", "cols", "cols", "cols", "rows", "rows", "cols", "rows"),
        0,
    )
    small_f = small_all.astype(F32)
    gate_taps_f = small_f[:32]
    gate_gain_f, gate_shift_f = small_f[31:32], small_f[32:33]
    merge_taps_f = jnp.pad(merge_taps.astype(F32), ((0, 1), (0, 0)))

    start = features.astype(F32)
    u1, inv1 = unit_norm(start)
    in1 = (u1 * vec(first_gain) + vec(first_shift)).astype(BF16)
    act1 = product(in1, up1)
    hid1 = (act1 * jax.nn.sigmoid(act1)).astype(BF16)
    middle = start + 0.5 * product(hid1, down1)
    u2, inv2 = unit_norm(middle)
    attn_in = (u2 * vec(attn_gain) + vec(attn_shift)).astype(BF16)
    cg_in = (u2 * vec(cgmlp_gain) + vec(cgmlp_shift)).astype(BF16)
    qkv_rows = product(attn_in, qkv_w).astype(BF16)
    c0 = product(cg_in, cg0)
    c1 = product(cg_in, cg1)
    root = 1.0 / math.sqrt(2.0)
    phi0 = 0.5 * (1.0 + lax.erf(c0 * root))
    phi1 = 0.5 * (1.0 + lax.erf(c1 * root))
    half0 = c0 * phi0
    ug, invg = unit_norm(c1 * phi1)
    gate_norm = (ug * gate_gain_f + gate_shift_f) * live
    gate_conv, gn_prev, gn_next, qkv = conv_forward(gate_norm, gate_taps_f, 1, qkv_rows)
    gate_out = (half0 * gate_conv).astype(BF16)
    attended, weights = attention_forward(qkv, w_pos, biases, mask, table, sin, cos)
    attended_rows = exchange(attended, False, 2)
    joined = jnp.concatenate([product(attended_rows, out_w), product(gate_out, cg_down)], axis=1)
    joined_live = joined * live
    merge_conv, jl_prev, jl_next = conv_forward(joined_live, merge_taps_f, 3)
    mixed = (joined + merge_conv).astype(BF16)
    merged = middle + product(mixed, merge_proj)
    u3, inv3 = unit_norm(merged)
    in2 = (u3 * vec(second_gain) + vec(second_shift)).astype(BF16)
    act2 = product(in2, up2)
    sig2 = jax.nn.sigmoid(act2)
    hid2 = (act2 * sig2).astype(BF16)
    last = merged + 0.5 * product(hid2, down2)
    u4, inv4 = unit_norm(last)
    encoded = u4 * vec(final_gain) + vec(final_shift)

    cot = cotangent.astype(F32)
    g_final_gain = jnp.sum(cot * u4, 0)
    g_final_shift = jnp.sum(cot, 0)
    g_last = norm_back(cot * vec(final_gain), u4, inv4)
    gy2 = (0.5 * g_last).astype(BF16)
    g_down2 = contract_rows(hid2, gy2)
    g_act2 = (times_transpose(gy2, down2) * sig2 * (1.0 + act2 * (1.0 - sig2))).astype(BF16)
    g_up2 = contract_rows(in2, g_act2)
    g_in2 = times_transpose(g_act2, up2)
    g_second_gain = jnp.sum(g_in2 * u3, 0)
    g_second_shift = jnp.sum(g_in2, 0)
    g_merged = g_last + norm_back(g_in2 * vec(second_gain), u3, inv3)
    gm = g_merged.astype(BF16)
    g_merge_proj = contract_rows(mixed, gm)
    gx = times_transpose(gm, merge_proj)
    merge_back, g_merge_taps = conv_backward(gx, joined_live, jl_prev, jl_next, merge_taps_f, 4)
    g_joined = (gx + live * merge_back).astype(BF16)
    ga, gb = g_joined[:, :D], g_joined[:, D:]
    g_attn_out = contract_rows(attended_rows, ga)
    g_attended_rows = times_transpose(ga, out_w).astype(BF16)
    g_cg_down = contract_rows(gate_out, gb)
    gg = times_transpose(gb, cg_down)
    g_conv = gg * half0
    g_norm_raw, g_gate_taps, g_attended = conv_backward(
        g_conv, gate_norm, gn_prev, gn_next, gate_taps_f, 5, g_attended_rows
    )
    gq, gk, gv, g_w_pos, g_bias = attention_backward(
        qkv, weights, attended, g_attended, w_pos, biases, table, sin, cos
    )
    g_qkv = exchange(jnp.concatenate([gq, gk, gv], axis=1), False, 6)
    g_gate_norm = g_norm_raw * live
    g_gate_gain = jnp.sum(g_gate_norm * ug, 0)
    g_gate_shift = jnp.sum(g_gate_norm, 0)
    g_half1 = norm_back(g_gate_norm * gate_gain_f, ug, invg)
    density = 1.0 / math.sqrt(2.0 * math.pi)
    g_c0 = (gg * gate_conv * (phi0 + c0 * (density * jnp.exp(-0.5 * c0 * c0)))).astype(BF16)
    g_c1 = (g_half1 * (phi1 + c1 * (density * jnp.exp(-0.5 * c1 * c1)))).astype(BF16)
    g_cg0 = contract_rows(cg_in, g_c0)
    g_cg1 = contract_rows(cg_in, g_c1)
    g_cg_in = times_transpose(g_c0, cg0) + times_transpose(g_c1, cg1)
    g_attn_in = times_transpose(g_qkv, qkv_w)
    g_wide = contract_rows(attn_in, g_qkv)
    g_attn_gain = jnp.sum(g_attn_in * u2, 0)
    g_attn_shift = jnp.sum(g_attn_in, 0)
    g_cgmlp_gain = jnp.sum(g_cg_in * u2, 0)
    g_cgmlp_shift = jnp.sum(g_cg_in, 0)
    g_middle = g_merged + norm_back(
        g_attn_in * vec(attn_gain) + g_cg_in * vec(cgmlp_gain), u2, inv2
    )
    gy1 = (0.5 * g_middle).astype(BF16)
    sig1 = jax.nn.sigmoid(act1)
    g_down1 = contract_rows(hid1, gy1)
    g_act1 = (times_transpose(gy1, down1) * sig1 * (1.0 + act1 * (1.0 - sig1))).astype(BF16)
    g_up1 = contract_rows(in1, g_act1)
    g_in1 = times_transpose(g_act1, up1)
    g_first_gain = jnp.sum(g_in1 * u1, 0)
    g_first_shift = jnp.sum(g_in1, 0)
    g_features = g_middle + norm_back(g_in1 * vec(first_gain), u1, inv1)

    g_small = jnp.concatenate(
        [g_gate_taps[:31], g_gate_gain[None], g_gate_shift[None], jnp.zeros((95, GATE), F32)]
    ).astype(BF16)
    g_pos = jnp.concatenate([g_w_pos, g_bias, jnp.zeros((120, 128), F32)]).astype(BF16)
    g_pos = lax.dynamic_update_slice(jnp.zeros((640, D), BF16), g_pos, (0, me * 128))
    g_shared = jnp.concatenate(
        [g_merge_taps[:31].reshape(62, D)]
        + [
            g[None]
            for g in (
                g_first_gain, g_first_shift, g_attn_gain, g_attn_shift, g_cgmlp_gain,
                g_cgmlp_shift, g_second_gain, g_second_shift, g_final_gain, g_final_shift,
            )
        ]
        + [jnp.zeros((56, D), F32)]
    ).astype(BF16)
    plan, (owned, every) = reduce_gradients(
        [
            a.astype(BF16)
            for a in (
                g_up1, g_down1, g_wide, g_cg0, g_cg1, g_attn_out, g_cg_down, g_up2, g_down2,
                g_small, g_pos, g_merge_proj, g_shared,
            )
        ],
        ("cols", "rows", "cols", "cols", "cols", "rows", "rows", "cols", "rows", "cols", "cols", "rows", "rows"),
        (320, 320, 768, 768),
        144,
        7,
    )
    (d_up1, d_down1, d_wide, d_cg0, d_cg1, d_out, d_cg_down, d_up2, d_down2, d_small, d_pos) = (
        plan.shard(owned, i) for i in range(11)
    )
    d_merge = every[:, :, :128].reshape(1024, D).astype(F32)
    d_shared = every[:, :, 128:].reshape(128, D).astype(F32)
    d_bias, d_pos = d_pos[512:514], d_pos[:512]
    shared = [d_shared[62 + k] for k in range(6)]
    shared += [d_shared[:62].reshape(31, 1024), d_merge]
    shared += [d_shared[68 + k] for k in range(4)]
    return (
        encoded,
        g_features,
        shared[0],
        shared[1],
        d_up1,
        d_down1,
        shared[2],
        shared[3],
        d_wide[:, :128],
        d_wide[:, 128:256],
        d_wide[:, 256:],
        d_pos,
        d_bias[0].reshape(2, 64),
        d_bias[1].reshape(2, 64),
        d_out,
        shared[4],
        shared[5],
        jnp.stack([d_cg0, d_cg1], axis=1),
        d_small[31],
        d_small[32],
        d_small[:31],
        d_cg_down,
        shared[6],
        shared[7],
        shared[8],
        shared[9],
        d_up2,
        d_down2,
        shared[10],
        shared[11],
    )


def solution(mesh):
    devices = mesh.devices.reshape(4, 4, 2, GROUP)
    fine = Mesh(devices, ("z", "x", "core", "y"))
    rows = P(("z", "x", "core", "y"), None)
    column, row = P(None, "y"), P("y", None)
    placed = (
        rows,
        P(("z", "x", "core")),
        P(),
        P(),
        column,
        row,
        P(),
        P(),
        column,
        column,
        column,
        column,
        row,
        row,
        row,
        P(),
        P(),
        P(None, None, "y"),
        P("y"),
        P("y"),
        column,
        row,
        P(),
        P(),
        P(),
        P(),
        column,
        row,
        P(),
        P(),
        rows,
    )
    return jax.shard_map(
        local,
        mesh=fine,
        in_specs=placed,
        out_specs=(rows,) + (rows,) + placed[2:30],
        check_vma=False,
    )
```

```python
import math

import jax
import jax.numpy as jnp
from jax import lax
from jax.experimental import pallas as pl
from jax.experimental.pallas import tpu as pltpu
from jax.sharding import Mesh, PartitionSpec as P

GATE = 1536
KERNEL = 31
D = 512
ROWS = 320
HALO = 16
GROUP = 4
EPS = 1e-05
F32 = jnp.float32
BF16 = jnp.bfloat16
MESH = pl.DeviceIdType.MESH
ANY = pl.BlockSpec(memory_space=pl.ANY)
VM = pl.BlockSpec(memory_space=pltpu.VMEM)


def product(a, b):
    return jnp.dot(a, b, preferred_element_type=F32)


def contract_rows(a, b):
    return lax.dot_general(a, b, (((0,), (0,)), ((), ())), preferred_element_type=F32)


def times_transpose(a, b):
    return lax.dot_general(a, b, (((1,), (1,)), ((), ())), preferred_element_type=F32)


def unit_norm(rows):
    center = rows - jnp.mean(rows, -1, keepdims=True)
    inverse = lax.rsqrt(jnp.mean(center * center, -1, keepdims=True) + EPS)
    return center * inverse, inverse


def norm_back(scaled, unit, inverse):
    inner = (
        scaled
        - jnp.mean(scaled, -1, keepdims=True)
        - unit * jnp.mean(scaled * unit, -1, keepdims=True)
    )
    return inner * inverse


def params(cid, vmem=48, **more):
    return pltpu.CompilerParams(
        collective_id=cid, has_side_effects=True, vmem_limit_bytes=vmem * 2**20, **more
    )


def ring():
    me = lax.axis_index("y")
    return me, lax.rem(me + 1, GROUP), lax.rem(me + GROUP - 1, GROUP), lax.rem(me + 2, GROUP)


def to_y(where):
    return dict(device_id={"y": where}, device_id_type=MESH)


def greet_ring(offsets):
    me = lax.axis_index("y")
    barrier = pltpu.get_barrier_semaphore()
    for off in offsets:
        pl.semaphore_signal(barrier, inc=1, **to_y(lax.rem(me + off, GROUP)))
    pl.semaphore_wait(barrier, len(offsets))


def greet(y=False, xz=False, pair=False):
    barrier = pltpu.get_barrier_semaphore()
    count = 0
    for axis in (("y",) if y else ()) + (("x", "z") if xz else ()):
        me = lax.axis_index(axis)
        for off in (1, 2, 3):
            where = {axis: lax.rem(me + off, 4)}
            pl.semaphore_signal(barrier, inc=1, device_id=where, device_id_type=MESH)
            count += 1
    if pair:
        where = {"core": 1 - lax.axis_index("core")}
        pl.semaphore_signal(barrier, inc=1, device_id=where, device_id_type=MESH)
        count += 1
    pl.semaphore_wait(barrier, count)


class Gather:
    def __init__(self, shards, kinds, routes):
        self.kinds = kinds
        self.routes = routes
        self.shapes = [s.shape for s in shards]
        self.count = len(shards)
        self.outs = []
        for s, kind in zip(shards, kinds):
            rows, cols = s.shape
            shape = (GROUP, rows, cols) if kind == "rows" else (rows, GROUP * cols)
            self.outs.append(jax.ShapeDtypeStruct(shape, s.dtype))
        self.scratch = [
            pltpu.SemaphoreType.DMA((self.count,)),
            pltpu.SemaphoreType.DMA((self.count, 10)),
            pltpu.SemaphoreType.DMA((self.count, 10)),
        ]

    def run(self, srcs, dsts, scratch):
        local_sem, send, recv = scratch
        core, x, y, z = (lax.axis_index(a) for a in ("core", "x", "y", "z"))
        mine = {"x": x, "y": y, "z": z}
        pair = dict(device_id={"core": 1 - core}, device_id_type=MESH)
        count = self.count

        def spot(i, slot, slots, start, size, lane=None):
            cols = self.shapes[i][1]
            if self.kinds[i] == "rows":
                at = pl.ds(0, cols) if lane is None else lane
                return dsts[i].at[pl.ds(slot, slots), pl.ds(start, size), at]
            return dsts[i].at[pl.ds(start, size), pl.ds(slot * cols, slots * cols)]

        def cut(i, level):
            rows, cols = self.shapes[i]
            half = rows // 2
            route = self.routes[i]
            if level == 2 or route == "A":
                return core * half, half, None
            if self.kinds[i] == "rows":
                lane = pl.ds(pl.multiple_of(z * (cols // 4), 128), cols // 4)
                row, size = core * half + x * (half // 4), half // 4
                if level == 0:
                    return row, size, lane
                return (row, size, None) if route == "B" else (core * half, half, lane)
            a, b = (x, z) if route == "B" else (z, x)
            if level == 0:
                return core * half + (a * 4 + b) * (half // 16), half // 16, None
            return core * half + a * (half // 4), half // 4, None

        def remote(src, dst, i, k, where):
            return pltpu.make_async_remote_copy(
                src_ref=src, dst_ref=dst, send_sem=send.at[i, k], recv_sem=recv.at[i, k], **where
            )

        def spread(i, axis, level, k):
            at = spot(i, 1, 3, *cut(i, level))
            copies = []
            for off in (2, 1, 3):
                where = dict(device_id={axis: lax.rem(mine[axis] + off, 4)}, device_id_type=MESH)
                copies.append(remote(at, at, i, k + off - 1, where))
                copies[-1].start()
            return copies

        def to_pair(i):
            at = spot(i, 1, 3, *cut(i, 2))
            c = remote(at, at, i, 9, pair)
            c.start()
            return c

        def wait(copies):
            for c in copies:
                c.wait()

        flight, own, done = [None] * count, [], []
        spreading = [i for i in range(count) if self.routes[i] != "A"]
        for i in spreading + [i for i in range(count) if self.routes[i] == "A"]:
            start, size, lane = cut(i, 0)
            if lane is None:
                piece = srcs[i].at[pl.ds(start, size), :]
            else:
                piece = srcs[i].at[pl.ds(start, size), lane]
            copies = []
            for off in (2, 1, 3):
                there = spot(i, 4 - off, 1, start, size, lane)
                there = there.at[0] if self.kinds[i] == "rows" else there
                copies.append(remote(piece, there, i, off - 1, to_y(lax.rem(y + off, 4))))
                copies[-1].start()
            flight[i] = copies
        for i in range(count):
            rows = self.shapes[i][0]
            there = spot(i, 0, 1, 0, rows)
            there = there.at[0] if self.kinds[i] == "rows" else there
            c = pltpu.make_async_copy(srcs[i], there, local_sem.at[i])
            c.start()
            own.append(c)
        yield
        for i in spreading:
            wait(flight[i])
            flight[i] = spread(i, "z" if self.routes[i] == "B" else "x", 0, 3)
        yield
        for i in spreading:
            wait(flight[i])
            flight[i] = spread(i, "x" if self.routes[i] == "B" else "z", 1, 6)
        for i in range(count):
            if self.routes[i] == "A":
                wait(flight[i])
                done.append(to_pair(i))
        yield
        for i in spreading:
            wait(flight[i])
            done.append(to_pair(i))
        yield
        wait(own)
        wait(done)


def gather_weights(shards, kinds, routes, cid):
    plan = Gather(shards, kinds, routes)
    count = len(shards)

    def kernel(*refs):
        greet(y=True, xz=True, pair=True)
        for _ in plan.run(refs[:count], refs[count : 2 * count], refs[2 * count :]):
            pass

    return pl.pallas_call(
        kernel,
        out_shape=plan.outs,
        in_specs=[ANY] * count,
        out_specs=[ANY] * count,
        scratch_shapes=plan.scratch,
        compiler_params=params(cid),
        name="gather_weights",
    )(*shards)


def split_copies(src, dst, send, recv, local_sem):
    me = lax.axis_index("y")
    width = src.shape[1] // GROUP
    there = dst.at[pl.ds(pl.multiple_of(me * ROWS, ROWS), ROWS), :]
    copies = []
    for off in (2, 1, 3):
        c = pltpu.make_async_remote_copy(
            src_ref=src.at[:, pl.ds(off * width, width)],
            dst_ref=there,
            send_sem=send.at[off],
            recv_sem=recv.at[off],
            **to_y(lax.rem(me + off, GROUP)),
        )
        c.start()
        copies.append(c)
    own = pltpu.make_async_copy(src.at[:, pl.ds(0, width)], there, local_sem)
    own.start()
    copies.append(own)
    return copies


def start_halo(edges, prev, nxt, send, recv, slots):
    _, up, down, _ = ring()
    cols = prev.shape[1]
    w = cols // GROUP
    turns = ((w, 0, 3 * w), (0, 3 * w, w)) if slots else ((0, 0, cols),)
    copies = []
    for t, (here, there, size) in enumerate(turns):
        for side, ref, where in ((1, prev, up), (0, nxt, down)):
            a, b = (here, there) if side else (there, here)
            c = pltpu.make_async_remote_copy(
                src_ref=edges.at[side, :, pl.ds(a, size)],
                dst_ref=ref.at[:, pl.ds(b, size)],
                send_sem=send.at[side, t],
                recv_sem=recv.at[side, t],
                **to_y(where),
            )
            c.start()
            copies.append(c)
    return copies


def lanes(b):
    return pl.ds(pl.multiple_of(b * 128, 128), 128)


CHUNK = 64


def conv_block(pad, taps, b, flip):
    weights = [taps[pl.ds(KERNEL - 1 - o if flip else o, 1), lanes(b)] for o in range(KERNEL)]
    for r in range(0, ROWS, CHUNK):
        total = None
        for o in range(KERNEL):
            term = weights[o] * pad[b, pl.ds(r + o + 1, CHUNK), :]
            total = term if total is None else total + term
        yield r, total


def taps_block(pad, g_pad, b, out):
    sums = [None] * KERNEL
    for r in range(0, ROWS, CHUNK):
        g = g_pad[b, pl.ds(HALO + r, CHUNK), :]
        for o in range(KERNEL):
            term = g * pad[b, pl.ds(r + o + 1, CHUNK), :]
            term = jnp.sum(term.reshape(CHUNK // 8, 8, 128), 0)
            sums[o] = term if sums[o] is None else sums[o] + term
    for o in range(KERNEL):
        out[pl.ds(o, 1), lanes(b)] = jnp.sum(sums[o], 0, keepdims=True)


def fill_middle(x_ref, pad, blocks):
    @pl.loop(0, blocks)
    def _(b):
        pad[b, pl.ds(HALO, ROWS), :] = x_ref[:, lanes(b)].astype(F32)


def fill_ends(prev, nxt, pad, blocks):
    me = lax.axis_index("y")
    has_prev = jnp.where(me > 0, 1.0, 0.0)
    has_next = jnp.where(me < GROUP - 1, 1.0, 0.0)

    @pl.loop(0, blocks)
    def _(b):
        pad[b, pl.ds(0, HALO), :] = prev[:, lanes(b)].astype(F32) * has_prev
        pad[b, pl.ds(HALO + ROWS, HALO), :] = nxt[:, lanes(b)].astype(F32) * has_next


def set_edges(x_ref, edges):
    edges[0] = x_ref[pl.ds(0, HALO), :].astype(BF16)
    edges[1] = x_ref[pl.ds(ROWS - HALO, HALO), :].astype(BF16)


def conv_forward(x, taps, cid, heads_in=None, shards=(), kinds=(), routes=()):
    cols = x.shape[1]
    blocks = cols // 128
    extra = heads_in is not None
    plan = Gather(shards, kinds, routes)
    count = len(shards)

    def kernel(*refs):
        if extra:
            x_ref, t_ref, h_ref = refs[:3]
            srcs, refs = refs[3 : 3 + count], refs[3 + count :]
            o_ref, prev, nxt, ho_ref = refs[:4]
            dsts, refs = refs[4 : 4 + count], refs[4 + count :]
            pad, edges, hs, hr, ss, sr, sl = refs[:7]
            riding = plan.run(srcs, dsts, refs[7:])
            greet(y=True, xz=True, pair=True)
        else:
            x_ref, t_ref, o_ref, prev, nxt = refs[:5]
            pad, edges, hs, hr = refs[5:]
            greet_ring((1, 3))
        set_edges(x_ref, edges)
        halos = start_halo(edges, prev, nxt, hs, hr, extra)
        if extra:
            next(riding)
        waits = split_copies(h_ref, ho_ref, ss, sr, sl) if extra else []
        fill_middle(x_ref, pad, blocks)
        for c in halos:
            c.wait()
        fill_ends(prev, nxt, pad, blocks)
        parts = ((0, 2), (2, 5), (5, 9), (9, blocks))
        for low, high in parts if extra else ((0, blocks),):
            if extra:
                next(riding, None)

            @pl.loop(low, high)
            def _(blk):
                for r, value in conv_block(pad, t_ref, blk, False):
                    o_ref[pl.ds(r, CHUNK), lanes(blk)] = value

        if extra:
            for _ in riding:
                pass
        for c in waits:
            c.wait()

    edge = jax.ShapeDtypeStruct((HALO, cols), BF16)
    outs = [jax.ShapeDtypeStruct((ROWS, cols), F32), edge, edge]
    ins = [x, taps]
    scratch = [
        pltpu.VMEM((blocks, ROWS + 2 * HALO, 128), F32),
        pltpu.VMEM((2, HALO, cols), BF16),
        pltpu.SemaphoreType.DMA((2, 2)),
        pltpu.SemaphoreType.DMA((2, 2)),
    ]
    in_specs, out_specs = [VM, VM], [VM, VM, VM]
    if extra:
        ins += [heads_in, *shards]
        in_specs += [ANY] * (1 + count)
        outs.append(
            jax.ShapeDtypeStruct((ROWS * GROUP, heads_in.shape[1] // GROUP), heads_in.dtype)
        )
        outs += plan.outs
        out_specs += [ANY] * (1 + count)
        scratch += [
            pltpu.SemaphoreType.DMA((GROUP,)),
            pltpu.SemaphoreType.DMA((GROUP,)),
            pltpu.SemaphoreType.DMA,
        ] + plan.scratch
    return pl.pallas_call(
        kernel,
        out_shape=outs,
        in_specs=in_specs,
        out_specs=out_specs,
        scratch_shapes=scratch,
        compiler_params=params(cid),
        name="conv_forward",
    )(*ins)


def conv_backward(g, x, x_prev, x_next, taps, cid, heads_in=None, arrays=(), plan=None):
    cols = g.shape[1]
    blocks = cols // 128
    extra = heads_in is not None
    count = len(arrays)
    firsts = len(plan.first_outs) if extra else 0

    def kernel(*refs):
        g_ref, x_ref, xp_ref, xn_ref, t_ref = refs[:5]
        if extra:
            h_ref, refs = refs[5], refs[6:]
            ins, refs = refs[:count], refs[count:]
            o_ref, tg_ref, ho_ref = refs[:3]
            sums, refs = refs[3 : 3 + firsts], refs[3 + firsts :]
            g_pad, pad, edges, prev, nxt, hs, hr, ss, sr, sl = refs[:10]
            riding = plan.first(ins, sums, refs[10:])
            greet(y=True, xz=True, pair=True)
        else:
            o_ref, tg_ref = refs[5:7]
            g_pad, pad, edges, prev, nxt, hs, hr = refs[7:]
            greet_ring((1, 3))
        set_edges(g_ref, edges)
        halos = start_halo(edges, prev, nxt, hs, hr, extra)
        waits = split_copies(h_ref, ho_ref, ss, sr, sl) if extra else []
        if extra:
            next(riding)
        fill_middle(g_ref, g_pad, blocks)
        fill_middle(x_ref, pad, blocks)
        fill_ends(xp_ref, xn_ref, pad, blocks)
        tg_ref[pl.ds(24, 8), :] = jnp.zeros((8, cols), F32)
        parts = ((0, 7), (7, blocks)) if extra else ((0, blocks),)
        for low, high in parts:

            @pl.loop(low, high)
            def _(blk):
                taps_block(pad, g_pad, blk, tg_ref)

            if extra and low == 0:
                next(riding)

        for c in halos:
            c.wait()
        fill_ends(prev, nxt, g_pad, blocks)

        @pl.loop(0, blocks)
        def _(blk):
            for r, value in conv_block(g_pad, t_ref, blk, True):
                o_ref[pl.ds(r, CHUNK), lanes(blk)] = value

        for c in waits:
            c.wait()
        if extra:
            for _ in riding:
                pass

    outs = [jax.ShapeDtypeStruct((ROWS, cols), F32), jax.ShapeDtypeStruct((32, cols), F32)]
    ins = [g, x, x_prev, x_next, taps]
    scratch = [
        pltpu.VMEM((blocks, ROWS + 2 * HALO, 128), F32),
        pltpu.VMEM((blocks, ROWS + 2 * HALO, 128), F32),
        pltpu.VMEM((2, HALO, cols), BF16),
        pltpu.VMEM((HALO, cols), BF16),
        pltpu.VMEM((HALO, cols), BF16),
        pltpu.SemaphoreType.DMA((2, 2)),
        pltpu.SemaphoreType.DMA((2, 2)),
    ]
    in_specs, out_specs = [VM] * 5, [VM, VM]
    if extra:
        ins += [heads_in, *arrays]
        in_specs += [ANY] * (1 + count)
        outs.append(
            jax.ShapeDtypeStruct((ROWS * GROUP, heads_in.shape[1] // GROUP), heads_in.dtype)
        )
        outs += plan.first_outs
        out_specs += [ANY] + [VM] * firsts
        scratch += [
            pltpu.SemaphoreType.DMA((GROUP,)),
            pltpu.SemaphoreType.DMA((GROUP,)),
            pltpu.SemaphoreType.DMA,
        ] + plan.first_scratch
    return pl.pallas_call(
        kernel,
        out_shape=outs,
        in_specs=in_specs,
        out_specs=out_specs,
        scratch_shapes=scratch,
        compiler_params=params(cid),
        name="conv_backward",
    )(*ins)


def position_factors(frames, width):
    frequency = jnp.exp(
        jnp.arange(width // 2, dtype=jnp.int32).astype(F32) * (-2.0 * math.log(10000.0) / width)
    )
    steps = jnp.concatenate(
        [32 * jnp.arange(frames // 32, dtype=jnp.int32), jnp.arange(32, dtype=jnp.int32)]
    )
    angles = steps.astype(F32)[:, None] * frequency[None]
    return jnp.sin(angles), jnp.cos(angles)


def fill_table(sin_parts, cos_parts, sin, cos, table):
    frames, half = sin.shape
    sb, cb = sin_parts[pl.ds(frames // 32, 32), :], cos_parts[pl.ds(frames // 32, 32), :]

    @pl.loop(0, frames // 32)
    def _(a):
        at = pl.ds(pl.multiple_of(a * 32, 32), 32)
        sa, ca = sin_parts[pl.ds(a, 1), :], cos_parts[pl.ds(a, 1), :]
        s, c = sa * cb + ca * sb, ca * cb - sa * sb
        sin[at, :] = s
        cos[at, :] = c
        table[at, pl.ds(0, half)] = s.astype(BF16)
        table[at, pl.ds(half, half)] = c.astype(BF16)


def head_mask(h):
    column = lax.broadcasted_iota(jnp.int32, (1, 128), 1)
    return jnp.where((column >= 64 * h) & (column < 64 * h + 64), 1.0, 0.0)


def rotated(query, sin, cos, w_pos):
    z = times_transpose(query, w_pos)
    zs, zc = z[:, : D // 2], z[:, D // 2 :]
    return jnp.concatenate([zc * sin - zs * cos, zs * sin + zc * cos], axis=1).astype(BF16)


def attention_forward(qkv, w_pos, biases, mask, sin, cos, shards, kinds, routes, cid):
    frames = qkv.shape[0]
    plan = Gather(shards, kinds, routes)
    count = len(shards)

    def kernel(*refs):
        x_ref, wp_ref, b_ref, m_ref, sp_ref, cp_ref = refs[:6]
        srcs, refs = refs[6 : 6 + count], refs[6 + count :]
        o_ref, rows_ref, p_ref = refs[:3]
        dsts, refs = refs[3 : 3 + count], refs[3 + count :]
        p_buf, t_ref, s_ref, c_ref, p_sem, ss, sr, sl = refs[:8]
        riding = plan.run(srcs, dsts, refs[8:])
        me = lax.axis_index("y")
        greet(y=True, xz=True, pair=True)
        next(riding)
        fill_table(sp_ref, cp_ref, s_ref, c_ref, t_ref)
        saves, sends = [], []
        for k in range(GROUP):
            peer = lax.rem(me + 1 + k, GROUP)
            at = pl.ds(pl.multiple_of(peer * ROWS, ROWS), ROWS)
            query = x_ref[at, pl.ds(0, 128)].astype(F32)
            if k >= 2:
                saves[k - 2].wait()
            total = jnp.zeros((ROWS, 128), F32)
            for h in range(2):
                keep = head_mask(h)
                content = ((query + b_ref[pl.ds(0, 1), :]) * (0.125 * keep)).astype(BF16)
                position = ((query + b_ref[pl.ds(1, 1), :]) * (0.125 * keep)).astype(BF16)
                turned = rotated(position, s_ref[at, :], c_ref[at, :], wp_ref[...])
                scores = times_transpose(turned, t_ref[...])
                scores = scores + times_transpose(content, x_ref[:, pl.ds(128, 128)])
                scores = scores + m_ref[...]
                top = jnp.max(scores, -1, keepdims=True)
                weights = jnp.exp(scores - top)
                weights = (weights * (1.0 / jnp.sum(weights, -1, keepdims=True))).astype(BF16)
                p_buf[k % 2, h] = weights
                total = total + product(weights, x_ref[:, pl.ds(256, 128)]) * keep
                if (k, h) in ((0, 0), (1, 0), (3, 0)):
                    next(riding)
            o_ref[at, :] = total.astype(BF16)
            save = pltpu.make_async_copy(p_buf.at[k % 2], p_ref.at[:, at, :], p_sem.at[k % 2])
            save.start()
            saves.append(save)
            into = rows_ref.at[:, pl.ds((3 - k) * 128, 128)]
            if k < GROUP - 1:
                c = pltpu.make_async_remote_copy(
                    src_ref=o_ref.at[at, :],
                    dst_ref=into,
                    send_sem=ss.at[k],
                    recv_sem=sr.at[k],
                    **to_y(peer),
                )
            else:
                c = pltpu.make_async_copy(o_ref.at[at, :], into, sl)
            c.start()
            sends.append(c)
        for _ in riding:
            pass
        saves[2].wait()
        saves[3].wait()
        for c in sends:
            c.wait()

    return pl.pallas_call(
        kernel,
        in_specs=[VM] * 6 + [ANY] * count,
        out_specs=[VM, ANY, ANY] + [ANY] * count,
        out_shape=[
            jax.ShapeDtypeStruct((frames, 128), BF16),
            jax.ShapeDtypeStruct((ROWS, D), BF16),
            jax.ShapeDtypeStruct((2, frames, frames), BF16),
        ]
        + plan.outs,
        scratch_shapes=[
            pltpu.VMEM((2, 2, ROWS, frames), BF16),
            pltpu.VMEM((frames, D), BF16),
            pltpu.VMEM((frames, D // 2), F32),
            pltpu.VMEM((frames, D // 2), F32),
            pltpu.SemaphoreType.DMA((2,)),
            pltpu.SemaphoreType.DMA((3,)),
            pltpu.SemaphoreType.DMA((3,)),
            pltpu.SemaphoreType.DMA,
        ]
        + plan.scratch,
        compiler_params=params(cid),
        name="attention_forward",
    )(qkv, w_pos, biases, mask, sin, cos, *shards)


def attention_backward(
    qkv, weights, attended, g_attended, w_pos, biases, sin, cos, arrays, plan, earlier, before, cid,
):
    frames = qkv.shape[0]
    count = len(arrays)
    firsts = len(plan.first_outs)

    def kernel(*refs):
        x_ref, p_ref, a_ref, ga_ref, wp_ref, b_ref, sp_ref, cp_ref = refs[:8]
        ins, refs = refs[8 : 8 + count], refs[8 + count :]
        begun, refs = refs[:2], refs[2:]
        rows_ref, gw_ref, gb_ref = refs[:3]
        sums, refs = refs[3 : 3 + firsts], refs[3 + firsts :]
        finished, refs = refs[:2], refs[2:]
        p_buf, gq_buf, kv_buf, gk_acc, gv_acc, p_sem, qs, qr, ql, ks, kr, kl = refs[:12]
        t_ref, s_ref, c_ref = refs[12:15]
        refs = refs[15:]
        riding = plan.first(ins, sums, refs[: len(plan.first_scratch)])
        old = earlier.second(begun, finished, refs[len(plan.first_scratch) :])
        me = lax.axis_index("y")

        def block(k):
            peer = lax.rem(me + 1 + k, GROUP)
            return peer, pl.ds(pl.multiple_of(peer * ROWS, ROWS), ROWS)

        def load(k):
            c = pltpu.make_async_copy(p_ref.at[:, block(k)[1], :], p_buf.at[k % 2], p_sem.at[k % 2])
            c.start()
            return c

        loads = [load(0), load(1)]
        greet(y=True, xz=True, pair=True)
        next(old)
        next(riding)
        fill_table(sp_ref, cp_ref, s_ref, c_ref, t_ref)
        gk_acc[...] = jnp.zeros_like(gk_acc)
        gv_acc[...] = jnp.zeros_like(gv_acc)
        gw_ref[...] = jnp.zeros_like(gw_ref)
        gb_ref[...] = jnp.zeros_like(gb_ref)
        sends = []
        for k in range(GROUP):
            peer, at = block(k)
            query = x_ref[at, pl.ds(0, 128)].astype(F32)
            g_out = ga_ref[at, :]
            dots = g_out.astype(F32) * a_ref[at, :].astype(F32)
            sin_, cos_ = s_ref[at, :], c_ref[at, :]
            g_content = jnp.zeros((ROWS, 128), F32)
            g_position = jnp.zeros((ROWS, 128), F32)
            loads[k].wait()
            for h in range(2):
                keep = head_mask(h)
                content = ((query + b_ref[pl.ds(0, 1), :]) * (0.125 * keep)).astype(BF16)
                position = ((query + b_ref[pl.ds(1, 1), :]) * (0.125 * keep)).astype(BF16)
                g_head = (g_out.astype(F32) * keep).astype(BF16)
                p = p_buf[k % 2, h]
                g_weights = times_transpose(g_head, x_ref[:, pl.ds(256, 128)])
                inner = jnp.sum(dots * keep, -1, keepdims=True)
                g_scores = (p.astype(F32) * (g_weights - inner)).astype(BF16)
                gv_acc[...] += contract_rows(g_head, p)
                gk_acc[...] += contract_rows(content, g_scores)
                g_content = g_content + product(g_scores, x_ref[:, pl.ds(128, 128)]) * keep
                turned = product(g_scores, t_ref[...])
                ts, tc = turned[:, : D // 2], turned[:, D // 2 :]
                g_z = jnp.concatenate([tc * sin_ - ts * cos_, ts * sin_ + tc * cos_], axis=1)
                g_z = g_z.astype(BF16)
                g_position = g_position + product(g_z, wp_ref[...]) * keep
                gw_ref[...] += contract_rows(g_z, position)
                if (k, h) in ((0, 0), (1, 0), (3, 0)):
                    next(old)
                if (k, h) == (1, 0):
                    next(riding)
            g_content = g_content * 0.125
            g_position = g_position * 0.125
            gq_buf[at, :] = (g_content + g_position).astype(BF16)
            gb_ref[pl.ds(0, 1), :] += jnp.sum(g_content, 0, keepdims=True)
            gb_ref[pl.ds(1, 1), :] += jnp.sum(g_position, 0, keepdims=True)
            if k < 2:
                loads.append(load(k + 2))
            into = rows_ref.at[:, pl.ds((3 - k) * 384, 128)]
            if k < GROUP - 1:
                c = pltpu.make_async_remote_copy(
                    src_ref=gq_buf.at[at, :],
                    dst_ref=into,
                    send_sem=qs.at[k],
                    recv_sem=qr.at[k],
                    **to_y(peer),
                )
            else:
                c = pltpu.make_async_copy(gq_buf.at[at, :], into, ql)
            c.start()
            sends.append(c)
        kv_buf[:, pl.ds(0, 128)] = gk_acc[...].T.astype(BF16)
        kv_buf[:, pl.ds(128, 128)] = gv_acc[...].T.astype(BF16)
        for k in range(GROUP):
            into = rows_ref.at[:, pl.ds((3 - k) * 384 + 128, 256)]
            peer, at = block(k)
            if k < GROUP - 1:
                c = pltpu.make_async_remote_copy(
                    src_ref=kv_buf.at[at, :],
                    dst_ref=into,
                    send_sem=ks.at[k],
                    recv_sem=kr.at[k],
                    **to_y(peer),
                )
            else:
                c = pltpu.make_async_copy(kv_buf.at[at, :], into, kl)
            c.start()
            sends.append(c)
        for _ in old:
            pass
        for _ in riding:
            pass
        for c in sends:
            c.wait()

    return pl.pallas_call(
        kernel,
        in_specs=[VM, ANY] + [VM] * 6 + [ANY] * count + [VM] * 2,
        out_specs=[ANY, VM, VM] + [VM] * (firsts + 2),
        out_shape=[
            jax.ShapeDtypeStruct((ROWS, 3 * D), BF16),
            jax.ShapeDtypeStruct((D, 128), F32),
            jax.ShapeDtypeStruct((8, 128), F32),
        ]
        + plan.first_outs
        + earlier.outs,
        scratch_shapes=[
            pltpu.VMEM((2, 2, ROWS, frames), BF16),
            pltpu.VMEM((frames, 128), BF16),
            pltpu.VMEM((frames, 256), BF16),
            pltpu.VMEM((128, frames), F32),
            pltpu.VMEM((128, frames), F32),
            pltpu.SemaphoreType.DMA((2,)),
            pltpu.SemaphoreType.DMA((3,)),
            pltpu.SemaphoreType.DMA((3,)),
            pltpu.SemaphoreType.DMA,
            pltpu.SemaphoreType.DMA((3,)),
            pltpu.SemaphoreType.DMA((3,)),
            pltpu.SemaphoreType.DMA,
            pltpu.VMEM((frames, D), BF16),
            pltpu.VMEM((frames, D // 2), F32),
            pltpu.VMEM((frames, D // 2), F32),
        ]
        + plan.first_scratch
        + earlier.scratch,
        compiler_params=params(cid, 58),
        name="attention_backward",
    )(qkv, weights, attended, g_attended, w_pos, biases, sin, cos, *arrays, *before)


class Reduction:
    def __init__(self, shapes, kinds, parts, shared_rows=0):
        self.kinds = kinds
        self.halves = []
        self.offsets = []
        at = 0
        for (rows, cols), kind in zip(shapes, kinds):
            h, c = (rows // 2, cols // 4) if kind == "cols" else (rows // 8, cols)
            self.halves.append((h, c))
            self.offsets.append(at)
            at += h * c // D
        self.used = at
        self.parts = parts
        self.rows = sum(parts)
        self.shared = shared_rows
        count = len(shapes)
        n_a = parts[0]
        n_b = parts[2]
        self.first_scratch = []
        for (h, c), kind in zip(self.halves, kinds):
            shape = (h, 4 * c) if kind == "cols" else (4, h, c)
            self.first_scratch += [pltpu.VMEM(shape, BF16)] * 2
        self.first_scratch += [
            pltpu.VMEM((4, self.rows, D), BF16),
            pltpu.VMEM((2, 3, n_a, D), BF16),
            pltpu.VMEM((2, 3, 4, n_b // 4, D), BF16),
            pltpu.SemaphoreType.DMA((count, 4)),
            pltpu.SemaphoreType.DMA((count, 4)),
            pltpu.SemaphoreType.DMA((count, 4)),
            pltpu.SemaphoreType.DMA((4, 3)),
            pltpu.SemaphoreType.DMA((4, 3)),
        ]
        self.first_outs = [
            jax.ShapeDtypeStruct((2, n_a, D), BF16),
            jax.ShapeDtypeStruct((2, 4, n_b // 4, D), BF16),
        ]
        self.scratch = [
            pltpu.VMEM((2, 3, n_a // 4, D), BF16),
            pltpu.VMEM((2, 3, n_b // 4, D), BF16),
            pltpu.VMEM((2, 4, n_a // 4, D), BF16),
            pltpu.VMEM((2, 4, n_b // 4, D), BF16),
            pltpu.SemaphoreType.DMA((16, 3)),
            pltpu.SemaphoreType.DMA((16, 3)),
        ]
        self.outs = [jax.ShapeDtypeStruct((2, self.rows, D), BF16)]
        if shared_rows:
            self.outs.append(jax.ShapeDtypeStruct((4, 2, shared_rows, D), BF16))

    def helpers(self, g_send, g_recv):
        mine = {a: lax.axis_index(a) for a in ("x", "y", "z")}
        group = [0]

        def send_all(axis, src, dst):
            g = group[0]
            group[0] += 1
            copies = []
            for off in (2, 1, 3):
                peer = lax.rem(mine[axis] + off, 4)
                c = pltpu.make_async_remote_copy(
                    src_ref=src(peer, off),
                    dst_ref=dst(off - 1),
                    send_sem=g_send.at[g, off - 1],
                    recv_sem=g_recv.at[g, off - 1],
                    device_id={axis: peer},
                    device_id_type=MESH,
                )
                c.start()
                copies.append(c)
            return copies

        def wait(copies):
            for c in copies:
                c.wait()

        def add(dest, terms, rows, lead=None):
            step = 32 if rows % 32 == 0 else 16

            @pl.loop(0, rows, step=step)
            def _(r):
                at = pl.ds(pl.multiple_of(r, step), step)
                for b in range(lead or 1):
                    key = (b, at) if lead else (at,)
                    total = terms[0][key].astype(F32)
                    for t in terms[1:]:
                        total = total + t[key].astype(F32)
                    dest[key] = total.astype(BF16)

        def quarter(start, n, i):
            q = n // 4
            return pl.ds(pl.multiple_of(start + i * q, 16), q)

        return send_all, wait, add, quarter

    def first(self, ins, sums, scratch):
        count = len(ins)
        own, other = scratch[0 : 2 * count : 2], scratch[1 : 2 * count : 2]
        packed, ya, xz, s_loc, s_send, s_recv, g_send, g_recv = scratch[2 * count :]
        ta, tb = sums
        send_all, wait, add, quarter = self.helpers(g_send, g_recv)
        core, x, y, z = (lax.axis_index(a) for a in ("core", "x", "y", "z"))
        starts = [sum(self.parts[:k]) for k in range(4)]
        flight = []

        def begin(ready):
            while len(flight) < 4 and starts[len(flight)] + self.parts[len(flight)] <= ready:
                k = len(flight)
                at, n = starts[k], self.parts[k]
                if k < 2:
                    c = send_all(
                        "y", lambda p, o: packed.at[o, pl.ds(at, n), :], lambda s: ya.at[k, s]
                    )
                else:
                    c = send_all(
                        "xz"[k - 2],
                        lambda p, o: packed.at[:, quarter(at, n, p), :],
                        lambda s: xz.at[k - 2, s],
                    )
                flight.append(c)

        pair = dict(device_id={"core": 1 - core}, device_id_type=MESH)
        copies, locals_ = [], []
        for i in range(count):
            h, c = self.halves[i]
            if self.kinds[i] != "cols":
                for b in range(4):
                    part = lax.rem(y + b, 4) if self.kinds[i] == "whole" else b
                    r = pltpu.make_async_remote_copy(
                        src_ref=ins[i].at[pl.ds(part * 2 * h + (1 - core) * h, h), :],
                        dst_ref=other[i].at[b],
                        send_sem=s_send.at[i, b],
                        recv_sem=s_recv.at[i, b],
                        **pair,
                    )
                    l = pltpu.make_async_copy(
                        ins[i].at[pl.ds(part * 2 * h + core * h, h), :], own[i].at[b], s_loc.at[i, b]
                    )
                    r.start()
                    l.start()
                    copies.append((i, r))
                    locals_.append((i, l))
            else:
                r = pltpu.make_async_remote_copy(
                    src_ref=ins[i].at[pl.ds((1 - core) * h, h), :],
                    dst_ref=other[i],
                    send_sem=s_send.at[i, 0],
                    recv_sem=s_recv.at[i, 0],
                    **pair,
                )
                l = pltpu.make_async_copy(
                    ins[i].at[pl.ds(core * h, h), :], own[i], s_loc.at[i, 0]
                )
                r.start()
                l.start()
                copies.append((i, r))
                locals_.append((i, l))
        yield
        if self.rows > self.used:
            gap = self.rows - self.used
            for b in range(4):
                packed[b, pl.ds(self.used, gap), :] = jnp.zeros((gap, D), BF16)
        for i in range(count):
            for j, c in copies + locals_:
                if j == i:
                    c.wait()
            h, c = self.halves[i]
            at = self.offsets[i]
            tiles = c // 128
            if self.kinds[i] != "cols":

                @pl.loop(0, h, step=16)
                def _(r):
                    row = pl.ds(pl.multiple_of(r, 16), 16)
                    to = pl.ds(pl.multiple_of(at + r, 16), 16)
                    for b in range(4):
                        packed[b, to, :] = own[i][b, row, :] + other[i][b, row, :]

            elif tiles == 4:

                @pl.loop(0, h, step=16)
                def _(r):
                    row = pl.ds(pl.multiple_of(r, 16), 16)
                    to = pl.ds(pl.multiple_of(at + r, 16), 16)
                    for b in range(4):
                        col = pl.ds(b * D, D)
                        packed[b, to, :] = own[i][row, col] + other[i][row, col]

            else:
                q = h // 4
                for g in range(4):
                    for t in range(tiles):
                        k = g * tiles + t
                        for b in range(4):
                            row, col = pl.ds(g * q, q), pl.ds(b * c + t * 128, 128)
                            to, tile = pl.ds(at + k // 4 * q, q), pl.ds(k % 4 * 128, 128)
                            packed[b, to, tile] = own[i][row, col] + other[i][row, col]

            begin(self.offsets[i + 1] if i + 1 < count else self.rows)

        yield
        for k in range(4):
            at, n = starts[k], self.parts[k]
            wait(flight[k])
            if k < 2:
                terms = [packed.at[0, pl.ds(at, n)]] + [ya.at[k, s] for s in range(3)]
                add(ta.at[k], terms, n)
            else:
                i = (x, z)[k - 2]
                terms = [packed.at[:, quarter(at, n, i), :]] + [xz.at[k - 2, s] for s in range(3)]
                add(tb.at[k - 2], terms, n // 4, 4)

    def second(self, sums, outs, scratch):
        ta, tb = sums
        ra, rb, fa, fb, g_send, g_recv = scratch
        out = outs[0]
        send_all, wait, add, quarter = self.helpers(g_send, g_recv)
        core, x, y, z = (lax.axis_index(a) for a in ("core", "x", "y", "z"))
        mine = {"x": x, "z": z}
        pair = dict(device_id={"core": 1 - core}, device_id_type=MESH)
        starts = [sum(self.parts[:k]) for k in range(4)]
        n_a, n_b = self.parts[0], self.parts[2]
        flight = []
        for k in range(2):
            flight.append(
                send_all(
                    "xz"[k], lambda p, _: ta.at[k, quarter(0, n_a, p), :], lambda s: ra.at[k, s]
                )
            )
        for k in range(2):
            flight.append(send_all("y", lambda p, o: tb.at[k, o], lambda s: rb.at[k, s]))
        yield
        for k in range(4):
            wait(flight[k])
            last_axis = "zx"[k % 2]
            here = mine[last_axis]
            held = (fa, fa, fb, fb)[k].at[k % 2]
            if k < 2:
                terms = [ta.at[k, quarter(0, n_a, (x, z)[k]), :]] + [ra.at[k, s] for s in range(3)]
                add(held.at[here], terms, n_a // 4)
            else:
                terms = [tb.at[k - 2, 0]] + [rb.at[k - 2, s] for s in range(3)]
                add(held.at[here], terms, n_b // 4)
            flight[k] = send_all(last_axis, lambda p, _: held.at[here], lambda s: held.at[here])
        yield
        for k in range(4):
            wait(flight[k])
            held = (fa, fa, fb, fb)[k].at[k % 2]
            n = self.parts[k]
            piece = out.at[core, quarter(starts[k], n, (x, z)[k % 2]), :]
            add(piece, [held.at[j] for j in range(4)], n // 4)
            flight[k] = send_all("xz"[k % 2], lambda p, _: piece, lambda s: piece)
        yield
        for k in range(4):
            wait(flight[k])
        last = pltpu.make_async_remote_copy(
            src_ref=out.at[core],
            dst_ref=out.at[core],
            send_sem=g_send.at[14, 0],
            recv_sem=g_recv.at[14, 0],
            **pair,
        )
        last.start()
        if not self.shared:
            yield
            last.wait()
            return
        every = outs[1]
        start = self.used - self.shared
        every[y, core] = out[core, pl.ds(start, self.shared), :]
        spread = send_all("y", lambda p, _: every.at[y, core], lambda s: every.at[y, core])
        yield
        wait(spread)
        more = pltpu.make_async_remote_copy(
            src_ref=every.at[:, core],
            dst_ref=every.at[:, core],
            send_sem=g_send.at[15, 0],
            recv_sem=g_recv.at[15, 0],
            **pair,
        )
        more.start()
        yield
        last.wait()
        more.wait()

    def unpack(self, i, owned, dests):
        h, c = self.halves[i]
        at = self.offsets[i]
        tiles = c // 128
        if tiles == 4:
            for core in range(2):

                @pl.loop(0, h, step=16)
                def _(r):
                    to = pl.ds(pl.multiple_of(core * h + r, 16), 16)
                    row = pl.ds(pl.multiple_of(at + r, 16), 16)
                    dests[0][to, :] = owned[core, row, :].astype(F32)

            return
        q = h // 4
        each = tiles // len(dests)
        for core in range(2):
            for g in range(4):
                for t in range(tiles):
                    k = g * tiles + t
                    value = owned[core, pl.ds(at + k // 4 * q, q), pl.ds(k % 4 * 128, 128)]
                    to = pl.ds(core * h + g * q, q)
                    dests[t // each][to, pl.ds(t % each * 128, 128)] = value.astype(F32)


def write_gradients(late, owned, every, mid, owned_mid, early, owned_early, every_early, channels):
    shapes = [(512, 512), (512, 512)] + [(512, 128)] * 4
    shapes += [(512, 512), (512, 512), (512, channels), (512, channels), (128, 512), (channels, 512)]
    shapes += [(1024, 512), (31, 1024)] + [(1, 512)] * 10
    shapes += [(31, channels), (1, channels), (1, channels), (2, 128)]

    def kernel(o_ref, e_ref, om_ref, oe_ref, ee_ref, *refs):
        (up1, down1, wq, wk, wv, pos, up2, down2, cg0, cg1, out, cgd, proj, taps) = refs[:14]
        vectors, refs = refs[14:24], refs[24:]
        gate_taps, gain, shift, bias, small = refs
        late.unpack(0, o_ref, [up1])
        late.unpack(1, o_ref, [down1])
        late.unpack(2, o_ref, [wq, wk, wv])
        late.unpack(3, o_ref, [small])
        late.unpack(4, o_ref, [pos])
        early.unpack(0, oe_ref, [up2])
        early.unpack(1, oe_ref, [down2])
        mid.unpack(0, om_ref, [cg0])
        mid.unpack(1, om_ref, [cg1])
        mid.unpack(2, om_ref, [out])
        mid.unpack(3, om_ref, [cgd])
        for y in range(4):
            for core in range(2):

                @pl.loop(0, 128, step=16)
                def _(r):
                    to = pl.ds(pl.multiple_of(y * 256 + core * 128 + r, 16), 16)
                    row = pl.ds(pl.multiple_of(r, 16), 16)
                    proj[to, :] = ee_ref[y, core, row, :].astype(F32)

        rest = jnp.concatenate([e_ref[y, core].astype(F32) for y in range(3) for core in range(2)])
        taps[:, pl.ds(0, 512)] = rest[0:31]
        taps[:, pl.ds(512, 512)] = rest[32:63]
        for k in range(10):
            vectors[k][...] = rest[64 + k : 65 + k]
        gate_taps[...] = small[pl.ds(0, 31), :]
        gain[...] = small[pl.ds(32, 1), :]
        shift[...] = small[pl.ds(33, 1), :]
        bias[...] = small[pl.ds(34, 2), pl.ds(0, 128)]

    return pl.pallas_call(
        kernel,
        out_shape=[jax.ShapeDtypeStruct(s, F32) for s in shapes],
        in_specs=[VM] * 5,
        out_specs=[VM] * len(shapes),
        scratch_shapes=[pltpu.VMEM((128, channels), F32)],
        compiler_params=pltpu.CompilerParams(vmem_limit_bytes=48 * 2**20),
        name="write_gradients",
    )(owned, every, owned_mid, owned_early, every_early)


def reduce_gradients(arrays, smalls, vectors, plan, earlier, before, cid):
    count = len(arrays)
    little = len(smalls) + len(vectors)

    def kernel(*refs):
        ins, refs = refs[:count], refs[count:]
        gate_taps, gain, shift, bias, pos, merge_taps = refs[: len(smalls)]
        rows, refs = refs[len(smalls) : little], refs[little:]
        begun, refs = refs[:2], refs[2:]
        outs, early, refs = refs[:2], refs[2:3], refs[3:]
        sums, refs = refs[:2], refs[2:]
        small_f, shared_f, small, wide_pos, shared = refs[:5]
        refs = refs[5:]
        n1, n2 = len(plan.first_scratch), len(plan.scratch)
        one = plan.first([*ins, small, wide_pos, shared], sums, refs[:n1])
        old = earlier.second(begun, early, refs[n1 + n2 :])
        small_f[...] = jnp.zeros_like(small_f)
        small_f[pl.ds(0, 32), :] = gate_taps[...]
        small_f[pl.ds(32, 1), :] = gain[...]
        small_f[pl.ds(33, 1), :] = shift[...]
        small_f[pl.ds(34, 2), pl.ds(0, 128)] = bias[pl.ds(0, 2), :]
        small[...] = small_f[...].astype(BF16)
        wide_pos[...] = jnp.zeros_like(wide_pos)
        wide_pos[:, pl.ds(0, 128)] = pos[...].astype(BF16)
        shared_f[...] = jnp.zeros_like(shared_f)
        shared_f[pl.ds(0, 32), :] = merge_taps[:, pl.ds(0, D)]
        shared_f[pl.ds(32, 32), :] = merge_taps[:, pl.ds(D, D)]
        for k, v in enumerate(rows):
            shared_f[pl.ds(64 + k, 1), :] = v[...]
        shared[...] = shared_f[...].astype(BF16)
        greet(y=True, xz=True, pair=True)
        next(old)
        next(one)
        next(old)
        next(one)
        next(old)
        for _ in one:
            pass
        two = plan.second(sums, outs, refs[n1 : n1 + n2])
        next(two)
        next(old)
        next(two)
        for _ in old:
            pass
        for _ in two:
            pass

    outs = pl.pallas_call(
        kernel,
        out_shape=plan.outs + earlier.outs,
        in_specs=[ANY] * count + [VM] * (little + 2),
        out_specs=[VM] * 3,
        scratch_shapes=[pltpu.VMEM(o.shape, BF16) for o in plan.first_outs]
        + [
            pltpu.VMEM((128, GATE), F32),
            pltpu.VMEM((128, D), F32),
            pltpu.VMEM((128, GATE), BF16),
            pltpu.VMEM((D, D), BF16),
            pltpu.VMEM((128, D), BF16),
        ]
        + plan.first_scratch
        + plan.scratch
        + earlier.scratch,
        compiler_params=params(cid, 56),
        name="reduce_gradients",
    )(*arrays, *smalls, *vectors, *before)
    return outs


def local(
    features,
    lengths,
    first_gain,
    first_shift,
    first_up,
    first_down,
    attn_gain,
    attn_shift,
    w_query,
    w_key,
    w_value,
    w_pos,
    bias_content,
    bias_position,
    attn_out,
    cgmlp_gain,
    cgmlp_shift,
    cgmlp_up,
    gate_gain,
    gate_shift,
    gate_taps,
    cgmlp_down,
    merge_taps,
    merge_proj,
    second_gain,
    second_shift,
    second_up,
    second_down,
    final_gain,
    final_shift,
    cotangent,
):
    frames = ROWS * GROUP
    channels = gate_gain.shape[0]
    me = lax.axis_index("y")
    length = lengths[0]
    live = (jnp.arange(ROWS, dtype=jnp.int32) + me * ROWS < length).astype(F32)[:, None]
    mask = jnp.where(jnp.arange(frames, dtype=jnp.int32) < length, 0.0, -1e30)[None].astype(F32)
    vec = lambda v: v.astype(F32)[None]
    sin, cos = position_factors(frames, D)
    biases = jnp.concatenate(
        [
            bias_content.astype(F32).reshape(1, 128),
            bias_position.astype(F32).reshape(1, 128),
            jnp.zeros((6, 128), F32),
        ]
    )
    small = jnp.concatenate(
        [gate_taps, gate_gain[None], gate_shift[None], jnp.zeros((31, channels), BF16)]
    )
    wide = jnp.concatenate([w_query, w_key, w_value], axis=1)
    halves = cgmlp_up[:, 0], cgmlp_up[:, 1]
    up1, down1, qkv_w, cg0, cg1, small_all = gather_weights(
        (first_up, first_down, wide, halves[0], halves[1], small),
        ("cols", "rows", "cols", "cols", "cols", "cols"),
        ("B", "C", "A", "A", "B", "A"),
        0,
    )
    flat = lambda w: w.reshape(-1, w.shape[-1])
    down1 = flat(down1)
    small_f = small_all.astype(F32)
    gate_taps_f = small_f[:32]
    gate_gain_f, gate_shift_f = small_f[31:32], small_f[32:33]
    merge_taps_f = jnp.pad(merge_taps.astype(F32), ((0, 1), (0, 0)))

    start = features.astype(F32)
    u1, inv1 = unit_norm(start)
    in1 = (u1 * vec(first_gain) + vec(first_shift)).astype(BF16)
    act1 = product(in1, up1)
    hid1 = (act1 * jax.nn.sigmoid(act1)).astype(BF16)
    middle = start + 0.5 * product(hid1, down1)
    u2, inv2 = unit_norm(middle)
    attn_in = (u2 * vec(attn_gain) + vec(attn_shift)).astype(BF16)
    cg_in = (u2 * vec(cgmlp_gain) + vec(cgmlp_shift)).astype(BF16)
    qkv_rows = product(attn_in, qkv_w).astype(BF16)
    c0 = product(cg_in, cg0)
    c1 = product(cg_in, cg1)
    root = 1.0 / math.sqrt(2.0)
    phi0 = 0.5 * (1.0 + lax.erf(c0 * root))
    phi1 = 0.5 * (1.0 + lax.erf(c1 * root))
    half0 = c0 * phi0
    ug, invg = unit_norm(c1 * phi1)
    gate_norm = (ug * gate_gain_f + gate_shift_f) * live
    gate_conv, gn_prev, gn_next, qkv, out_w, cg_down = conv_forward(
        gate_norm, gate_taps_f, 1, qkv_rows, (attn_out, cgmlp_down), ("rows", "rows"), ("B", "C")
    )
    out_w, cg_down = flat(out_w), flat(cg_down)
    gate_out = (half0 * gate_conv).astype(BF16)
    attended, attended_rows, weights, up2, down2 = attention_forward(
        qkv, w_pos, biases, mask, sin, cos, (second_up, second_down), ("cols", "rows"), ("B", "C"), 2
    )
    down2 = flat(down2)
    joined = jnp.concatenate([product(attended_rows, out_w), product(gate_out, cg_down)], axis=1)
    joined_live = joined * live
    merge_conv, jl_prev, jl_next = conv_forward(joined_live, merge_taps_f, 3)
    mixed = (joined + merge_conv).astype(BF16)
    merged = middle + product(mixed, merge_proj)
    u3, inv3 = unit_norm(merged)
    in2 = (u3 * vec(second_gain) + vec(second_shift)).astype(BF16)
    act2 = product(in2, up2)
    sig2 = jax.nn.sigmoid(act2)
    hid2 = (act2 * sig2).astype(BF16)
    last = merged + 0.5 * product(hid2, down2)
    u4, inv4 = unit_norm(last)
    encoded = u4 * vec(final_gain) + vec(final_shift)

    cot = cotangent.astype(F32)
    g_final_gain = jnp.sum(cot * u4, 0)
    g_final_shift = jnp.sum(cot, 0)
    g_last = norm_back(cot * vec(final_gain), u4, inv4)
    gy2 = (0.5 * g_last).astype(BF16)
    g_down2 = contract_rows(hid2, gy2)
    g_act2 = (times_transpose(gy2, down2) * sig2 * (1.0 + act2 * (1.0 - sig2))).astype(BF16)
    g_up2 = contract_rows(in2, g_act2)
    g_in2 = times_transpose(g_act2, up2)
    g_second_gain = jnp.sum(g_in2 * u3, 0)
    g_second_shift = jnp.sum(g_in2, 0)
    g_merged = g_last + norm_back(g_in2 * vec(second_gain), u3, inv3)
    gm = g_merged.astype(BF16)
    g_merge_proj = contract_rows(mixed, gm)
    gx = times_transpose(gm, merge_proj)
    merge_back, g_merge_taps = conv_backward(gx, joined_live, jl_prev, jl_next, merge_taps_f, 4)
    g_joined = (gx + live * merge_back).astype(BF16)
    ga, gb = g_joined[:, :D], g_joined[:, D:]
    g_attn_out = contract_rows(attended_rows, ga)
    g_attended_rows = times_transpose(ga, out_w).astype(BF16)
    g_cg_down = contract_rows(gate_out, gb)
    gg = times_transpose(gb, cg_down)
    g_conv = gg * half0
    early = [a.astype(BF16) for a in (g_up2, g_down2, g_merge_proj)]
    plan_early = Reduction(
        [a.shape for a in early], ("cols", "rows", "whole"), (64, 64, 256, 256), 128
    )
    g_norm_raw, g_gate_taps, g_attended, *begun = conv_backward(
        g_conv, gate_norm, gn_prev, gn_next, gate_taps_f, 5, g_attended_rows, early, plan_early
    )
    g_gate_norm = g_norm_raw * live
    g_gate_gain = jnp.sum(g_gate_norm * ug, 0)
    g_gate_shift = jnp.sum(g_gate_norm, 0)
    g_half1 = norm_back(g_gate_norm * gate_gain_f, ug, invg)
    density = 1.0 / math.sqrt(2.0 * math.pi)
    g_c0 = (gg * gate_conv * (phi0 + c0 * (density * jnp.exp(-0.5 * c0 * c0)))).astype(BF16)
    g_c1 = (g_half1 * (phi1 + c1 * (density * jnp.exp(-0.5 * c1 * c1)))).astype(BF16)
    g_cg0 = contract_rows(cg_in, g_c0)
    g_cg1 = contract_rows(cg_in, g_c1)
    g_cg_in = times_transpose(g_c0, cg0) + times_transpose(g_c1, cg1)
    mid = [a.astype(BF16) for a in (g_cg0, g_cg1, g_attn_out, g_cg_down)]
    plan_mid = Reduction(
        [a.shape for a in mid], ("cols", "cols", "rows", "rows"), (64, 64, 256, 256)
    )
    g_qkv, g_w_pos, g_bias, *begun_mid = attention_backward(
        qkv, weights, attended, g_attended, w_pos, biases, sin, cos, mid, plan_mid, plan_early,
        begun, 6,
    )
    begun_mid, (owned_early, every_early) = begun_mid[:2], begun_mid[2:]
    g_attn_in = times_transpose(g_qkv, qkv_w)
    g_wide = contract_rows(attn_in, g_qkv)
    g_attn_gain = jnp.sum(g_attn_in * u2, 0)
    g_attn_shift = jnp.sum(g_attn_in, 0)
    g_cgmlp_gain = jnp.sum(g_cg_in * u2, 0)
    g_cgmlp_shift = jnp.sum(g_cg_in, 0)
    g_middle = g_merged + norm_back(
        g_attn_in * vec(attn_gain) + g_cg_in * vec(cgmlp_gain), u2, inv2
    )
    gy1 = (0.5 * g_middle).astype(BF16)
    sig1 = jax.nn.sigmoid(act1)
    g_down1 = contract_rows(hid1, gy1)
    g_act1 = (times_transpose(gy1, down1) * sig1 * (1.0 + act1 * (1.0 - sig1))).astype(BF16)
    g_up1 = contract_rows(in1, g_act1)
    g_in1 = times_transpose(g_act1, up1)
    g_first_gain = jnp.sum(g_in1 * u1, 0)
    g_first_shift = jnp.sum(g_in1, 0)
    g_features = g_middle + norm_back(g_in1 * vec(first_gain), u1, inv1)

    late = [a.astype(BF16) for a in (g_up1, g_down1, g_wide)]
    plan_late = Reduction(
        [a.shape for a in late] + [(128, GATE), (D, D), (128, D)],
        ("cols", "rows", "cols", "cols", "cols", "whole"),
        (128, 128, 320, 320),
        16,
    )
    vectors = (
        g_first_gain, g_first_shift, g_attn_gain, g_attn_shift, g_cgmlp_gain, g_cgmlp_shift,
        g_second_gain, g_second_shift, g_final_gain, g_final_shift,
    )
    owned, every, owned_mid = reduce_gradients(
        late,
        (g_gate_taps, g_gate_gain[None], g_gate_shift[None], g_bias, g_w_pos, g_merge_taps),
        [v[None] for v in vectors],
        plan_late,
        plan_mid,
        begun_mid,
        7,
    )
    (
        d_up1, d_down1, d_query, d_key, d_value, d_pos, d_up2, d_down2, d_cg0, d_cg1, d_out,
        d_cg_down, d_proj, d_taps, *vectors, d_gate_taps, d_gain, d_shift, d_bias,
    ) = write_gradients(
        plan_late, owned, every, plan_mid, owned_mid, plan_early, owned_early, every_early, channels
    )
    vectors = [v.reshape(D) for v in vectors]
    return (
        encoded,
        g_features,
        vectors[0],
        vectors[1],
        d_up1,
        d_down1,
        vectors[2],
        vectors[3],
        d_query,
        d_key,
        d_value,
        d_pos,
        d_bias[0].reshape(2, 64),
        d_bias[1].reshape(2, 64),
        d_out,
        vectors[4],
        vectors[5],
        jnp.stack([d_cg0, d_cg1], axis=1),
        d_gain.reshape(channels),
        d_shift.reshape(channels),
        d_gate_taps,
        d_cg_down,
        d_taps,
        d_proj,
        vectors[6],
        vectors[7],
        d_up2,
        d_down2,
        vectors[8],
        vectors[9],
    )


def solution(mesh):
    devices = mesh.devices.reshape(4, 4, 2, GROUP)
    fine = Mesh(devices, ("z", "x", "core", "y"))
    rows = P(("z", "x", "core", "y"), None)
    column, row = P(None, "y"), P("y", None)
    placed = (
        rows,
        P(("z", "x", "core")),
        P(),
        P(),
        column,
        row,
        P(),
        P(),
        column,
        column,
        column,
        column,
        row,
        row,
        row,
        P(),
        P(),
        P(None, None, "y"),
        P("y"),
        P("y"),
        column,
        row,
        P(),
        P(),
        P(),
        P(),
        column,
        row,
        P(),
        P(),
        rows,
    )
    return jax.shard_map(
        local,
        mesh=fine,
        in_specs=placed,
        out_specs=(rows,) + (rows,) + placed[2:30],
        check_vma=False,
    )
```

```python
import math

import jax
import jax.numpy as jnp
from jax import lax
from jax.experimental import pallas as pl
from jax.experimental.pallas import tpu as pltpu
from jax.sharding import Mesh, PartitionSpec as P

GATE = 1536
KERNEL = 31
D = 512
ROWS = 320
HALO = 16
GROUP = 4
EPS = 1e-05
F32 = jnp.float32
BF16 = jnp.bfloat16
MESH = pl.DeviceIdType.MESH
ANY = pl.BlockSpec(memory_space=pl.ANY)
VM = pl.BlockSpec(memory_space=pltpu.VMEM)


def product(a, b):
    return jnp.dot(a, b, preferred_element_type=F32)


def contract_rows(a, b):
    return lax.dot_general(a, b, (((0,), (0,)), ((), ())), preferred_element_type=F32)


def times_transpose(a, b):
    return lax.dot_general(a, b, (((1,), (1,)), ((), ())), preferred_element_type=F32)


def unit_norm(rows):
    center = rows - jnp.mean(rows, -1, keepdims=True)
    inverse = lax.rsqrt(jnp.mean(center * center, -1, keepdims=True) + EPS)
    return center * inverse, inverse


def norm_back(scaled, unit, inverse):
    inner = (
        scaled
        - jnp.mean(scaled, -1, keepdims=True)
        - unit * jnp.mean(scaled * unit, -1, keepdims=True)
    )
    return inner * inverse


def params(cid, vmem=48, **more):
    return pltpu.CompilerParams(
        collective_id=cid, has_side_effects=True, vmem_limit_bytes=vmem * 2**20, **more
    )


def ring():
    me = lax.axis_index("y")
    return me, lax.rem(me + 1, GROUP), lax.rem(me + GROUP - 1, GROUP), lax.rem(me + 2, GROUP)


def to_y(where):
    return dict(device_id={"y": where}, device_id_type=MESH)


def greet_ring(offsets):
    me = lax.axis_index("y")
    barrier = pltpu.get_barrier_semaphore()
    for off in offsets:
        pl.semaphore_signal(barrier, inc=1, **to_y(lax.rem(me + off, GROUP)))
    pl.semaphore_wait(barrier, len(offsets))


def greet(y=False, xz=False, pair=False):
    barrier = pltpu.get_barrier_semaphore()
    count = 0
    for axis in (("y",) if y else ()) + (("x", "z") if xz else ()):
        me = lax.axis_index(axis)
        for off in (1, 2, 3):
            where = {axis: lax.rem(me + off, 4)}
            pl.semaphore_signal(barrier, inc=1, device_id=where, device_id_type=MESH)
            count += 1
    if pair:
        where = {"core": 1 - lax.axis_index("core")}
        pl.semaphore_signal(barrier, inc=1, device_id=where, device_id_type=MESH)
        count += 1
    pl.semaphore_wait(barrier, count)


class Gather:
    def __init__(self, shards, kinds, entries):
        self.kinds = kinds
        self.entries = entries
        self.shapes = [s.shape for s in shards]
        count = len(entries)
        self.outs = []
        for s, kind in zip(shards, kinds):
            rows, cols = s.shape
            shape = (GROUP, rows, cols) if kind == "rows" else (rows, GROUP * cols)
            self.outs.append(jax.ShapeDtypeStruct(shape, s.dtype))
        self.scratch = [
            pltpu.SemaphoreType.DMA((count,)),
            pltpu.SemaphoreType.DMA((count, 10)),
            pltpu.SemaphoreType.DMA((count, 10)),
        ]

    def open(self, srcs, dsts, scratch):
        local_sem, send, recv = scratch
        core, x, y, z = (lax.axis_index(a) for a in ("core", "x", "y", "z"))
        mine = {"x": x, "y": y, "z": z}
        pair = dict(device_id={"core": 1 - core}, device_id_type=MESH)

        def spot(e, slot, slots, start, size, lane=None):
            i, first, width, _ = self.entries[e]
            cols = self.shapes[i][1]
            if self.kinds[i] == "rows":
                at = pl.ds(first, width) if lane is None else lane
                return dsts[i].at[pl.ds(slot, slots), pl.ds(start, size), at]
            return dsts[i].at[pl.ds(start, size), pl.ds(slot * cols, slots * cols)]

        def cut(e, level):
            i, first, width, route = self.entries[e]
            half = self.shapes[i][0] // 2
            if level == 2 or route == "A":
                return core * half, half, None
            if half % 256:
                lane = pl.ds(pl.multiple_of(z * (width // 4), 128), width // 4)
                row, size = core * half + x * (half // 4), half // 4
                if level == 0:
                    return row, size, lane
                return (row, size, None) if route == "B" else (core * half, half, lane)
            a, b = (x, z) if route == "B" else (z, x)
            if level == 0:
                return core * half + (a * 4 + b) * (half // 16), half // 16, None
            return core * half + a * (half // 4), half // 4, None

        def remote(src, dst, e, k, where):
            return pltpu.make_async_remote_copy(
                src_ref=src, dst_ref=dst, send_sem=send.at[e, k], recv_sem=recv.at[e, k], **where
            )

        def spread(e, axis, level, k):
            at = spot(e, 1, 3, *cut(e, level))
            copies = []
            for off in (2, 1, 3):
                where = dict(device_id={axis: lax.rem(mine[axis] + off, 4)}, device_id_type=MESH)
                copies.append(remote(at, at, e, k + off - 1, where))
                copies[-1].start()
            return copies

        def to_pair(e):
            at = spot(e, 1, 3, *cut(e, 2))
            c = remote(at, at, e, 9, pair)
            c.start()
            return c

        flight, level = {}, {}

        def start(e):
            i, first, width, _ = self.entries[e]
            row, size, lane = cut(e, 0)
            at = pl.ds(first, width) if lane is None else lane
            piece = srcs[i].at[pl.ds(row, size), at]
            copies = []
            for off in (2, 1, 3):
                there = spot(e, 4 - off, 1, row, size, lane)
                there = there.at[0] if self.kinds[i] == "rows" else there
                copies.append(remote(piece, there, e, off - 1, to_y(lax.rem(y + off, 4))))
                copies[-1].start()
            there = spot(e, 0, 1, 0, self.shapes[i][0])
            there = there.at[0] if self.kinds[i] == "rows" else there
            own = pltpu.make_async_copy(srcs[i].at[:, pl.ds(first, width)], there, local_sem.at[e])
            own.start()
            flight[e], level[e] = copies, 0
            return own

        def step(e):
            for c in flight[e]:
                c.wait()
            route, at = self.entries[e][3], level[e]
            if route == "A" and at == 0:
                at = 2
            if at == 0:
                flight[e] = spread(e, "z" if route == "B" else "x", 0, 3)
            elif at == 1:
                flight[e] = spread(e, "x" if route == "B" else "z", 1, 6)
            elif at == 2:
                flight[e] = [to_pair(e)]
            level[e] = at + 1

        return start, step


def split_copies(src, dst, send, recv, local_sem):
    me = lax.axis_index("y")
    width = src.shape[1] // GROUP
    there = dst.at[pl.ds(pl.multiple_of(me * ROWS, ROWS), ROWS), :]
    copies = []
    for off in (2, 1, 3):
        c = pltpu.make_async_remote_copy(
            src_ref=src.at[:, pl.ds(off * width, width)],
            dst_ref=there,
            send_sem=send.at[off],
            recv_sem=recv.at[off],
            **to_y(lax.rem(me + off, GROUP)),
        )
        c.start()
        copies.append(c)
    own = pltpu.make_async_copy(src.at[:, pl.ds(0, width)], there, local_sem)
    own.start()
    copies.append(own)
    return copies


def start_halo(edges, prev, nxt, send, recv, slots):
    _, up, down, _ = ring()
    cols = prev.shape[1]
    w = cols // GROUP
    turns = ((w, 0, 3 * w), (0, 3 * w, w)) if slots else ((0, 0, cols),)
    copies = []
    for t, (here, there, size) in enumerate(turns):
        for side, ref, where in ((1, prev, up), (0, nxt, down)):
            a, b = (here, there) if side else (there, here)
            c = pltpu.make_async_remote_copy(
                src_ref=edges.at[side, :, pl.ds(a, size)],
                dst_ref=ref.at[:, pl.ds(b, size)],
                send_sem=send.at[side, t],
                recv_sem=recv.at[side, t],
                **to_y(where),
            )
            c.start()
            copies.append(c)
    return copies


def lanes(b):
    return pl.ds(pl.multiple_of(b * 128, 128), 128)


CHUNK = 64


def conv_block(pad, taps, b, flip):
    weights = [taps[pl.ds(KERNEL - 1 - o if flip else o, 1), lanes(b)] for o in range(KERNEL)]
    for r in range(0, ROWS, CHUNK):
        total = None
        for o in range(KERNEL):
            term = weights[o] * pad[b, pl.ds(r + o + 1, CHUNK), :]
            total = term if total is None else total + term
        yield r, total


def taps_block(pad, g_pad, b, out):
    sums = [None] * KERNEL
    for r in range(0, ROWS, CHUNK):
        g = g_pad[b, pl.ds(HALO + r, CHUNK), :]
        for o in range(KERNEL):
            term = g * pad[b, pl.ds(r + o + 1, CHUNK), :]
            term = jnp.sum(term.reshape(CHUNK // 8, 8, 128), 0)
            sums[o] = term if sums[o] is None else sums[o] + term
    for o in range(KERNEL):
        out[pl.ds(o, 1), lanes(b)] = jnp.sum(sums[o], 0, keepdims=True)


def fill_middle(x_ref, pad, blocks):
    @pl.loop(0, blocks)
    def _(b):
        pad[b, pl.ds(HALO, ROWS), :] = x_ref[:, lanes(b)].astype(F32)


def fill_ends(prev, nxt, pad, blocks):
    me = lax.axis_index("y")
    has_prev = jnp.where(me > 0, 1.0, 0.0)
    has_next = jnp.where(me < GROUP - 1, 1.0, 0.0)

    @pl.loop(0, blocks)
    def _(b):
        pad[b, pl.ds(0, HALO), :] = prev[:, lanes(b)].astype(F32) * has_prev
        pad[b, pl.ds(HALO + ROWS, HALO), :] = nxt[:, lanes(b)].astype(F32) * has_next


def set_edges(x_ref, edges):
    edges[0] = x_ref[pl.ds(0, HALO), :].astype(BF16)
    edges[1] = x_ref[pl.ds(ROWS - HALO, HALO), :].astype(BF16)


def conv_forward(x, taps, cid):
    cols = x.shape[1]
    blocks = cols // 128

    def kernel(x_ref, t_ref, o_ref, pad, edges, prev, nxt, hs, hr):
        greet_ring((1, 3))
        set_edges(x_ref, edges)
        halos = start_halo(edges, prev, nxt, hs, hr, False)
        fill_middle(x_ref, pad, blocks)
        for c in halos:
            c.wait()
        fill_ends(prev, nxt, pad, blocks)

        @pl.loop(0, blocks)
        def _(blk):
            for r, value in conv_block(pad, t_ref, blk, False):
                o_ref[pl.ds(r, CHUNK), lanes(blk)] = value

    return pl.pallas_call(
        kernel,
        out_shape=[
            jax.ShapeDtypeStruct((ROWS, cols), F32),
            jax.ShapeDtypeStruct((blocks, ROWS + 2 * HALO, 128), F32),
        ],
        in_specs=[VM, VM],
        out_specs=[VM, VM],
        scratch_shapes=[
            pltpu.VMEM((2, HALO, cols), BF16),
            pltpu.VMEM((HALO, cols), BF16),
            pltpu.VMEM((HALO, cols), BF16),
            pltpu.SemaphoreType.DMA((2, 2)),
            pltpu.SemaphoreType.DMA((2, 2)),
        ],
        compiler_params=params(cid),
        name="conv_forward",
    )(x, taps)


def erf(v):
    v = jnp.clip(v, -3.832506856900711, 3.832506856900711)
    w = v * v
    top = jnp.full_like(w, -2.72614225801306e-10)
    for c in (
        2.77068142495902e-08, -2.10102402082508e-06, -5.69250639462346e-05, -7.34990630326855e-04,
        -2.95459980854025e-03, -1.60960333262415e-02,
    ):
        top = top * w + c
    low = jnp.full_like(w, -1.45660718464996e-05)
    for c in (-2.13374055278905e-04, -1.68282697438203e-03, -7.37332916720468e-03, -1.42647390514189e-02):
        low = low * w + c
    return v * top / low


def prepare(vectors, w_query, w_key, w_value, gate_taps, gate_gain, gate_shift):
    count = len(vectors)
    cols = gate_taps.shape[1]

    def kernel(*refs):
        wq, wk, wv, taps, gain, shift = refs[count : count + 6]
        rows, wide, small, small_f = refs[count + 6 :]
        rows[...] = jnp.zeros_like(rows)
        for k in range(count):
            rows[pl.ds(k, 1), :] = refs[k][...].astype(F32).reshape(1, D)
        for k, w in enumerate((wq, wk, wv)):
            wide[:, pl.ds(k * 128, 128)] = w[...]
        small_f[...] = jnp.zeros_like(small_f)
        small_f[pl.ds(0, KERNEL), :] = taps[...].astype(F32)
        small_f[pl.ds(31, 1), :] = gain[...].astype(F32).reshape(1, cols)
        small_f[pl.ds(32, 1), :] = shift[...].astype(F32).reshape(1, cols)
        small[...] = small_f[...].astype(BF16)

    return pl.pallas_call(
        kernel,
        out_shape=[
            jax.ShapeDtypeStruct((16, D), F32),
            jax.ShapeDtypeStruct((D, 384), BF16),
            jax.ShapeDtypeStruct((64, cols), BF16),
        ],
        in_specs=[VM] * (count + 6),
        out_specs=[VM] * 3,
        scratch_shapes=[pltpu.VMEM((64, cols), F32)],
        name="prepare",
    )(*vectors, w_query, w_key, w_value, gate_taps, gate_gain, gate_shift)


def front(features, live, vectors, shards, cid):
    kinds = ("rows", "rows", "cols", "cols", "cols", "cols", "rows", "rows", "cols", "rows")
    up1, down1, wide, cg0, cg1, small, out, cgd, up2, down2 = range(10)
    half = D // 2
    entries = (
        (up1, 0, half, "A"),
        (down1, 0, half, "A"),
        (up1, half, half, "B"),
        (down1, half, half, "C"),
        (wide, 0, 384, "B"),
        (cg0, 0, 384, "C"),
        (cg1, 0, 384, "A"),
        (small, 0, 384, "A"),
        (out, 0, D, "B"),
        (cgd, 0, D, "C"),
        (up2, 0, D, "B"),
        (down2, 0, D, "C"),
    )
    plan = Gather(shards, kinds, entries)
    blocks = GATE // 128
    hidden = GROUP * D

    def kernel(*refs):
        x_ref, live_ref, v_ref = refs[:3]
        srcs, refs = refs[3:13], refs[13:]
        middle, inv, gate_out = refs[:3]
        act_out, c0_out, c1_out, ug_out, conv_out, pad_out, qkv_out = refs[3:10]
        w_out, refs = refs[10:20], refs[20:]
        w_in, refs = refs[:6], refs[6:]
        act, c0, c1, ug, conv, pad, qkv, acc, cg_in, half, taps, edges, prev, nxt = refs[:14]
        hs, hr, ss, sr, sl, out_sem = refs[14:20]
        dsts = [*w_in, *w_out[6:]]
        start, step = plan.open(srcs, dsts, refs[20:])
        greet(y=True, xz=True, pair=True)
        own = {}
        for e in (2, 3, 4, 5, 0, 1, 10, 11, 8, 9, 6, 7):
            own[e] = start(e)
        saves = []

        def save(src, dst):
            c = pltpu.make_async_copy(src, dst, out_sem.at[len(saves)])
            c.start()
            saves.append(c)

        rows = x_ref[...].astype(F32)
        unit, _ = unit_norm(rows)
        in1 = (unit * v_ref[pl.ds(0, 1), :] + v_ref[pl.ds(1, 1), :]).astype(BF16)

        def hidden_slot(k):
            at = pl.ds(k * D, D)
            a = product(in1, w_in[up1][k])
            act[:, at] = a
            return product((a * jax.nn.sigmoid(a)).astype(BF16), w_in[down1][k])

        for e in range(4):
            own[e].wait()
        acc[...] = hidden_slot(0)
        for e in (2, 3, 4, 5, 2, 3, 4, 5):
            step(e)
        for e in (0, 1, 2, 3, 10, 11, 8, 9, 0, 1, 2, 3):
            step(e)
        total = acc[...]
        for k in range(1, 4):
            total = total + hidden_slot(k)
        save(act, act_out)
        save(w_in[up1], w_out[up1])
        save(w_in[down1], w_out[down1])
        rows = rows + 0.5 * total
        middle[...] = rows
        unit, _ = unit_norm(rows)
        attn_in = (unit * v_ref[pl.ds(2, 1), :] + v_ref[pl.ds(3, 1), :]).astype(BF16)
        cg_in[...] = (unit * v_ref[pl.ds(4, 1), :] + v_ref[pl.ds(5, 1), :]).astype(BF16)
        for e in (4, 5, 10, 11, 8, 9, 6, 7):
            step(e)
        step(4)
        own[4].wait()
        for k in range(4):
            at = pl.ds(k * 384, 384)
            qkv[:, at] = product(attn_in, w_in[wide][:, at]).astype(BF16)
        waits = split_copies(qkv, qkv_out, ss, sr, sl)
        save(w_in[wide], w_out[wide])
        for e in (6, 7, 5):
            step(e)
            own[e].wait()
        for k in range(3):
            at = pl.ds(k * D, D)
            c1[:, at] = product(cg_in[...], w_in[cg1][:, at])
        save(c1, c1_out)
        save(w_in[cg1], w_out[cg1])
        gain = w_in[small][pl.ds(16, 16), :][15:16].astype(F32)
        shift = w_in[small][pl.ds(32, 16), :][0:1].astype(F32)
        root = 1.0 / math.sqrt(2.0)

        @pl.loop(0, ROWS, step=16)
        def _(r):
            at = pl.ds(pl.multiple_of(r, 16), 16)
            c = c1[at, :]
            unit, inverse = unit_norm(c * (0.5 * (1.0 + erf(c * root))))
            ug[at, :] = unit
            inv[at, :] = inverse
            norm = (unit * gain + shift) * live_ref[at, :]
            for b in range(blocks):
                pad[b, pl.ds(pl.multiple_of(HALO + r, 16), 16), :] = norm[:, b * 128 : b * 128 + 128]

        save(ug, ug_out)
        for side, r in ((0, HALO), (1, ROWS)):
            for b in range(blocks):
                edges[side, :, pl.ds(b * 128, 128)] = pad[b, pl.ds(r, HALO), :].astype(BF16)
        halos = start_halo(edges, prev, nxt, hs, hr, True)
        for k in range(3):
            at = pl.ds(k * D, D)
            c0[:, at] = product(cg_in[...], w_in[cg0][:, at])
        save(c0, c0_out)
        save(w_in[cg0], w_out[cg0])
        save(w_in[small], w_out[small])

        @pl.loop(0, ROWS, step=16)
        def _(r):
            at = pl.ds(pl.multiple_of(r, 16), 16)
            c = c0[at, :]
            half[at, :] = c * (0.5 * (1.0 + erf(c * root)))

        for c in halos:
            c.wait()
        fill_ends(prev, nxt, pad, blocks)
        save(pad, pad_out)
        for e in (10, 11, 8, 9):
            step(e)
        taps[...] = w_in[small][pl.ds(0, 32), :].astype(F32)

        @pl.loop(0, blocks)
        def _(blk):
            for r, value in conv_block(pad, taps, blk, False):
                at = pl.ds(r, CHUNK)
                conv[at, lanes(blk)] = value
                gate_out[at, lanes(blk)] = (value * half[at, lanes(blk)]).astype(BF16)

        save(conv, conv_out)
        for e in (10, 11, 8, 9):
            step(e)
            own[e].wait()
        for c in waits + saves:
            c.wait()

    f32 = lambda *shape: jax.ShapeDtypeStruct(shape, F32)
    pad_shape = (blocks, ROWS + 2 * HALO, 128)
    outs = [f32(ROWS, D), f32(ROWS, 1), jax.ShapeDtypeStruct((ROWS, GATE), BF16)]
    outs += [f32(ROWS, hidden)] + [f32(ROWS, GATE)] * 4 + [f32(*pad_shape)]
    outs += [jax.ShapeDtypeStruct((ROWS * GROUP, 3 * 128), BF16)]
    return pl.pallas_call(
        kernel,
        out_shape=outs + plan.outs,
        in_specs=[VM] * 3 + [ANY] * 10,
        out_specs=[VM] * 3 + [ANY] * 17,
        scratch_shapes=[pltpu.VMEM(o.shape, o.dtype) for o in plan.outs[:6]]
        + [
            pltpu.VMEM((ROWS, hidden), F32),
            pltpu.VMEM((ROWS, GATE), F32),
            pltpu.VMEM((ROWS, GATE), F32),
            pltpu.VMEM((ROWS, GATE), F32),
            pltpu.VMEM((ROWS, GATE), F32),
            pltpu.VMEM(pad_shape, F32),
            pltpu.VMEM((ROWS, 3 * D), BF16),
            pltpu.VMEM((ROWS, D), F32),
            pltpu.VMEM((ROWS, D), BF16),
            pltpu.VMEM((ROWS, GATE), F32),
            pltpu.VMEM((32, GATE), F32),
            pltpu.VMEM((2, HALO, GATE), BF16),
            pltpu.VMEM((HALO, GATE), BF16),
            pltpu.VMEM((HALO, GATE), BF16),
            pltpu.SemaphoreType.DMA((2, 2)),
            pltpu.SemaphoreType.DMA((2, 2)),
            pltpu.SemaphoreType.DMA((GROUP,)),
            pltpu.SemaphoreType.DMA((GROUP,)),
            pltpu.SemaphoreType.DMA,
            pltpu.SemaphoreType.DMA((12,)),
        ]
        + plan.scratch,
        compiler_params=params(cid, 60),
        name="front",
    )(features, live, vectors, *shards)


def conv_backward(g, pad, taps, cid, heads_in=None, arrays=(), plan=None):
    cols = g.shape[1]
    blocks = cols // 128
    extra = heads_in is not None
    count = len(arrays)
    firsts = len(plan.first_outs) if extra else 0

    def kernel(*refs):
        g_ref, pad_in, t_ref = refs[:3]
        if extra:
            h_ref, refs = refs[3], refs[4:]
            ins, refs = refs[:count], refs[count:]
            o_ref, tg_ref, ho_ref = refs[:3]
            sums, refs = refs[3 : 3 + firsts], refs[3 + firsts :]
            g_pad, pad, load_sem, edges, prev, nxt, hs, hr, ss, sr, sl = refs[:11]
            start, riding = plan.first(ins, sums, refs[11:])
        else:
            o_ref, tg_ref = refs[3:5]
            g_pad, pad, load_sem, edges, prev, nxt, hs, hr = refs[5:]
        load = pltpu.make_async_copy(pad_in, pad, load_sem)
        load.start()
        if extra:
            greet(y=True, xz=True, pair=True)
        else:
            greet_ring((1, 3))
        set_edges(g_ref, edges)
        halos = start_halo(edges, prev, nxt, hs, hr, extra)
        waits = split_copies(h_ref, ho_ref, ss, sr, sl) if extra else []
        for i in range(count):
            start(i)
        fill_middle(g_ref, g_pad, blocks)
        tg_ref[pl.ds(24, 8), :] = jnp.zeros((8, cols), F32)
        load.wait()
        parts = ((0, 7), (7, blocks)) if extra else ((0, blocks),)
        for low, high in parts:

            @pl.loop(low, high)
            def _(blk):
                taps_block(pad, g_pad, blk, tg_ref)

            if extra and low == 0:
                next(riding)

        for c in halos:
            c.wait()
        fill_ends(prev, nxt, g_pad, blocks)

        @pl.loop(0, blocks)
        def _(blk):
            for r, value in conv_block(g_pad, t_ref, blk, True):
                o_ref[pl.ds(r, CHUNK), lanes(blk)] = value

        for c in waits:
            c.wait()
        if extra:
            for _ in riding:
                pass

    outs = [jax.ShapeDtypeStruct((ROWS, cols), F32), jax.ShapeDtypeStruct((32, cols), F32)]
    ins = [g, pad, taps]
    scratch = [
        pltpu.VMEM((blocks, ROWS + 2 * HALO, 128), F32),
        pltpu.VMEM((blocks, ROWS + 2 * HALO, 128), F32),
        pltpu.SemaphoreType.DMA,
        pltpu.VMEM((2, HALO, cols), BF16),
        pltpu.VMEM((HALO, cols), BF16),
        pltpu.VMEM((HALO, cols), BF16),
        pltpu.SemaphoreType.DMA((2, 2)),
        pltpu.SemaphoreType.DMA((2, 2)),
    ]
    in_specs, out_specs = [VM, ANY, VM], [VM, VM]
    if extra:
        ins += [heads_in, *arrays]
        in_specs += [ANY] * (1 + count)
        outs.append(
            jax.ShapeDtypeStruct((ROWS * GROUP, heads_in.shape[1] // GROUP), heads_in.dtype)
        )
        outs += plan.first_outs
        out_specs += [ANY] + [VM] * firsts
        scratch += [
            pltpu.SemaphoreType.DMA((GROUP,)),
            pltpu.SemaphoreType.DMA((GROUP,)),
            pltpu.SemaphoreType.DMA,
        ] + plan.first_scratch
    return pl.pallas_call(
        kernel,
        out_shape=outs,
        in_specs=in_specs,
        out_specs=out_specs,
        scratch_shapes=scratch,
        compiler_params=params(cid),
        name="conv_backward",
    )(*ins)


def position_factors(frames, width):
    frequency = jnp.exp(
        jnp.arange(width // 2, dtype=jnp.int32).astype(F32) * (-2.0 * math.log(10000.0) / width)
    )
    steps = jnp.concatenate(
        [32 * jnp.arange(frames // 32, dtype=jnp.int32), jnp.arange(32, dtype=jnp.int32)]
    )
    angles = steps.astype(F32)[:, None] * frequency[None]
    return jnp.sin(angles), jnp.cos(angles)


def fill_table(sin_parts, cos_parts, sin, cos, table):
    frames, half = sin.shape
    sb, cb = sin_parts[pl.ds(frames // 32, 32), :], cos_parts[pl.ds(frames // 32, 32), :]

    @pl.loop(0, frames // 32)
    def _(a):
        at = pl.ds(pl.multiple_of(a * 32, 32), 32)
        sa, ca = sin_parts[pl.ds(a, 1), :], cos_parts[pl.ds(a, 1), :]
        s, c = sa * cb + ca * sb, ca * cb - sa * sb
        sin[at, :] = s
        cos[at, :] = c
        table[at, pl.ds(0, half)] = s.astype(BF16)
        table[at, pl.ds(half, half)] = c.astype(BF16)


def head_mask(h):
    column = lax.broadcasted_iota(jnp.int32, (1, 128), 1)
    return jnp.where((column >= 64 * h) & (column < 64 * h + 64), 1.0, 0.0)


def rotated(query, sin, cos, w_pos):
    z = times_transpose(query, w_pos)
    zs, zc = z[:, : D // 2], z[:, D // 2 :]
    return jnp.concatenate([zc * sin - zs * cos, zs * sin + zc * cos], axis=1).astype(BF16)


def attention_forward(qkv, w_pos, biases, mask, sin, cos, cid):
    frames = qkv.shape[0]

    def kernel(
        x_ref, wp_ref, b_ref, m_ref, sp_ref, cp_ref, o_ref, rows_ref, p_ref,
        p_buf, t_ref, s_ref, c_ref, p_sem, ss, sr, sl,
    ):
        me = lax.axis_index("y")
        greet_ring((1, 2, 3))
        fill_table(sp_ref, cp_ref, s_ref, c_ref, t_ref)
        saves, sends = [], []
        for k in range(GROUP):
            peer = lax.rem(me + 1 + k, GROUP)
            at = pl.ds(pl.multiple_of(peer * ROWS, ROWS), ROWS)
            query = x_ref[at, pl.ds(0, 128)].astype(F32)
            if k >= 2:
                saves[k - 2].wait()
            total = jnp.zeros((ROWS, 128), F32)
            for h in range(2):
                keep = head_mask(h)
                content = ((query + b_ref[pl.ds(0, 1), :]) * (0.125 * keep)).astype(BF16)
                position = ((query + b_ref[pl.ds(1, 1), :]) * (0.125 * keep)).astype(BF16)
                turned = rotated(position, s_ref[at, :], c_ref[at, :], wp_ref[...])
                scores = times_transpose(turned, t_ref[...])
                scores = scores + times_transpose(content, x_ref[:, pl.ds(128, 128)])
                scores = scores + m_ref[...]
                top = jnp.max(scores, -1, keepdims=True)
                weights = jnp.exp(scores - top)
                weights = (weights * (1.0 / jnp.sum(weights, -1, keepdims=True))).astype(BF16)
                p_buf[k % 2, h] = weights
                total = total + product(weights, x_ref[:, pl.ds(256, 128)]) * keep
            o_ref[at, :] = total.astype(BF16)
            save = pltpu.make_async_copy(p_buf.at[k % 2], p_ref.at[:, at, :], p_sem.at[k % 2])
            save.start()
            saves.append(save)
            into = rows_ref.at[:, pl.ds((3 - k) * 128, 128)]
            if k < GROUP - 1:
                c = pltpu.make_async_remote_copy(
                    src_ref=o_ref.at[at, :],
                    dst_ref=into,
                    send_sem=ss.at[k],
                    recv_sem=sr.at[k],
                    **to_y(peer),
                )
            else:
                c = pltpu.make_async_copy(o_ref.at[at, :], into, sl)
            c.start()
            sends.append(c)
        saves[2].wait()
        saves[3].wait()
        for c in sends:
            c.wait()

    return pl.pallas_call(
        kernel,
        in_specs=[VM] * 6,
        out_specs=[VM, ANY, ANY],
        out_shape=[
            jax.ShapeDtypeStruct((frames, 128), BF16),
            jax.ShapeDtypeStruct((ROWS, D), BF16),
            jax.ShapeDtypeStruct((2, frames, frames), BF16),
        ],
        scratch_shapes=[
            pltpu.VMEM((2, 2, ROWS, frames), BF16),
            pltpu.VMEM((frames, D), BF16),
            pltpu.VMEM((frames, D // 2), F32),
            pltpu.VMEM((frames, D // 2), F32),
            pltpu.SemaphoreType.DMA((2,)),
            pltpu.SemaphoreType.DMA((3,)),
            pltpu.SemaphoreType.DMA((3,)),
            pltpu.SemaphoreType.DMA,
        ],
        compiler_params=params(cid),
        name="attention_forward",
    )(qkv, w_pos, biases, mask, sin, cos)


def attention_backward(
    qkv, weights, attended, g_attended, w_pos, biases, sin, cos, plan, begun, factors,
    cid,
):
    frames = qkv.shape[0]

    def kernel(*refs):
        x_ref, p_ref, a_ref, ga_ref, wp_ref, b_ref, sp_ref, cp_ref = refs[:8]
        begun_refs, given, refs = refs[8:10], refs[10:16], refs[16:]
        rows_ref, gw_ref, gb_ref = refs[:3]
        finished, made, refs = refs[3:5], refs[5:9], refs[9:]
        p_buf, gq_buf, kv_buf, gk_acc, gv_acc, p_sem, qs, qr, ql, ks, kr, kl = refs[:12]
        t_ref, s_ref, c_ref = refs[12:15]
        cg_in, g_c0, g_c1, rows_in, gate_in, g_joined = held = refs[15:21]
        results, load_sem, save_sem = refs[21:25], refs[25], refs[26]
        riding = plan.second(begun_refs, finished, refs[27:])
        needed = [
            pltpu.make_async_copy(a, b, load_sem.at[k]) for k, (a, b) in enumerate(zip(given, held))
        ]
        me = lax.axis_index("y")

        def block(k):
            peer = lax.rem(me + 1 + k, GROUP)
            return peer, pl.ds(pl.multiple_of(peer * ROWS, ROWS), ROWS)

        def load(k):
            c = pltpu.make_async_copy(p_ref.at[:, block(k)[1], :], p_buf.at[k % 2], p_sem.at[k % 2])
            c.start()
            return c

        loads = [load(0), load(1)]
        greet(y=True, xz=True, pair=True)
        next(riding)
        fill_table(sp_ref, cp_ref, s_ref, c_ref, t_ref)
        gk_acc[...] = jnp.zeros_like(gk_acc)
        gv_acc[...] = jnp.zeros_like(gv_acc)
        gw_ref[...] = jnp.zeros_like(gw_ref)
        gb_ref[...] = jnp.zeros_like(gb_ref)
        sends = []
        for k in range(GROUP):
            peer, at = block(k)
            query = x_ref[at, pl.ds(0, 128)].astype(F32)
            g_out = ga_ref[at, :]
            dots = g_out.astype(F32) * a_ref[at, :].astype(F32)
            sin_, cos_ = s_ref[at, :], c_ref[at, :]
            g_content = jnp.zeros((ROWS, 128), F32)
            g_position = jnp.zeros((ROWS, 128), F32)
            loads[k].wait()
            for h in range(2):
                keep = head_mask(h)
                content = ((query + b_ref[pl.ds(0, 1), :]) * (0.125 * keep)).astype(BF16)
                position = ((query + b_ref[pl.ds(1, 1), :]) * (0.125 * keep)).astype(BF16)
                g_head = (g_out.astype(F32) * keep).astype(BF16)
                p = p_buf[k % 2, h]
                g_weights = times_transpose(g_head, x_ref[:, pl.ds(256, 128)])
                inner = jnp.sum(dots * keep, -1, keepdims=True)
                g_scores = (p.astype(F32) * (g_weights - inner)).astype(BF16)
                gv_acc[...] += contract_rows(g_head, p)
                gk_acc[...] += contract_rows(content, g_scores)
                g_content = g_content + product(g_scores, x_ref[:, pl.ds(128, 128)]) * keep
                turned = product(g_scores, t_ref[...])
                ts, tc = turned[:, : D // 2], turned[:, D // 2 :]
                g_z = jnp.concatenate([tc * sin_ - ts * cos_, ts * sin_ + tc * cos_], axis=1)
                g_z = g_z.astype(BF16)
                g_position = g_position + product(g_z, wp_ref[...]) * keep
                gw_ref[...] += contract_rows(g_z, position)
                if (k, h) in ((1, 0), (2, 0), (3, 0)):
                    next(riding)
            g_content = g_content * 0.125
            g_position = g_position * 0.125
            gq_buf[at, :] = (g_content + g_position).astype(BF16)
            gb_ref[pl.ds(0, 1), :] += jnp.sum(g_content, 0, keepdims=True)
            gb_ref[pl.ds(1, 1), :] += jnp.sum(g_position, 0, keepdims=True)
            if k < 2:
                loads.append(load(k + 2))
            into = rows_ref.at[:, pl.ds((3 - k) * 384, 128)]
            if k < GROUP - 1:
                c = pltpu.make_async_remote_copy(
                    src_ref=gq_buf.at[at, :],
                    dst_ref=into,
                    send_sem=qs.at[k],
                    recv_sem=qr.at[k],
                    **to_y(peer),
                )
            else:
                c = pltpu.make_async_copy(gq_buf.at[at, :], into, ql)
            c.start()
            sends.append(c)
            if k == 0:
                for c in needed:
                    c.start()
        kv_buf[:, pl.ds(0, 128)] = gk_acc[...].T.astype(BF16)
        kv_buf[:, pl.ds(128, 128)] = gv_acc[...].T.astype(BF16)
        for k in range(GROUP):
            into = rows_ref.at[:, pl.ds((3 - k) * 384 + 128, 256)]
            peer, at = block(k)
            if k < GROUP - 1:
                c = pltpu.make_async_remote_copy(
                    src_ref=kv_buf.at[at, :],
                    dst_ref=into,
                    send_sem=ks.at[k],
                    recv_sem=kr.at[k],
                    **to_y(peer),
                )
            else:
                c = pltpu.make_async_copy(kv_buf.at[at, :], into, kl)
            c.start()
            sends.append(c)
        for c in needed:
            c.wait()
        for k in range(3):
            at = pl.ds(k * D, D)
            results[0][:, at] = contract_rows(cg_in[...], g_c0[:, at]).astype(BF16)
            results[1][:, at] = contract_rows(cg_in[...], g_c1[:, at]).astype(BF16)
            results[3][at, :] = contract_rows(gate_in[:, at], g_joined[:, pl.ds(D, D)]).astype(BF16)
        results[2][...] = contract_rows(rows_in[...], g_joined[:, pl.ds(0, D)]).astype(BF16)
        for k in range(4):
            c = pltpu.make_async_copy(results[k], made[k], save_sem.at[k])
            c.start()
            sends.append(c)
        for _ in riding:
            pass
        for c in sends:
            c.wait()

    shapes = [(D, GATE), (D, GATE), (D, D), (GATE, D)]

    return pl.pallas_call(
        kernel,
        in_specs=[VM, ANY] + [VM] * 8 + [ANY] * 6,
        out_specs=[ANY, VM, VM] + [VM] * 2 + [ANY] * 4,
        out_shape=[
            jax.ShapeDtypeStruct((ROWS, 3 * D), BF16),
            jax.ShapeDtypeStruct((D, 128), F32),
            jax.ShapeDtypeStruct((8, 128), F32),
        ]
        + plan.outs
        + [jax.ShapeDtypeStruct(s, BF16) for s in shapes],
        scratch_shapes=[
            pltpu.VMEM((2, 2, ROWS, frames), BF16),
            pltpu.VMEM((frames, 128), BF16),
            pltpu.VMEM((frames, 256), BF16),
            pltpu.VMEM((128, frames), F32),
            pltpu.VMEM((128, frames), F32),
            pltpu.SemaphoreType.DMA((2,)),
            pltpu.SemaphoreType.DMA((3,)),
            pltpu.SemaphoreType.DMA((3,)),
            pltpu.SemaphoreType.DMA,
            pltpu.SemaphoreType.DMA((3,)),
            pltpu.SemaphoreType.DMA((3,)),
            pltpu.SemaphoreType.DMA,
            pltpu.VMEM((frames, D), BF16),
            pltpu.VMEM((frames, D // 2), F32),
            pltpu.VMEM((frames, D // 2), F32),
        ]
        + [pltpu.VMEM(a.shape, BF16) for a in factors]
        + [pltpu.VMEM(s, BF16) for s in shapes]
        + [pltpu.SemaphoreType.DMA((6,)), pltpu.SemaphoreType.DMA((4,))]
        + plan.scratch,
        compiler_params=params(cid, 58),
        name="attention_backward",
    )(qkv, weights, attended, g_attended, w_pos, biases, sin, cos, *begun, *factors)


class Reduction:
    def __init__(self, shapes, kinds, parts, shared_rows=0):
        self.kinds = kinds
        self.halves = []
        self.offsets = []
        at = 0
        for (rows, cols), kind in zip(shapes, kinds):
            h, c = (rows // 2, cols // 4) if kind == "cols" else (rows // 8, cols)
            if kind == "each":
                h = rows // 2
            self.halves.append((h, c))
            self.offsets.append(at)
            at += h * c // D
        self.used = at
        self.parts = parts
        self.rows = sum(parts)
        self.shared = shared_rows
        count = len(shapes)
        n_a, n_b = max(parts[:2]), max(parts[2:])
        self.first_scratch = []
        for (h, c), kind in zip(self.halves, kinds):
            shape = (h, 4 * c) if kind == "cols" else (4, h, c)
            if kind == "each":
                shape = (4, 2 * h, c)
            self.first_scratch += [pltpu.VMEM(shape, BF16)] * 2
        self.first_scratch += [
            pltpu.VMEM((4, self.rows, D), BF16),
            pltpu.VMEM((2, 3, n_a, D), BF16),
            pltpu.VMEM((2, 3, 4, n_b // 4, D), BF16),
            pltpu.SemaphoreType.DMA((count, 4)),
            pltpu.SemaphoreType.DMA((count, 4)),
            pltpu.SemaphoreType.DMA((count, 4)),
            pltpu.SemaphoreType.DMA((5, 3)),
            pltpu.SemaphoreType.DMA((5, 3)),
        ]
        self.first_outs = [
            jax.ShapeDtypeStruct((2, n_a, D), BF16),
            jax.ShapeDtypeStruct((2, 4, n_b // 4, D), BF16),
        ]
        self.scratch = [
            pltpu.VMEM((2, 3, n_a // 4, D), BF16),
            pltpu.VMEM((2, 3, n_b // 4, D), BF16),
            pltpu.VMEM((2, 4, n_a // 4, D), BF16),
            pltpu.VMEM((2, 4, n_b // 4, D), BF16),
            pltpu.SemaphoreType.DMA((16, 3)),
            pltpu.SemaphoreType.DMA((16, 3)),
        ]
        self.outs = [jax.ShapeDtypeStruct((2, self.rows, D), BF16)]
        if shared_rows:
            self.outs.append(jax.ShapeDtypeStruct((4, 2, shared_rows, D), BF16))

    def helpers(self, g_send, g_recv):
        mine = {a: lax.axis_index(a) for a in ("x", "y", "z")}
        group = [0]

        def send_all(axis, src, dst):
            g = group[0]
            group[0] += 1
            copies = []
            for off in (2, 1, 3):
                peer = lax.rem(mine[axis] + off, 4)
                c = pltpu.make_async_remote_copy(
                    src_ref=src(peer, off),
                    dst_ref=dst(off - 1),
                    send_sem=g_send.at[g, off - 1],
                    recv_sem=g_recv.at[g, off - 1],
                    device_id={axis: peer},
                    device_id_type=MESH,
                )
                c.start()
                copies.append(c)
            return copies

        def wait(copies):
            for c in copies:
                c.wait()

        def add(dest, terms, rows, lead=None):
            step = 32 if rows % 32 == 0 else 16

            @pl.loop(0, rows, step=step)
            def _(r):
                at = pl.ds(pl.multiple_of(r, step), step)
                for b in range(lead or 1):
                    key = (b, at) if lead else (at,)
                    total = terms[0][key].astype(F32)
                    for t in terms[1:]:
                        total = total + t[key].astype(F32)
                    dest[key] = total.astype(BF16)

        def quarter(start, n, i):
            q = n // 4
            return pl.ds(pl.multiple_of(start + i * q, 16), q)

        return send_all, wait, add, quarter

    def first(self, ins, sums, scratch):
        count = len(ins)
        own, other = scratch[0 : 2 * count : 2], scratch[1 : 2 * count : 2]
        packed, ya, xz, s_loc, s_send, s_recv, g_send, g_recv = scratch[2 * count :]
        ta, tb = sums
        send_all, wait, add, quarter = self.helpers(g_send, g_recv)
        core, x, y, z = (lax.axis_index(a) for a in ("core", "x", "y", "z"))
        starts = [sum(self.parts[:k]) for k in range(4)]
        flight = []

        def begin(ready):
            while len(flight) < 4 and starts[len(flight)] + self.parts[len(flight)] <= ready:
                k = len(flight)
                at, n = starts[k], self.parts[k]
                if n == 0:
                    c = []
                elif k < 2:
                    c = send_all(
                        "y",
                        lambda p, o: packed.at[o, pl.ds(at, n), :],
                        lambda s: ya.at[k, s, pl.ds(0, n), :],
                    )
                else:
                    c = send_all(
                        "xz"[k - 2],
                        lambda p, o: packed.at[:, quarter(at, n, p), :],
                        lambda s: xz.at[k - 2, s, :, pl.ds(0, n // 4), :],
                    )
                flight.append(c)

        pair = dict(device_id={"core": 1 - core}, device_id_type=MESH)
        copies, everywhere = [], []

        def start(i):
            h, c = self.halves[i]
            if self.kinds[i] == "each":
                own[i][y] = ins[i][...]
                everywhere.extend(
                    send_all("y", lambda p, _: own[i].at[y], lambda s: own[i].at[y])
                )
                return
            for b in range(1 if self.kinds[i] == "cols" else 4):
                if self.kinds[i] == "cols":
                    theirs = ins[i].at[pl.ds((1 - core) * h, h), :]
                    ours = ins[i].at[pl.ds(core * h, h), :]
                    to, keep = other[i], own[i]
                else:
                    part = lax.rem(y + b, 4) if self.kinds[i] == "whole" else b
                    theirs = ins[i].at[pl.ds(part * 2 * h + (1 - core) * h, h), :]
                    ours = ins[i].at[pl.ds(part * 2 * h + core * h, h), :]
                    to, keep = other[i].at[b], own[i].at[b]
                r = pltpu.make_async_remote_copy(
                    src_ref=theirs,
                    dst_ref=to,
                    send_sem=s_send.at[i, b],
                    recv_sem=s_recv.at[i, b],
                    **pair,
                )
                l = pltpu.make_async_copy(ours, keep, s_loc.at[i, b])
                r.start()
                l.start()
                copies.extend([(i, r), (i, l)])

        return start, self.first_steps(
            own, other, packed, ya, xz, copies, everywhere, begin, flight, sums, s_send, s_recv,
            (send_all, wait, add, quarter),
        )

    def first_steps(
        self, own, other, packed, ya, xz, copies, everywhere, begin, flight, sums, s_send, s_recv,
        helpers,
    ):
        send_all, wait, add, quarter = helpers
        ta, tb = sums
        count = len(own)
        core, x, y, z = (lax.axis_index(a) for a in ("core", "x", "y", "z"))
        pair = dict(device_id={"core": 1 - core}, device_id_type=MESH)
        starts = [sum(self.parts[:k]) for k in range(4)]
        for i in range(count):
            if self.kinds[i] != "each":
                continue
            h, c = self.halves[i]
            wait(everywhere)
            add(other[i].at[0], [own[i].at[j] for j in range(4)], 2 * h)
            r = pltpu.make_async_remote_copy(
                src_ref=other[i].at[0, pl.ds((1 - core) * h, h), :],
                dst_ref=other[i].at[1, pl.ds(0, h), :],
                send_sem=s_send.at[i, 0],
                recv_sem=s_recv.at[i, 0],
                **pair,
            )
            r.start()
            copies.append((i, r))
        if self.rows > self.used:
            gap = self.rows - self.used
            for b in range(4):
                packed[b, pl.ds(self.used, gap), :] = jnp.zeros((gap, D), BF16)
        for i in range(count):
            for j, c in copies:
                if j == i:
                    c.wait()
            h, c = self.halves[i]
            at = self.offsets[i]
            tiles = c // 128
            if self.kinds[i] == "each":
                here = other[i][0, pl.ds(pl.multiple_of(core * h, 16), h), :]
                packed[0, pl.ds(at, h), :] = here + other[i][1, pl.ds(0, h), :]
                for b in range(1, 4):
                    packed[b, pl.ds(at, h), :] = jnp.zeros((h, c), BF16)
            elif self.kinds[i] != "cols":

                @pl.loop(0, h, step=16)
                def _(r):
                    row = pl.ds(pl.multiple_of(r, 16), 16)
                    to = pl.ds(pl.multiple_of(at + r, 16), 16)
                    for b in range(4):
                        packed[b, to, :] = own[i][b, row, :] + other[i][b, row, :]

            elif tiles == 4:

                @pl.loop(0, h, step=16)
                def _(r):
                    row = pl.ds(pl.multiple_of(r, 16), 16)
                    to = pl.ds(pl.multiple_of(at + r, 16), 16)
                    for b in range(4):
                        col = pl.ds(b * D, D)
                        packed[b, to, :] = own[i][row, col] + other[i][row, col]

            else:
                q = h // 4
                for g in range(4):
                    for t in range(tiles):
                        k = g * tiles + t
                        for b in range(4):
                            row, col = pl.ds(g * q, q), pl.ds(b * c + t * 128, 128)
                            to, tile = pl.ds(at + k // 4 * q, q), pl.ds(k % 4 * 128, 128)
                            packed[b, to, tile] = own[i][row, col] + other[i][row, col]

            begin(self.offsets[i + 1] if i + 1 < count else self.rows)

        yield
        for k in range(4):
            at, n = starts[k], self.parts[k]
            wait(flight[k])
            if n and k < 2:
                terms = [packed.at[0, pl.ds(at, n)]] + [ya.at[k, s] for s in range(3)]
                add(ta.at[k], terms, n)
            elif n:
                i = (x, z)[k - 2]
                terms = [packed.at[:, quarter(at, n, i), :]] + [xz.at[k - 2, s] for s in range(3)]
                add(tb.at[k - 2], terms, n // 4, 4)

    def second(self, sums, outs, scratch):
        ta, tb = sums
        ra, rb, fa, fb, g_send, g_recv = scratch
        out = outs[0]
        send_all, wait, add, quarter = self.helpers(g_send, g_recv)
        core, x, y, z = (lax.axis_index(a) for a in ("core", "x", "y", "z"))
        mine = {"x": x, "z": z}
        pair = dict(device_id={"core": 1 - core}, device_id_type=MESH)
        starts = [sum(self.parts[:k]) for k in range(4)]
        flight = []
        for k in range(4):
            n = self.parts[k]
            q = pl.ds(0, n // 4)
            if n == 0:
                c = []
            elif k < 2:
                c = send_all(
                    "xz"[k],
                    lambda p, _: ta.at[k, quarter(0, n, p), :],
                    lambda s: ra.at[k, s, q, :],
                )
            else:
                c = send_all(
                    "y", lambda p, o: tb.at[k - 2, o, q, :], lambda s: rb.at[k - 2, s, q, :]
                )
            flight.append(c)
        yield
        held = [(fa, fa, fb, fb)[k].at[k % 2] for k in range(4)]
        for k in range(4):
            n = self.parts[k]
            if n == 0:
                continue
            wait(flight[k])
            last_axis = "zx"[k % 2]
            here = held[k].at[mine[last_axis], pl.ds(0, n // 4), :]
            if k < 2:
                terms = [ta.at[k, quarter(0, n, (x, z)[k]), :]] + [ra.at[k, s] for s in range(3)]
            else:
                terms = [tb.at[k - 2, 0]] + [rb.at[k - 2, s] for s in range(3)]
            add(here, terms, n // 4)
            flight[k] = send_all(last_axis, lambda p, _: here, lambda s: here)
        yield
        for k in range(4):
            n = self.parts[k]
            if n == 0:
                continue
            wait(flight[k])
            piece = out.at[core, quarter(starts[k], n, (x, z)[k % 2]), :]
            add(piece, [held[k].at[j] for j in range(4)], n // 4)
            flight[k] = send_all("xz"[k % 2], lambda p, _: piece, lambda s: piece)
        yield
        for k in range(4):
            wait(flight[k])
        last = pltpu.make_async_remote_copy(
            src_ref=out.at[core],
            dst_ref=out.at[core],
            send_sem=g_send.at[14, 0],
            recv_sem=g_recv.at[14, 0],
            **pair,
        )
        last.start()
        if not self.shared:
            yield
            last.wait()
            return
        every = outs[1]
        start = self.used - self.shared
        every[y, core] = out[core, pl.ds(start, self.shared), :]
        spread = send_all("y", lambda p, _: every.at[y, core], lambda s: every.at[y, core])
        yield
        wait(spread)
        more = pltpu.make_async_remote_copy(
            src_ref=every.at[:, core],
            dst_ref=every.at[:, core],
            send_sem=g_send.at[15, 0],
            recv_sem=g_recv.at[15, 0],
            **pair,
        )
        more.start()
        yield
        last.wait()
        more.wait()

    def unpack(self, i, owned, dests):
        h, c = self.halves[i]
        at = self.offsets[i]
        tiles = c // 128
        if tiles == 4:
            for core in range(2):

                @pl.loop(0, h, step=16)
                def _(r):
                    to = pl.ds(pl.multiple_of(core * h + r, 16), 16)
                    row = pl.ds(pl.multiple_of(at + r, 16), 16)
                    dests[0][to, :] = owned[core, row, :].astype(F32)

            return
        q = h // 4
        each = tiles // len(dests)
        for core in range(2):
            for g in range(4):
                for t in range(tiles):
                    k = g * tiles + t
                    value = owned[core, pl.ds(at + k // 4 * q, q), pl.ds(k % 4 * 128, 128)]
                    to = pl.ds(core * h + g * q, q)
                    dests[t // each][to, pl.ds(t % each * 128, 128)] = value.astype(F32)


def write_gradients(late, owned, last, owned_last, mid, owned_mid, early, owned_early, every_early, channels):
    large = [(512, 512)] * 4 + [(512, channels)] * 2 + [(128, 512), (channels, 512), (1024, 512)]
    shapes = large + [(512, 128)] * 4 + [(31, 1024)] + [(1, 512)] * 10
    shapes += [(31, channels), (1, channels), (1, channels), (2, 64), (2, 64)]
    count = len(large)
    sources = (owned_early, every_early, owned_mid, owned, owned_last)

    def kernel(*refs):
        given, refs = refs[:5], refs[5:]
        outs, refs = refs[:count], refs[count:]
        wq, wk, wv, pos, taps = refs[:5]
        vectors, refs = refs[5:15], refs[15:]
        gate_taps, gain, shift, content, position, small, sem, load_sem = refs[:8]
        held, refs = refs[8 : 8 + count], refs[8 + count :]
        oe_ref, ee_ref, om_ref, o_ref, ol_ref = refs
        loads = [
            pltpu.make_async_copy(a, b, load_sem.at[k]) for k, (a, b) in enumerate(zip(given, refs))
        ]
        for c in loads:
            c.start()
        copies = []

        def send(k):
            c = pltpu.make_async_copy(held[k], outs[k], sem.at[k])
            c.start()
            copies.append(c)

        loads[0].wait()
        early.unpack(0, oe_ref, [held[2]])
        send(2)
        early.unpack(1, oe_ref, [held[3]])
        send(3)
        loads[1].wait()
        for y in range(4):
            for core in range(2):

                @pl.loop(0, 128, step=16)
                def _(r):
                    to = pl.ds(pl.multiple_of(y * 256 + core * 128 + r, 16), 16)
                    row = pl.ds(pl.multiple_of(r, 16), 16)
                    held[8][to, :] = ee_ref[y, core, row, :].astype(F32)

        send(8)
        loads[2].wait()
        for k, i in ((4, 0), (5, 1), (6, 2), (7, 3)):
            mid.unpack(i, om_ref, [held[k]])
            send(k)
        loads[3].wait()
        late.unpack(3, o_ref, [held[1]])
        send(1)
        loads[4].wait()
        last.unpack(0, ol_ref, [held[0]])
        send(0)
        late.unpack(0, o_ref, [wq, wk, wv])
        late.unpack(1, o_ref, [small])
        late.unpack(2, o_ref, [pos])
        at = last.offsets[1]
        rest = jnp.concatenate([ol_ref[core, pl.ds(at, 48), :].astype(F32) for core in range(2)])
        taps[:, pl.ds(0, 512)] = rest[0:31]
        taps[:, pl.ds(512, 512)] = rest[32:63]
        for k in range(10):
            vectors[k][...] = rest[64 + k : 65 + k]
        gate_taps[...] = small[pl.ds(0, 31), :]
        gain[...] = small[pl.ds(32, 1), :]
        shift[...] = small[pl.ds(33, 1), :]
        for k, ref in enumerate((content, position)):
            both = small[pl.ds(34 + k, 1), pl.ds(0, 128)]
            ref[pl.ds(0, 1), :] = both[:, :64]
            ref[pl.ds(1, 1), :] = both[:, 64:]
        for c in copies:
            c.wait()

    return pl.pallas_call(
        kernel,
        out_shape=[jax.ShapeDtypeStruct(s, F32) for s in shapes],
        in_specs=[ANY] * 5,
        out_specs=[ANY] * count + [VM] * (len(shapes) - count),
        scratch_shapes=[
            pltpu.VMEM((128, channels), F32),
            pltpu.SemaphoreType.DMA((count,)),
            pltpu.SemaphoreType.DMA((5,)),
        ]
        + [pltpu.VMEM(s, F32) for s in large]
        + [pltpu.VMEM(a.shape, a.dtype) for a in sources],
        compiler_params=pltpu.CompilerParams(vmem_limit_bytes=62 * 2**20),
        name="write_gradients",
    )(*sources)


def back(tensors, smalls, vectors, arrays, plans, cid):
    mid, late, last = plans
    n_tensors, n_small, n_vec = len(tensors), len(smalls), len(vectors)
    hidden = tensors[4].shape[1]

    def kernel(*refs):
        gqkv, wide_in, x_ref, middle, act_in, up_in, down_in, g_cg_in, g_merged, v_ref = refs[:10]
        refs = refs[n_tensors:]
        gate_taps, gain, shift, bias, pos, merge_taps = refs[:n_small]
        rows, refs = refs[n_small : n_small + n_vec], refs[n_small + n_vec :]
        ins, refs = refs[:4], refs[4:]
        g_features, o_late, o_last, o_mid = refs[:4]
        refs = refs[4:]
        small_f, shared_f, small, wide_pos, shared, g_wide, g_down, g_up, in1, g_mid, acc = refs[:11]
        wide, act, up1, down1, load_sem = refs[11:16]
        refs = refs[16:]
        sums_late, sums_last, sums_mid, refs = refs[:2], refs[2:4], refs[4:6], refs[6:]
        loads = [
            pltpu.make_async_copy(a, b, load_sem.at[k])
            for k, (a, b) in enumerate(
                ((wide_in, wide), (act_in, act), (down_in, down1), (up_in, up1))
            )
        ]
        for c in loads:
            c.start()

        def take(n):
            nonlocal refs
            got, refs = refs[:n], refs[n:]
            return got

        start1, l1 = late.first(
            [g_wide, small, wide_pos, g_down], sums_late, take(len(late.first_scratch))
        )
        start2, l2 = last.first([g_up, shared], sums_last, take(len(last.first_scratch)))
        s1 = late.second(sums_late, [o_late], take(len(late.scratch)))
        s2 = last.second(sums_last, [o_last], take(len(last.scratch)))
        start0, m1 = mid.first(ins, sums_mid, take(len(mid.first_scratch)))
        m2 = mid.second(sums_mid, [o_mid], take(len(mid.scratch)))
        vec = lambda k: v_ref[pl.ds(k, 1), :]
        slot = lambda k: pl.ds(k * D, D)
        total = lambda a: jnp.sum(a, 0, keepdims=True)

        greet(y=True, xz=True, pair=True)
        for k in range(4):
            start0(k)
        u2, inv2 = unit_norm(middle[...])
        attn_in = (u2 * vec(2) + vec(3)).astype(BF16)
        for k in range(3):
            g_wide[:, slot(k)] = contract_rows(attn_in, gqkv[:, slot(k)]).astype(BF16)
        start1(0)
        small_f[...] = jnp.zeros_like(small_f)
        small_f[pl.ds(0, 32), :] = gate_taps[...]
        small_f[pl.ds(32, 1), :] = gain[...]
        small_f[pl.ds(33, 1), :] = shift[...]
        small_f[pl.ds(34, 2), pl.ds(0, 128)] = bias[pl.ds(0, 2), :]
        small[...] = small_f[...].astype(BF16)
        start1(1)
        wide_pos[...] = jnp.zeros_like(wide_pos)
        wide_pos[:, pl.ds(0, 128)] = pos[...].astype(BF16)
        start1(2)
        shared_f[...] = jnp.zeros_like(shared_f)
        shared_f[pl.ds(0, 32), :] = merge_taps[:, pl.ds(0, D)]
        shared_f[pl.ds(32, 32), :] = merge_taps[:, pl.ds(D, D)]
        loads[0].wait()
        g_attn_in = times_transpose(gqkv[...], wide[...])
        g_gated = g_cg_in[...]
        shared_f[pl.ds(66, 1), :] = total(g_attn_in * u2)
        shared_f[pl.ds(67, 1), :] = total(g_attn_in)
        shared_f[pl.ds(68, 1), :] = total(g_gated * u2)
        shared_f[pl.ds(69, 1), :] = total(g_gated)
        for k, v in enumerate(rows):
            shared_f[pl.ds(70 + k, 1), :] = v[...]
        g_middle = g_merged[...] + norm_back(g_attn_in * vec(2) + g_gated * vec(4), u2, inv2)
        g_mid[...] = g_middle
        next(m1)
        gy1 = (0.5 * g_middle).astype(BF16)
        loads[1].wait()
        for k in range(hidden // D):
            a = act[:, slot(k)]
            hid = (a * jax.nn.sigmoid(a)).astype(BF16)
            g_down[slot(k), :] = contract_rows(hid, gy1).astype(BF16)
        start1(3)
        loads[2].wait()
        loads[3].wait()
        u1, inv1 = unit_norm(x_ref[...].astype(F32))
        in1[...] = (u1 * vec(0) + vec(1)).astype(BF16)
        acc[...] = jnp.zeros_like(acc)
        for k in range(hidden // D):
            a = act[:, slot(k)]
            sig = jax.nn.sigmoid(a)
            g_act = times_transpose(gy1, down1[slot(k), :]) * sig * (1.0 + a * (1.0 - sig))
            g_act = g_act.astype(BF16)
            g_up[:, slot(k)] = contract_rows(in1[...], g_act).astype(BF16)
            acc[...] += times_transpose(g_act, up1[k])
            if k == 2:
                next(l1)
        start2(0)
        u1, inv1 = unit_norm(x_ref[...].astype(F32))
        g_in1 = acc[...]
        shared_f[pl.ds(64, 1), :] = total(g_in1 * u1)
        shared_f[pl.ds(65, 1), :] = total(g_in1)
        shared[...] = shared_f[...].astype(BF16)
        start2(1)
        g_features[...] = g_mid[...] + norm_back(g_in1 * vec(0), u1, inv1)
        for _ in m1:
            pass
        next(m2)
        next(l2)
        for _ in l1:
            pass
        next(s1)
        next(m2)
        for _ in l2:
            pass
        next(s2)
        next(s1)
        next(m2)
        next(s2)
        next(s1)
        next(m2)
        next(s2)
        next(s1)
        next(s2)
        for g in (m2, s1, s2):
            for _ in g:
                pass

    bf = lambda *shape: pltpu.VMEM(shape, BF16)
    outs = [jax.ShapeDtypeStruct((ROWS, D), F32)] + late.outs + last.outs + mid.outs
    return pl.pallas_call(
        kernel,
        out_shape=outs,
        in_specs=[VM, ANY, VM, VM, ANY, ANY, ANY] + [VM] * (n_tensors - 7 + n_small + n_vec) + [ANY] * 4,
        out_specs=[VM] * len(outs),
        scratch_shapes=[
            pltpu.VMEM((128, GATE), F32),
            pltpu.VMEM((96, D), F32),
            bf(128, GATE),
            bf(D, D),
            bf(96, D),
            bf(D, 3 * D),
            bf(hidden, D),
            bf(D, hidden),
            bf(ROWS, D),
            pltpu.VMEM((ROWS, D), F32),
            pltpu.VMEM((ROWS, D), F32),
            bf(D, 3 * D),
            pltpu.VMEM((ROWS, hidden), F32),
            bf(GROUP, D, D),
            bf(hidden, D),
            pltpu.SemaphoreType.DMA((4,)),
        ]
        + [pltpu.VMEM(o.shape, BF16) for o in late.first_outs + last.first_outs + mid.first_outs]
        + late.first_scratch
        + last.first_scratch
        + late.scratch
        + last.scratch
        + mid.first_scratch
        + mid.scratch,
        compiler_params=params(cid, 60),
        name="back",
    )(*tensors, *smalls, *vectors, *arrays)


def local(
    features,
    lengths,
    first_gain,
    first_shift,
    first_up,
    first_down,
    attn_gain,
    attn_shift,
    w_query,
    w_key,
    w_value,
    w_pos,
    bias_content,
    bias_position,
    attn_out,
    cgmlp_gain,
    cgmlp_shift,
    cgmlp_up,
    gate_gain,
    gate_shift,
    gate_taps,
    cgmlp_down,
    merge_taps,
    merge_proj,
    second_gain,
    second_shift,
    second_up,
    second_down,
    final_gain,
    final_shift,
    cotangent,
):
    frames = ROWS * GROUP
    channels = gate_gain.shape[0]
    me = lax.axis_index("y")
    length = lengths[0]
    live = (jnp.arange(ROWS, dtype=jnp.int32) + me * ROWS < length).astype(F32)[:, None]
    mask = jnp.where(jnp.arange(frames, dtype=jnp.int32) < length, 0.0, -1e30)[None].astype(F32)
    rows_f, wide, small = prepare(
        (
            first_gain, first_shift, attn_gain, attn_shift, cgmlp_gain, cgmlp_shift, second_gain,
            second_shift, final_gain, final_shift,
        ),
        w_query, w_key, w_value, gate_taps, gate_gain, gate_shift,
    )
    (
        first_gain, first_shift, attn_gain, attn_shift, cgmlp_gain, cgmlp_shift, second_gain,
        second_shift, final_gain, final_shift,
    ) = (rows_f[k : k + 1] for k in range(10))
    sin, cos = position_factors(frames, D)
    biases = jnp.concatenate(
        [
            jnp.concatenate([bias_content, bias_position]).reshape(2, 128).astype(F32),
            jnp.zeros((6, 128), F32),
        ]
    )
    halves = cgmlp_up[:, 0], cgmlp_up[:, 1]
    middle, invg, gate_out, act1, c0, c1, ug, gate_conv, gate_pad, qkv, *gathered = front(
        features,
        live,
        rows_f,
        (
            first_up, first_down, wide, halves[0], halves[1], small, attn_out, cgmlp_down,
            second_up, second_down,
        ),
        0,
    )
    up1, down1, qkv_w, cg0, cg1, small_all, out_w, cg_down, up2, down2 = gathered
    flat = lambda w: w.reshape(-1, w.shape[-1])
    down1, out_w, cg_down, down2 = flat(down1), flat(out_w), flat(cg_down), flat(down2)
    gate_taps_f = small_all[:32].astype(F32)
    gate_gain_f = small_all[31:32].astype(F32)
    merge_taps_f = jnp.pad(merge_taps.astype(F32), ((0, 1), (0, 0)))
    attended, attended_rows, weights = attention_forward(
        qkv, w_pos, biases, mask, sin, cos, 2
    )
    joined = jnp.concatenate([product(attended_rows, out_w), product(gate_out, cg_down)], axis=1)
    joined_live = joined * live
    merge_conv, joined_pad = conv_forward(joined_live, merge_taps_f, 3)
    mixed = (joined + merge_conv).astype(BF16)
    merged = middle + product(mixed, merge_proj)
    u3, inv3 = unit_norm(merged)
    in2 = (u3 * second_gain + second_shift).astype(BF16)
    act2 = product(in2, up2)
    sig2 = jax.nn.sigmoid(act2)
    hid2 = (act2 * sig2).astype(BF16)
    last = merged + 0.5 * product(hid2, down2)
    u4, inv4 = unit_norm(last)
    encoded = u4 * final_gain + final_shift

    u2, _ = unit_norm(middle)
    cg_in = (u2 * cgmlp_gain + cgmlp_shift).astype(BF16)
    root = 1.0 / math.sqrt(2.0)
    phi0 = 0.5 * (1.0 + lax.erf(c0 * root))
    phi1 = 0.5 * (1.0 + lax.erf(c1 * root))
    half0 = c0 * phi0

    cot = cotangent.astype(F32)
    g_final_gain = jnp.sum(cot * u4, 0)
    g_final_shift = jnp.sum(cot, 0)
    g_last = norm_back(cot * final_gain, u4, inv4)
    gy2 = (0.5 * g_last).astype(BF16)
    g_down2 = contract_rows(hid2, gy2)
    g_act2 = (times_transpose(gy2, down2) * sig2 * (1.0 + act2 * (1.0 - sig2))).astype(BF16)
    g_up2 = contract_rows(in2, g_act2)
    g_in2 = times_transpose(g_act2, up2)
    g_second_gain = jnp.sum(g_in2 * u3, 0)
    g_second_shift = jnp.sum(g_in2, 0)
    g_merged = g_last + norm_back(g_in2 * second_gain, u3, inv3)
    gm = g_merged.astype(BF16)
    g_merge_proj = contract_rows(mixed, gm)
    gx = times_transpose(gm, merge_proj)
    merge_back, g_merge_taps = conv_backward(gx, joined_pad, merge_taps_f, 4)
    g_joined = (gx + live * merge_back).astype(BF16)
    ga, gb = g_joined[:, :D], g_joined[:, D:]
    g_attended_rows = times_transpose(ga, out_w).astype(BF16)
    gg = times_transpose(gb, cg_down)
    g_conv = gg * half0
    early = [a.astype(BF16) for a in (g_up2, g_down2, g_merge_proj)]
    plan_early = Reduction(
        [a.shape for a in early], ("cols", "rows", "whole"), (64, 64, 256, 256), 128
    )
    g_norm_raw, g_gate_taps, g_attended, *begun = conv_backward(
        g_conv, gate_pad, gate_taps_f, 5, g_attended_rows, early, plan_early
    )
    g_gate_norm = g_norm_raw * live
    g_gate_gain = jnp.sum(g_gate_norm * ug, 0)
    g_gate_shift = jnp.sum(g_gate_norm, 0)
    g_half1 = norm_back(g_gate_norm * gate_gain_f, ug, invg)
    density = 1.0 / math.sqrt(2.0 * math.pi)
    g_c0 = (gg * gate_conv * (phi0 + c0 * (density * jnp.exp(-0.5 * c0 * c0)))).astype(BF16)
    g_c1 = (g_half1 * (phi1 + c1 * (density * jnp.exp(-0.5 * c1 * c1)))).astype(BF16)
    g_cg_in = times_transpose(g_c0, cg0) + times_transpose(g_c1, cg1)
    plan_mid = Reduction(
        [(D, GATE), (D, GATE), (D, D), (GATE, D)],
        ("cols", "cols", "rows", "rows"),
        (64, 64, 256, 256),
    )
    g_qkv, g_w_pos, g_bias, owned_early, every_early, *mid = attention_backward(
        qkv, weights, attended, g_attended, w_pos, biases, sin, cos, plan_early, begun,
        (cg_in, g_c0, g_c1, attended_rows, gate_out, g_joined), 6,
    )
    plan_late = Reduction(
        [(D, 3 * D), (128, GATE), (D, D), (4 * D, D)],
        ("cols", "cols", "cols", "rows"),
        (64, 128, 192, 192),
    )
    plan_last = Reduction([(D, 4 * D), (96, D)], ("cols", "each"), (64, 0, 128, 128))
    g_features, owned, owned_last, owned_mid = back(
        (g_qkv, qkv_w, features, middle, act1, up1, down1, g_cg_in, g_merged, rows_f),
        (g_gate_taps, g_gate_gain[None], g_gate_shift[None], g_bias, g_w_pos, g_merge_taps),
        [v[None] for v in (g_second_gain, g_second_shift, g_final_gain, g_final_shift)],
        mid,
        (plan_mid, plan_late, plan_last),
        7,
    )
    (
        d_up1, d_down1, d_up2, d_down2, d_cg0, d_cg1, d_out, d_cg_down, d_proj, d_query, d_key,
        d_value, d_pos, d_taps, *vectors, d_gate_taps, d_gain, d_shift, d_content,
        d_position,
    ) = write_gradients(
        plan_late, owned, plan_last, owned_last, plan_mid, owned_mid, plan_early, owned_early,
        every_early, channels,
    )
    vectors = [v.reshape(D) for v in vectors]
    return (
        encoded,
        g_features,
        vectors[0],
        vectors[1],
        d_up1,
        d_down1,
        vectors[2],
        vectors[3],
        d_query,
        d_key,
        d_value,
        d_pos,
        d_content,
        d_position,
        d_out,
        vectors[4],
        vectors[5],
        jnp.stack([d_cg0, d_cg1], axis=1),
        d_gain.reshape(channels),
        d_shift.reshape(channels),
        d_gate_taps,
        d_cg_down,
        d_taps,
        d_proj,
        vectors[6],
        vectors[7],
        d_up2,
        d_down2,
        vectors[8],
        vectors[9],
    )


def solution(mesh):
    devices = mesh.devices.reshape(4, 4, 2, GROUP)
    fine = Mesh(devices, ("z", "x", "core", "y"))
    rows = P(("z", "x", "core", "y"), None)
    column, row = P(None, "y"), P("y", None)
    placed = (
        rows,
        P(("z", "x", "core")),
        P(),
        P(),
        column,
        row,
        P(),
        P(),
        column,
        column,
        column,
        column,
        row,
        row,
        row,
        P(),
        P(),
        P(None, None, "y"),
        P("y"),
        P("y"),
        column,
        row,
        P(),
        P(),
        P(),
        P(),
        column,
        row,
        P(),
        P(),
        rows,
    )
    return jax.shard_map(
        local,
        mesh=fine,
        in_specs=placed,
        out_specs=(rows,) + (rows,) + placed[2:30],
        check_vma=False,
    )
```

```python
import math

import jax
import jax.numpy as jnp
from jax import lax
from jax.experimental import pallas as pl
from jax.experimental.pallas import tpu as pltpu
from jax.sharding import Mesh, PartitionSpec as P

GATE = 1536
KERNEL = 31
D = 512
ROWS = 320
HALO = 16
GROUP = 4
EPS = 1e-05
F32 = jnp.float32
BF16 = jnp.bfloat16
MESH = pl.DeviceIdType.MESH
ANY = pl.BlockSpec(memory_space=pl.ANY)
VM = pl.BlockSpec(memory_space=pltpu.VMEM)


def product(a, b):
    return jnp.dot(a, b, preferred_element_type=F32)


def contract_rows(a, b):
    return lax.dot_general(a, b, (((0,), (0,)), ((), ())), preferred_element_type=F32)


def times_transpose(a, b):
    return lax.dot_general(a, b, (((1,), (1,)), ((), ())), preferred_element_type=F32)


def unit_norm(rows):
    center = rows - jnp.mean(rows, -1, keepdims=True)
    inverse = lax.rsqrt(jnp.mean(center * center, -1, keepdims=True) + EPS)
    return center * inverse, inverse


def norm_back(scaled, unit, inverse):
    inner = (
        scaled
        - jnp.mean(scaled, -1, keepdims=True)
        - unit * jnp.mean(scaled * unit, -1, keepdims=True)
    )
    return inner * inverse


def params(cid, vmem=48, **more):
    return pltpu.CompilerParams(
        collective_id=cid, has_side_effects=True, vmem_limit_bytes=vmem * 2**20, **more
    )


def ring():
    me = lax.axis_index("y")
    return me, lax.rem(me + 1, GROUP), lax.rem(me + GROUP - 1, GROUP), lax.rem(me + 2, GROUP)


def to_y(where):
    return dict(device_id={"y": where}, device_id_type=MESH)


def greet_ring(offsets):
    me = lax.axis_index("y")
    barrier = pltpu.get_barrier_semaphore()
    for off in offsets:
        pl.semaphore_signal(barrier, inc=1, **to_y(lax.rem(me + off, GROUP)))
    pl.semaphore_wait(barrier, len(offsets))


def greet(y=False, xz=False, pair=False):
    barrier = pltpu.get_barrier_semaphore()
    count = 0
    for axis in (("y",) if y else ()) + (("x", "z") if xz else ()):
        me = lax.axis_index(axis)
        for off in (1, 2, 3):
            where = {axis: lax.rem(me + off, 4)}
            pl.semaphore_signal(barrier, inc=1, device_id=where, device_id_type=MESH)
            count += 1
    if pair:
        where = {"core": 1 - lax.axis_index("core")}
        pl.semaphore_signal(barrier, inc=1, device_id=where, device_id_type=MESH)
        count += 1
    pl.semaphore_wait(barrier, count)


class Gather:
    def __init__(self, shards, kinds, entries):
        self.kinds = kinds
        self.entries = entries
        self.shapes = [s.shape for s in shards]
        count = len(entries)
        self.outs = []
        for s, kind in zip(shards, kinds):
            rows, cols = s.shape
            shape = (GROUP, rows, cols) if kind == "rows" else (rows, GROUP * cols)
            self.outs.append(jax.ShapeDtypeStruct(shape, s.dtype))
        self.scratch = [
            pltpu.SemaphoreType.DMA((count,)),
            pltpu.SemaphoreType.DMA((count, 10)),
            pltpu.SemaphoreType.DMA((count, 10)),
        ]

    def open(self, srcs, dsts, scratch):
        local_sem, send, recv = scratch
        core, x, y, z = (lax.axis_index(a) for a in ("core", "x", "y", "z"))
        mine = {"x": x, "y": y, "z": z}
        pair = dict(device_id={"core": 1 - core}, device_id_type=MESH)

        def spot(e, slot, slots, start, size, lane=None):
            i, first, width, _ = self.entries[e]
            cols = self.shapes[i][1]
            if self.kinds[i] == "rows":
                at = pl.ds(first, width) if lane is None else lane
                return dsts[i].at[pl.ds(slot, slots), pl.ds(start, size), at]
            return dsts[i].at[pl.ds(start, size), pl.ds(slot * cols, slots * cols)]

        def cut(e, level):
            i, first, width, route = self.entries[e]
            half = self.shapes[i][0] // 2
            if level == 2 or route == "A":
                return core * half, half, None
            if half % 256:
                lane = pl.ds(pl.multiple_of(z * (width // 4), 128), width // 4)
                row, size = core * half + x * (half // 4), half // 4
                if level == 0:
                    return row, size, lane
                return (row, size, None) if route == "B" else (core * half, half, lane)
            a, b = (x, z) if route == "B" else (z, x)
            if level == 0:
                return core * half + (a * 4 + b) * (half // 16), half // 16, None
            return core * half + a * (half // 4), half // 4, None

        def remote(src, dst, e, k, where):
            return pltpu.make_async_remote_copy(
                src_ref=src, dst_ref=dst, send_sem=send.at[e, k], recv_sem=recv.at[e, k], **where
            )

        def spread(e, axis, level, k):
            at = spot(e, 1, 3, *cut(e, level))
            copies = []
            for off in (2, 1, 3):
                where = dict(device_id={axis: lax.rem(mine[axis] + off, 4)}, device_id_type=MESH)
                copies.append(remote(at, at, e, k + off - 1, where))
                copies[-1].start()
            return copies

        def to_pair(e):
            at = spot(e, 1, 3, *cut(e, 2))
            c = remote(at, at, e, 9, pair)
            c.start()
            return c

        flight, level = {}, {}

        def start(e):
            i, first, width, _ = self.entries[e]
            row, size, lane = cut(e, 0)
            at = pl.ds(first, width) if lane is None else lane
            piece = srcs[i].at[pl.ds(row, size), at]
            copies = []
            for off in (2, 1, 3):
                there = spot(e, 4 - off, 1, row, size, lane)
                there = there.at[0] if self.kinds[i] == "rows" else there
                copies.append(remote(piece, there, e, off - 1, to_y(lax.rem(y + off, 4))))
                copies[-1].start()
            there = spot(e, 0, 1, 0, self.shapes[i][0])
            there = there.at[0] if self.kinds[i] == "rows" else there
            own = pltpu.make_async_copy(srcs[i].at[:, pl.ds(first, width)], there, local_sem.at[e])
            own.start()
            flight[e], level[e] = copies, 0
            return own

        def step(e):
            for c in flight[e]:
                c.wait()
            route, at = self.entries[e][3], level[e]
            if route == "A" and at == 0:
                at = 2
            if at == 0:
                flight[e] = spread(e, "z" if route == "B" else "x", 0, 3)
            elif at == 1:
                flight[e] = spread(e, "x" if route == "B" else "z", 1, 6)
            elif at == 2:
                flight[e] = [to_pair(e)]
            level[e] = at + 1

        return start, step


def split_copies(src, dst, send, recv, local_sem):
    me = lax.axis_index("y")
    width = src.shape[1] // GROUP
    there = dst.at[pl.ds(pl.multiple_of(me * ROWS, ROWS), ROWS), :]
    copies = []
    for off in (2, 1, 3):
        c = pltpu.make_async_remote_copy(
            src_ref=src.at[:, pl.ds(off * width, width)],
            dst_ref=there,
            send_sem=send.at[off],
            recv_sem=recv.at[off],
            **to_y(lax.rem(me + off, GROUP)),
        )
        c.start()
        copies.append(c)
    own = pltpu.make_async_copy(src.at[:, pl.ds(0, width)], there, local_sem)
    own.start()
    copies.append(own)
    return copies


def start_halo(edges, prev, nxt, send, recv, slots):
    _, up, down, _ = ring()
    cols = prev.shape[1]
    w = cols // GROUP
    turns = ((w, 0, 3 * w), (0, 3 * w, w)) if slots else ((0, 0, cols),)
    copies = []
    for t, (here, there, size) in enumerate(turns):
        for side, ref, where in ((1, prev, up), (0, nxt, down)):
            a, b = (here, there) if side else (there, here)
            c = pltpu.make_async_remote_copy(
                src_ref=edges.at[side, :, pl.ds(a, size)],
                dst_ref=ref.at[:, pl.ds(b, size)],
                send_sem=send.at[side, t],
                recv_sem=recv.at[side, t],
                **to_y(where),
            )
            c.start()
            copies.append(c)
    return copies


def lanes(b):
    return pl.ds(pl.multiple_of(b * 128, 128), 128)


CHUNK = 64


def conv_block(pad, taps, b, flip):
    weights = [taps[pl.ds(KERNEL - 1 - o if flip else o, 1), lanes(b)] for o in range(KERNEL)]
    for r in range(0, ROWS, CHUNK):
        total = None
        for o in range(KERNEL):
            term = weights[o] * pad[b, pl.ds(r + o + 1, CHUNK), :]
            total = term if total is None else total + term
        yield r, total


def taps_block(pad, g_pad, b, out):
    sums = [None] * KERNEL
    for r in range(0, ROWS, CHUNK):
        g = g_pad[b, pl.ds(HALO + r, CHUNK), :]
        for o in range(KERNEL):
            term = g * pad[b, pl.ds(r + o + 1, CHUNK), :]
            term = jnp.sum(term.reshape(CHUNK // 8, 8, 128), 0)
            sums[o] = term if sums[o] is None else sums[o] + term
    for o in range(KERNEL):
        out[pl.ds(o, 1), lanes(b)] = jnp.sum(sums[o], 0, keepdims=True)


def fill_middle(x_ref, pad, blocks):
    @pl.loop(0, blocks)
    def _(b):
        pad[b, pl.ds(HALO, ROWS), :] = x_ref[:, lanes(b)].astype(F32)


def fill_ends(prev, nxt, pad, blocks):
    me = lax.axis_index("y")
    has_prev = jnp.where(me > 0, 1.0, 0.0)
    has_next = jnp.where(me < GROUP - 1, 1.0, 0.0)

    @pl.loop(0, blocks)
    def _(b):
        pad[b, pl.ds(0, HALO), :] = prev[:, lanes(b)].astype(F32) * has_prev
        pad[b, pl.ds(HALO + ROWS, HALO), :] = nxt[:, lanes(b)].astype(F32) * has_next


def set_edges(x_ref, edges):
    edges[0] = x_ref[pl.ds(0, HALO), :].astype(BF16)
    edges[1] = x_ref[pl.ds(ROWS - HALO, HALO), :].astype(BF16)


def conv_forward(x, taps, cid):
    cols = x.shape[1]
    blocks = cols // 128

    def kernel(x_ref, t_ref, o_ref, pad, edges, prev, nxt, hs, hr):
        greet_ring((1, 3))
        set_edges(x_ref, edges)
        halos = start_halo(edges, prev, nxt, hs, hr, False)
        fill_middle(x_ref, pad, blocks)
        for c in halos:
            c.wait()
        fill_ends(prev, nxt, pad, blocks)

        @pl.loop(0, blocks)
        def _(blk):
            for r, value in conv_block(pad, t_ref, blk, False):
                o_ref[pl.ds(r, CHUNK), lanes(blk)] = value

    return pl.pallas_call(
        kernel,
        out_shape=[
            jax.ShapeDtypeStruct((ROWS, cols), F32),
            jax.ShapeDtypeStruct((blocks, ROWS + 2 * HALO, 128), F32),
        ],
        in_specs=[VM, VM],
        out_specs=[VM, VM],
        scratch_shapes=[
            pltpu.VMEM((2, HALO, cols), BF16),
            pltpu.VMEM((HALO, cols), BF16),
            pltpu.VMEM((HALO, cols), BF16),
            pltpu.SemaphoreType.DMA((2, 2)),
            pltpu.SemaphoreType.DMA((2, 2)),
        ],
        compiler_params=params(cid),
        name="conv_forward",
    )(x, taps)


def erf(v):
    v = jnp.clip(v, -3.832506856900711, 3.832506856900711)
    w = v * v
    top = jnp.full_like(w, -2.72614225801306e-10)
    for c in (
        2.77068142495902e-08, -2.10102402082508e-06, -5.69250639462346e-05, -7.34990630326855e-04,
        -2.95459980854025e-03, -1.60960333262415e-02,
    ):
        top = top * w + c
    low = jnp.full_like(w, -1.45660718464996e-05)
    for c in (-2.13374055278905e-04, -1.68282697438203e-03, -7.37332916720468e-03, -1.42647390514189e-02):
        low = low * w + c
    return v * top / low


def prepare(vectors, w_query, w_key, w_value, gate_taps, gate_gain, gate_shift, gated):
    count = len(vectors)
    cols = gate_taps.shape[1]

    def kernel(*refs):
        wq, wk, wv, taps, gain, shift, both = refs[count : count + 7]
        rows, wide, small, first, second, small_f = refs[count + 7 :]
        first[...] = both[:, 0, :]
        second[...] = both[:, 1, :]
        rows[...] = jnp.zeros_like(rows)
        for k in range(count):
            rows[pl.ds(k, 1), :] = refs[k][...].astype(F32).reshape(1, D)
        for k, w in enumerate((wq, wk, wv)):
            wide[:, pl.ds(k * 128, 128)] = w[...]
        small_f[...] = jnp.zeros_like(small_f)
        small_f[pl.ds(0, KERNEL), :] = taps[...].astype(F32)
        small_f[pl.ds(31, 1), :] = gain[...].astype(F32).reshape(1, cols)
        small_f[pl.ds(32, 1), :] = shift[...].astype(F32).reshape(1, cols)
        small[...] = small_f[...].astype(BF16)

    return pl.pallas_call(
        kernel,
        out_shape=[
            jax.ShapeDtypeStruct((16, D), F32),
            jax.ShapeDtypeStruct((D, 384), BF16),
            jax.ShapeDtypeStruct((64, cols), BF16),
            jax.ShapeDtypeStruct((D, cols), BF16),
            jax.ShapeDtypeStruct((D, cols), BF16),
        ],
        in_specs=[VM] * (count + 7),
        out_specs=[VM] * 5,
        scratch_shapes=[pltpu.VMEM((64, cols), F32)],
        name="prepare",
    )(*vectors, w_query, w_key, w_value, gate_taps, gate_gain, gate_shift, gated)


def front(features, live, vectors, shards, cid):
    kinds = ("rows", "rows", "cols", "cols", "cols", "cols", "rows", "rows", "cols", "rows")
    up1, down1, wide, cg0, cg1, small, out, cgd, up2, down2 = range(10)
    half = D // 2
    entries = (
        (up1, 0, half, "A"),
        (down1, 0, half, "A"),
        (up1, half, half, "B"),
        (down1, half, half, "C"),
        (wide, 0, 384, "B"),
        (cg0, 0, 384, "C"),
        (cg1, 0, 384, "A"),
        (small, 0, 384, "A"),
        (out, 0, D, "B"),
        (cgd, 0, D, "C"),
        (up2, 0, D, "B"),
        (down2, 0, D, "C"),
    )
    plan = Gather(shards, kinds, entries)
    blocks = GATE // 128
    hidden = GROUP * D

    def kernel(*refs):
        x_ref, live_ref, v_ref = refs[:3]
        srcs, refs = refs[3:13], refs[13:]
        middle, inv, gate_out = refs[:3]
        act_out, c0_out, c1_out, ug_out, conv_out, pad_out, qkv_out = refs[3:10]
        w_out, refs = refs[10:20], refs[20:]
        w_in, refs = refs[:6], refs[6:]
        act, c0, c1, ug, conv, pad, qkv, acc, cg_in, half, taps, edges, prev, nxt = refs[:14]
        hs, hr, ss, sr, sl, out_sem = refs[14:20]
        dsts = [*w_in, *w_out[6:]]
        start, step = plan.open(srcs, dsts, refs[20:])
        greet(y=True, xz=True, pair=True)
        own = {}
        for e in (2, 3, 4, 5, 0, 1, 10, 11, 8, 9, 6, 7):
            own[e] = start(e)
        saves = []

        def save(src, dst):
            c = pltpu.make_async_copy(src, dst, out_sem.at[len(saves)])
            c.start()
            saves.append(c)

        rows = x_ref[...].astype(F32)
        unit, _ = unit_norm(rows)
        in1 = (unit * v_ref[pl.ds(0, 1), :] + v_ref[pl.ds(1, 1), :]).astype(BF16)

        def hidden_slot(k):
            at = pl.ds(k * D, D)
            a = product(in1, w_in[up1][k])
            act[:, at] = a
            return product((a * jax.nn.sigmoid(a)).astype(BF16), w_in[down1][k])

        for e in range(4):
            own[e].wait()
        acc[...] = hidden_slot(0)
        for e in (2, 3, 4, 5, 2, 3, 4, 5):
            step(e)
        for e in (0, 1, 2, 3, 10, 11, 8, 9, 0, 1, 2, 3):
            step(e)
        total = acc[...]
        for k in range(1, 4):
            total = total + hidden_slot(k)
        save(act, act_out)
        save(w_in[up1], w_out[up1])
        save(w_in[down1], w_out[down1])
        rows = rows + 0.5 * total
        middle[...] = rows
        unit, _ = unit_norm(rows)
        attn_in = (unit * v_ref[pl.ds(2, 1), :] + v_ref[pl.ds(3, 1), :]).astype(BF16)
        cg_in[...] = (unit * v_ref[pl.ds(4, 1), :] + v_ref[pl.ds(5, 1), :]).astype(BF16)
        for e in (4, 5, 10, 11, 8, 9, 6, 7):
            step(e)
        step(4)
        own[4].wait()
        for k in range(4):
            at = pl.ds(k * 384, 384)
            qkv[:, at] = product(attn_in, w_in[wide][:, at]).astype(BF16)
        waits = split_copies(qkv, qkv_out, ss, sr, sl)
        save(w_in[wide], w_out[wide])
        for e in (6, 7, 5):
            step(e)
            own[e].wait()
        for k in range(3):
            at = pl.ds(k * D, D)
            c1[:, at] = product(cg_in[...], w_in[cg1][:, at])
        save(c1, c1_out)
        save(w_in[cg1], w_out[cg1])
        gain = w_in[small][pl.ds(16, 16), :][15:16].astype(F32)
        shift = w_in[small][pl.ds(32, 16), :][0:1].astype(F32)
        root = 1.0 / math.sqrt(2.0)

        @pl.loop(0, ROWS, step=16)
        def _(r):
            at = pl.ds(pl.multiple_of(r, 16), 16)
            c = c1[at, :]
            unit, inverse = unit_norm(c * (0.5 * (1.0 + erf(c * root))))
            ug[at, :] = unit
            inv[at, :] = inverse
            norm = (unit * gain + shift) * live_ref[at, :]
            for b in range(blocks):
                pad[b, pl.ds(pl.multiple_of(HALO + r, 16), 16), :] = norm[:, b * 128 : b * 128 + 128]

        save(ug, ug_out)
        for side, r in ((0, HALO), (1, ROWS)):
            for b in range(blocks):
                edges[side, :, pl.ds(b * 128, 128)] = pad[b, pl.ds(r, HALO), :].astype(BF16)
        halos = start_halo(edges, prev, nxt, hs, hr, True)
        for k in range(3):
            at = pl.ds(k * D, D)
            c0[:, at] = product(cg_in[...], w_in[cg0][:, at])
        save(c0, c0_out)
        save(w_in[cg0], w_out[cg0])
        save(w_in[small], w_out[small])

        @pl.loop(0, ROWS, step=16)
        def _(r):
            at = pl.ds(pl.multiple_of(r, 16), 16)
            c = c0[at, :]
            half[at, :] = c * (0.5 * (1.0 + erf(c * root)))

        for c in halos:
            c.wait()
        fill_ends(prev, nxt, pad, blocks)
        save(pad, pad_out)
        for e in (10, 11, 8, 9):
            step(e)
        taps[...] = w_in[small][pl.ds(0, 32), :].astype(F32)

        @pl.loop(0, blocks)
        def _(blk):
            for r, value in conv_block(pad, taps, blk, False):
                at = pl.ds(r, CHUNK)
                conv[at, lanes(blk)] = value
                gate_out[at, lanes(blk)] = (value * half[at, lanes(blk)]).astype(BF16)

        save(conv, conv_out)
        for e in (10, 11, 8, 9):
            step(e)
            own[e].wait()
        for c in waits + saves:
            c.wait()

    f32 = lambda *shape: jax.ShapeDtypeStruct(shape, F32)
    pad_shape = (blocks, ROWS + 2 * HALO, 128)
    outs = [f32(ROWS, D), f32(ROWS, 1), jax.ShapeDtypeStruct((ROWS, GATE), BF16)]
    outs += [f32(ROWS, hidden)] + [f32(ROWS, GATE)] * 4 + [f32(*pad_shape)]
    outs += [jax.ShapeDtypeStruct((ROWS * GROUP, 3 * 128), BF16)]
    return pl.pallas_call(
        kernel,
        out_shape=outs + plan.outs,
        in_specs=[VM] * 3 + [ANY] * 10,
        out_specs=[VM] * 3 + [ANY] * 17,
        scratch_shapes=[pltpu.VMEM(o.shape, o.dtype) for o in plan.outs[:6]]
        + [
            pltpu.VMEM((ROWS, hidden), F32),
            pltpu.VMEM((ROWS, GATE), F32),
            pltpu.VMEM((ROWS, GATE), F32),
            pltpu.VMEM((ROWS, GATE), F32),
            pltpu.VMEM((ROWS, GATE), F32),
            pltpu.VMEM(pad_shape, F32),
            pltpu.VMEM((ROWS, 3 * D), BF16),
            pltpu.VMEM((ROWS, D), F32),
            pltpu.VMEM((ROWS, D), BF16),
            pltpu.VMEM((ROWS, GATE), F32),
            pltpu.VMEM((32, GATE), F32),
            pltpu.VMEM((2, HALO, GATE), BF16),
            pltpu.VMEM((HALO, GATE), BF16),
            pltpu.VMEM((HALO, GATE), BF16),
            pltpu.SemaphoreType.DMA((2, 2)),
            pltpu.SemaphoreType.DMA((2, 2)),
            pltpu.SemaphoreType.DMA((GROUP,)),
            pltpu.SemaphoreType.DMA((GROUP,)),
            pltpu.SemaphoreType.DMA,
            pltpu.SemaphoreType.DMA((12,)),
        ]
        + plan.scratch,
        compiler_params=params(cid, 60),
        name="front",
    )(features, live, vectors, *shards)


def conv_backward(g, pad, taps, cid, heads_in=None, arrays=(), plan=None, factors=()):
    cols = g.shape[1]
    blocks = cols // 128
    extra = heads_in is not None
    count = len(arrays)
    firsts = len(plan.first_outs) if extra else 0
    pairs = len(factors) // 2
    shapes = [(factors[2 * k].shape[1], factors[2 * k + 1].shape[1]) for k in range(pairs)]

    def kernel(*refs):
        g_ref, pad_in, t_ref = refs[:3]
        if extra:
            h_ref, refs = refs[3], refs[4:]
            ins, refs = refs[:count], refs[count:]
            o_ref, tg_ref, ho_ref = refs[:3]
            sums, refs = refs[3 : 3 + firsts], refs[3 + firsts :]
            g_pad, pad, load_sem, edges, prev, nxt, hs, hr, ss, sr, sl = refs[:11]
            start, riding = plan.first(ins, sums, refs[11:])
        else:
            given, refs = refs[3 : 3 + 2 * pairs], refs[3 + 2 * pairs :]
            o_ref, tg_ref = refs[:2]
            made, refs = refs[2 : 2 + pairs], refs[2 + pairs :]
            g_pad, pad, load_sem, edges, prev, nxt, hs, hr = refs[:8]
            held, results = refs[8 : 8 + 2 * pairs], refs[8 + 2 * pairs : 8 + 3 * pairs]
            in_sem, out_sem = refs[8 + 3 * pairs :]
            needed = [
                pltpu.make_async_copy(a, b, in_sem.at[k])
                for k, (a, b) in enumerate(zip(given, held))
            ]
            for c in needed:
                c.start()
        load = pltpu.make_async_copy(pad_in, pad, load_sem)
        load.start()
        if extra:
            greet(y=True, xz=True, pair=True)
        else:
            greet_ring((1, 3))
        set_edges(g_ref, edges)
        halos = start_halo(edges, prev, nxt, hs, hr, extra)
        waits = split_copies(h_ref, ho_ref, ss, sr, sl) if extra else []
        for i in range(count):
            start(i)
        fill_middle(g_ref, g_pad, blocks)
        tg_ref[pl.ds(24, 8), :] = jnp.zeros((8, cols), F32)
        load.wait()
        parts = ((0, 7), (7, blocks)) if extra else ((0, blocks),)
        for low, high in parts:

            @pl.loop(low, high)
            def _(blk):
                taps_block(pad, g_pad, blk, tg_ref)

            if extra and low == 0:
                next(riding)

        saves = []
        if not extra:
            for c in needed:
                c.wait()
            for k in range(pairs):
                left, right, result = held[2 * k], held[2 * k + 1], results[k]
                for at in range(0, max(result.shape), D):
                    part = pl.ds(at, D)
                    if result.shape[0] > result.shape[1]:
                        result[part, :] = contract_rows(left[:, part], right[...]).astype(BF16)
                    else:
                        result[:, part] = contract_rows(left[...], right[:, part]).astype(BF16)
                saves.append(pltpu.make_async_copy(result, made[k], out_sem.at[k]))
                saves[-1].start()
        for c in halos:
            c.wait()
        fill_ends(prev, nxt, g_pad, blocks)

        @pl.loop(0, blocks)
        def _(blk):
            for r, value in conv_block(g_pad, t_ref, blk, True):
                o_ref[pl.ds(r, CHUNK), lanes(blk)] = value

        for c in waits + saves:
            c.wait()
        if extra:
            for _ in riding:
                pass

    outs = [jax.ShapeDtypeStruct((ROWS, cols), F32), jax.ShapeDtypeStruct((32, cols), F32)]
    ins = [g, pad, taps]
    scratch = [
        pltpu.VMEM((blocks, ROWS + 2 * HALO, 128), F32),
        pltpu.VMEM((blocks, ROWS + 2 * HALO, 128), F32),
        pltpu.SemaphoreType.DMA,
        pltpu.VMEM((2, HALO, cols), BF16),
        pltpu.VMEM((HALO, cols), BF16),
        pltpu.VMEM((HALO, cols), BF16),
        pltpu.SemaphoreType.DMA((2, 2)),
        pltpu.SemaphoreType.DMA((2, 2)),
    ]
    in_specs, out_specs = [VM, ANY, VM], [VM, VM]
    if extra:
        ins += [heads_in, *arrays]
        in_specs += [ANY] * (1 + count)
        outs.append(
            jax.ShapeDtypeStruct((ROWS * GROUP, heads_in.shape[1] // GROUP), heads_in.dtype)
        )
        outs += plan.first_outs
        out_specs += [ANY] + [VM] * firsts
        scratch += [
            pltpu.SemaphoreType.DMA((GROUP,)),
            pltpu.SemaphoreType.DMA((GROUP,)),
            pltpu.SemaphoreType.DMA,
        ] + plan.first_scratch
    else:
        ins += factors
        in_specs += [ANY] * (2 * pairs)
        outs += [jax.ShapeDtypeStruct(s, BF16) for s in shapes]
        out_specs += [ANY] * pairs
        scratch += [pltpu.VMEM(a.shape, BF16) for a in factors]
        scratch += [pltpu.VMEM(s, BF16) for s in shapes]
        scratch += [pltpu.SemaphoreType.DMA((2 * pairs,)), pltpu.SemaphoreType.DMA((pairs,))]
    return pl.pallas_call(
        kernel,
        out_shape=outs,
        in_specs=in_specs,
        out_specs=out_specs,
        scratch_shapes=scratch,
        compiler_params=params(cid),
        name="conv_backward",
    )(*ins)


def position_factors(frames, width):
    frequency = jnp.exp(
        jnp.arange(width // 2, dtype=jnp.int32).astype(F32) * (-2.0 * math.log(10000.0) / width)
    )
    steps = jnp.concatenate(
        [32 * jnp.arange(frames // 32, dtype=jnp.int32), jnp.arange(32, dtype=jnp.int32)]
    )
    angles = steps.astype(F32)[:, None] * frequency[None]
    return jnp.sin(angles), jnp.cos(angles)


def fill_table(sin_parts, cos_parts, sin, cos, table):
    frames, half = sin.shape
    sb, cb = sin_parts[pl.ds(frames // 32, 32), :], cos_parts[pl.ds(frames // 32, 32), :]

    @pl.loop(0, frames // 32)
    def _(a):
        at = pl.ds(pl.multiple_of(a * 32, 32), 32)
        sa, ca = sin_parts[pl.ds(a, 1), :], cos_parts[pl.ds(a, 1), :]
        s, c = sa * cb + ca * sb, ca * cb - sa * sb
        sin[at, :] = s
        cos[at, :] = c
        table[at, pl.ds(0, half)] = s.astype(BF16)
        table[at, pl.ds(half, half)] = c.astype(BF16)


def head_mask(h):
    column = lax.broadcasted_iota(jnp.int32, (1, 128), 1)
    return jnp.where((column >= 64 * h) & (column < 64 * h + 64), 1.0, 0.0)


def rotated(query, sin, cos, w_pos):
    z = times_transpose(query, w_pos)
    zs, zc = z[:, : D // 2], z[:, D // 2 :]
    return jnp.concatenate([zc * sin - zs * cos, zs * sin + zc * cos], axis=1).astype(BF16)


def attention_forward(qkv, w_pos, biases, mask, sin, cos, cid):
    frames = qkv.shape[0]

    def kernel(
        x_ref, wp_ref, b_ref, m_ref, sp_ref, cp_ref, o_ref, rows_ref, p_ref,
        p_buf, t_ref, s_ref, c_ref, p_sem, ss, sr, sl,
    ):
        me = lax.axis_index("y")
        greet_ring((1, 2, 3))
        fill_table(sp_ref, cp_ref, s_ref, c_ref, t_ref)
        saves, sends = [], []
        for k in range(GROUP):
            peer = lax.rem(me + 1 + k, GROUP)
            at = pl.ds(pl.multiple_of(peer * ROWS, ROWS), ROWS)
            query = x_ref[at, pl.ds(0, 128)].astype(F32)
            if k >= 2:
                saves[k - 2].wait()
            total = jnp.zeros((ROWS, 128), F32)
            for h in range(2):
                keep = head_mask(h)
                content = ((query + b_ref[pl.ds(0, 1), :]) * (0.125 * keep)).astype(BF16)
                position = ((query + b_ref[pl.ds(1, 1), :]) * (0.125 * keep)).astype(BF16)
                turned = rotated(position, s_ref[at, :], c_ref[at, :], wp_ref[...])
                scores = times_transpose(turned, t_ref[...])
                scores = scores + times_transpose(content, x_ref[:, pl.ds(128, 128)])
                scores = scores + m_ref[...]
                top = jnp.max(scores, -1, keepdims=True)
                weights = jnp.exp(scores - top)
                weights = (weights * (1.0 / jnp.sum(weights, -1, keepdims=True))).astype(BF16)
                p_buf[k % 2, h] = weights
                total = total + product(weights, x_ref[:, pl.ds(256, 128)]) * keep
            o_ref[at, :] = total.astype(BF16)
            save = pltpu.make_async_copy(p_buf.at[k % 2], p_ref.at[:, at, :], p_sem.at[k % 2])
            save.start()
            saves.append(save)
            into = rows_ref.at[:, pl.ds((3 - k) * 128, 128)]
            if k < GROUP - 1:
                c = pltpu.make_async_remote_copy(
                    src_ref=o_ref.at[at, :],
                    dst_ref=into,
                    send_sem=ss.at[k],
                    recv_sem=sr.at[k],
                    **to_y(peer),
                )
            else:
                c = pltpu.make_async_copy(o_ref.at[at, :], into, sl)
            c.start()
            sends.append(c)
        saves[2].wait()
        saves[3].wait()
        for c in sends:
            c.wait()

    return pl.pallas_call(
        kernel,
        in_specs=[VM] * 6,
        out_specs=[VM, ANY, ANY],
        out_shape=[
            jax.ShapeDtypeStruct((frames, 128), BF16),
            jax.ShapeDtypeStruct((ROWS, D), BF16),
            jax.ShapeDtypeStruct((2, frames, frames), BF16),
        ],
        scratch_shapes=[
            pltpu.VMEM((2, 2, ROWS, frames), BF16),
            pltpu.VMEM((frames, D), BF16),
            pltpu.VMEM((frames, D // 2), F32),
            pltpu.VMEM((frames, D // 2), F32),
            pltpu.SemaphoreType.DMA((2,)),
            pltpu.SemaphoreType.DMA((3,)),
            pltpu.SemaphoreType.DMA((3,)),
            pltpu.SemaphoreType.DMA,
        ],
        compiler_params=params(cid),
        name="attention_forward",
    )(qkv, w_pos, biases, mask, sin, cos)


def attention_backward(
    qkv, weights, attended, g_attended, w_pos, biases, sin, cos, plan, begun, factors,
    cid,
):
    frames = qkv.shape[0]

    def kernel(*refs):
        x_ref, p_ref, a_ref, ga_ref, wp_ref, b_ref, sp_ref, cp_ref = refs[:8]
        begun_refs, given, refs = refs[8:10], refs[10:16], refs[16:]
        rows_ref, gw_ref, gb_ref = refs[:3]
        finished, made, refs = refs[3:5], refs[5:9], refs[9:]
        p_buf, gq_buf, kv_buf, gk_acc, gv_acc, p_sem, qs, qr, ql, ks, kr, kl = refs[:12]
        t_ref, s_ref, c_ref = refs[12:15]
        cg_in, g_c0, g_c1, rows_in, gate_in, g_joined = held = refs[15:21]
        results, load_sem, save_sem = refs[21:25], refs[25], refs[26]
        riding = plan.second(begun_refs, finished, refs[27:])
        needed = [
            pltpu.make_async_copy(a, b, load_sem.at[k]) for k, (a, b) in enumerate(zip(given, held))
        ]
        me = lax.axis_index("y")

        def block(k):
            peer = lax.rem(me + 1 + k, GROUP)
            return peer, pl.ds(pl.multiple_of(peer * ROWS, ROWS), ROWS)

        def load(k):
            c = pltpu.make_async_copy(p_ref.at[:, block(k)[1], :], p_buf.at[k % 2], p_sem.at[k % 2])
            c.start()
            return c

        loads = [load(0), load(1)]
        greet(y=True, xz=True, pair=True)
        next(riding)
        fill_table(sp_ref, cp_ref, s_ref, c_ref, t_ref)
        gk_acc[...] = jnp.zeros_like(gk_acc)
        gv_acc[...] = jnp.zeros_like(gv_acc)
        gw_ref[...] = jnp.zeros_like(gw_ref)
        gb_ref[...] = jnp.zeros_like(gb_ref)
        sends = []
        for k in range(GROUP):
            peer, at = block(k)
            query = x_ref[at, pl.ds(0, 128)].astype(F32)
            g_out = ga_ref[at, :]
            dots = g_out.astype(F32) * a_ref[at, :].astype(F32)
            sin_, cos_ = s_ref[at, :], c_ref[at, :]
            g_content = jnp.zeros((ROWS, 128), F32)
            g_position = jnp.zeros((ROWS, 128), F32)
            loads[k].wait()
            for h in range(2):
                keep = head_mask(h)
                content = ((query + b_ref[pl.ds(0, 1), :]) * (0.125 * keep)).astype(BF16)
                position = ((query + b_ref[pl.ds(1, 1), :]) * (0.125 * keep)).astype(BF16)
                g_head = (g_out.astype(F32) * keep).astype(BF16)
                p = p_buf[k % 2, h]
                g_weights = times_transpose(g_head, x_ref[:, pl.ds(256, 128)])
                inner = jnp.sum(dots * keep, -1, keepdims=True)
                g_scores = (p.astype(F32) * (g_weights - inner)).astype(BF16)
                gv_acc[...] += contract_rows(g_head, p)
                gk_acc[...] += contract_rows(content, g_scores)
                g_content = g_content + product(g_scores, x_ref[:, pl.ds(128, 128)]) * keep
                turned = product(g_scores, t_ref[...])
                ts, tc = turned[:, : D // 2], turned[:, D // 2 :]
                g_z = jnp.concatenate([tc * sin_ - ts * cos_, ts * sin_ + tc * cos_], axis=1)
                g_z = g_z.astype(BF16)
                g_position = g_position + product(g_z, wp_ref[...]) * keep
                gw_ref[...] += contract_rows(g_z, position)
                if (k, h) in ((1, 0), (2, 0), (3, 0)):
                    next(riding)
            g_content = g_content * 0.125
            g_position = g_position * 0.125
            gq_buf[at, :] = (g_content + g_position).astype(BF16)
            gb_ref[pl.ds(0, 1), :] += jnp.sum(g_content, 0, keepdims=True)
            gb_ref[pl.ds(1, 1), :] += jnp.sum(g_position, 0, keepdims=True)
            if k < 2:
                loads.append(load(k + 2))
            into = rows_ref.at[:, pl.ds((3 - k) * 384, 128)]
            if k < GROUP - 1:
                c = pltpu.make_async_remote_copy(
                    src_ref=gq_buf.at[at, :],
                    dst_ref=into,
                    send_sem=qs.at[k],
                    recv_sem=qr.at[k],
                    **to_y(peer),
                )
            else:
                c = pltpu.make_async_copy(gq_buf.at[at, :], into, ql)
            c.start()
            sends.append(c)
            if k == 0:
                for c in needed:
                    c.start()
        kv_buf[:, pl.ds(0, 128)] = gk_acc[...].T.astype(BF16)
        kv_buf[:, pl.ds(128, 128)] = gv_acc[...].T.astype(BF16)
        for k in range(GROUP):
            into = rows_ref.at[:, pl.ds((3 - k) * 384 + 128, 256)]
            peer, at = block(k)
            if k < GROUP - 1:
                c = pltpu.make_async_remote_copy(
                    src_ref=kv_buf.at[at, :],
                    dst_ref=into,
                    send_sem=ks.at[k],
                    recv_sem=kr.at[k],
                    **to_y(peer),
                )
            else:
                c = pltpu.make_async_copy(kv_buf.at[at, :], into, kl)
            c.start()
            sends.append(c)
        for c in needed:
            c.wait()
        for k in range(3):
            at = pl.ds(k * D, D)
            results[0][:, at] = contract_rows(cg_in[...], g_c0[:, at]).astype(BF16)
            results[1][:, at] = contract_rows(cg_in[...], g_c1[:, at]).astype(BF16)
            results[3][at, :] = contract_rows(gate_in[:, at], g_joined[:, pl.ds(D, D)]).astype(BF16)
        results[2][...] = contract_rows(rows_in[...], g_joined[:, pl.ds(0, D)]).astype(BF16)
        for k in range(4):
            c = pltpu.make_async_copy(results[k], made[k], save_sem.at[k])
            c.start()
            sends.append(c)
        for _ in riding:
            pass
        for c in sends:
            c.wait()

    shapes = [(D, GATE), (D, GATE), (D, D), (GATE, D)]

    return pl.pallas_call(
        kernel,
        in_specs=[VM, ANY] + [VM] * 8 + [ANY] * 6,
        out_specs=[ANY, VM, VM] + [VM] * 2 + [ANY] * 4,
        out_shape=[
            jax.ShapeDtypeStruct((ROWS, 3 * D), BF16),
            jax.ShapeDtypeStruct((D, 128), F32),
            jax.ShapeDtypeStruct((8, 128), F32),
        ]
        + plan.outs
        + [jax.ShapeDtypeStruct(s, BF16) for s in shapes],
        scratch_shapes=[
            pltpu.VMEM((2, 2, ROWS, frames), BF16),
            pltpu.VMEM((frames, 128), BF16),
            pltpu.VMEM((frames, 256), BF16),
            pltpu.VMEM((128, frames), F32),
            pltpu.VMEM((128, frames), F32),
            pltpu.SemaphoreType.DMA((2,)),
            pltpu.SemaphoreType.DMA((3,)),
            pltpu.SemaphoreType.DMA((3,)),
            pltpu.SemaphoreType.DMA,
            pltpu.SemaphoreType.DMA((3,)),
            pltpu.SemaphoreType.DMA((3,)),
            pltpu.SemaphoreType.DMA,
            pltpu.VMEM((frames, D), BF16),
            pltpu.VMEM((frames, D // 2), F32),
            pltpu.VMEM((frames, D // 2), F32),
        ]
        + [pltpu.VMEM(a.shape, BF16) for a in factors]
        + [pltpu.VMEM(s, BF16) for s in shapes]
        + [pltpu.SemaphoreType.DMA((6,)), pltpu.SemaphoreType.DMA((4,))]
        + plan.scratch,
        compiler_params=params(cid, 58),
        name="attention_backward",
    )(qkv, weights, attended, g_attended, w_pos, biases, sin, cos, *begun, *factors)


class Reduction:
    def __init__(self, shapes, kinds, parts, shared_rows=0):
        self.kinds = kinds
        self.halves = []
        self.offsets = []
        at = 0
        for (rows, cols), kind in zip(shapes, kinds):
            h, c = (rows // 2, cols // 4) if kind == "cols" else (rows // 8, cols)
            if kind == "each":
                h = rows // 2
            self.halves.append((h, c))
            self.offsets.append(at)
            at += h * c // D
        self.used = at
        self.parts = parts
        self.rows = sum(parts)
        self.shared = shared_rows
        count = len(shapes)
        n_a, n_b = max(parts[:2]), max(parts[2:])
        self.first_scratch = []
        for (h, c), kind in zip(self.halves, kinds):
            shape = (h, 4 * c) if kind == "cols" else (4, h, c)
            if kind == "each":
                shape = (4, 2 * h, c)
            self.first_scratch += [pltpu.VMEM(shape, BF16)] * 2
        self.first_scratch += [
            pltpu.VMEM((4, self.rows, D), BF16),
            pltpu.VMEM((2, 3, n_a, D), BF16),
            pltpu.VMEM((2, 3, 4, n_b // 4, D), BF16),
            pltpu.SemaphoreType.DMA((count, 4)),
            pltpu.SemaphoreType.DMA((count, 4)),
            pltpu.SemaphoreType.DMA((count, 4)),
            pltpu.SemaphoreType.DMA((5, 3)),
            pltpu.SemaphoreType.DMA((5, 3)),
        ]
        self.first_outs = [
            jax.ShapeDtypeStruct((2, n_a, D), BF16),
            jax.ShapeDtypeStruct((2, 4, n_b // 4, D), BF16),
        ]
        self.scratch = [
            pltpu.VMEM((2, 3, n_a // 4, D), BF16),
            pltpu.VMEM((2, 3, n_b // 4, D), BF16),
            pltpu.VMEM((2, 4, n_a // 4, D), BF16),
            pltpu.VMEM((2, 4, n_b // 4, D), BF16),
            pltpu.SemaphoreType.DMA((16, 3)),
            pltpu.SemaphoreType.DMA((16, 3)),
        ]
        self.outs = [jax.ShapeDtypeStruct((2, self.rows, D), BF16)]
        if shared_rows:
            self.outs.append(jax.ShapeDtypeStruct((4, 2, shared_rows, D), BF16))

    def helpers(self, g_send, g_recv):
        mine = {a: lax.axis_index(a) for a in ("x", "y", "z")}
        group = [0]

        def send_all(axis, src, dst):
            g = group[0]
            group[0] += 1
            copies = []
            for off in (2, 1, 3):
                peer = lax.rem(mine[axis] + off, 4)
                c = pltpu.make_async_remote_copy(
                    src_ref=src(peer, off),
                    dst_ref=dst(off - 1),
                    send_sem=g_send.at[g, off - 1],
                    recv_sem=g_recv.at[g, off - 1],
                    device_id={axis: peer},
                    device_id_type=MESH,
                )
                c.start()
                copies.append(c)
            return copies

        def wait(copies):
            for c in copies:
                c.wait()

        def add(dest, terms, rows, lead=None):
            step = 32 if rows % 32 == 0 else 16

            @pl.loop(0, rows, step=step)
            def _(r):
                at = pl.ds(pl.multiple_of(r, step), step)
                for b in range(lead or 1):
                    key = (b, at) if lead else (at,)
                    total = terms[0][key].astype(F32)
                    for t in terms[1:]:
                        total = total + t[key].astype(F32)
                    dest[key] = total.astype(BF16)

        def quarter(start, n, i):
            q = n // 4
            return pl.ds(pl.multiple_of(start + i * q, 16), q)

        return send_all, wait, add, quarter

    def first(self, ins, sums, scratch):
        count = len(ins)
        own, other = scratch[0 : 2 * count : 2], scratch[1 : 2 * count : 2]
        packed, ya, xz, s_loc, s_send, s_recv, g_send, g_recv = scratch[2 * count :]
        ta, tb = sums
        send_all, wait, add, quarter = self.helpers(g_send, g_recv)
        core, x, y, z = (lax.axis_index(a) for a in ("core", "x", "y", "z"))
        starts = [sum(self.parts[:k]) for k in range(4)]
        flight = []

        def begin(ready):
            while len(flight) < 4 and starts[len(flight)] + self.parts[len(flight)] <= ready:
                k = len(flight)
                at, n = starts[k], self.parts[k]
                if n == 0:
                    c = []
                elif k < 2:
                    c = send_all(
                        "y",
                        lambda p, o: packed.at[o, pl.ds(at, n), :],
                        lambda s: ya.at[k, s, pl.ds(0, n), :],
                    )
                else:
                    c = send_all(
                        "xz"[k - 2],
                        lambda p, o: packed.at[:, quarter(at, n, p), :],
                        lambda s: xz.at[k - 2, s, :, pl.ds(0, n // 4), :],
                    )
                flight.append(c)

        pair = dict(device_id={"core": 1 - core}, device_id_type=MESH)
        copies, everywhere = [], []

        def start(i):
            h, c = self.halves[i]
            if self.kinds[i] == "each":
                own[i][y] = ins[i][...]
                everywhere.extend(
                    send_all("y", lambda p, _: own[i].at[y], lambda s: own[i].at[y])
                )
                return
            for b in range(1 if self.kinds[i] == "cols" else 4):
                if self.kinds[i] == "cols":
                    theirs = ins[i].at[pl.ds((1 - core) * h, h), :]
                    ours = ins[i].at[pl.ds(core * h, h), :]
                    to, keep = other[i], own[i]
                else:
                    part = lax.rem(y + b, 4) if self.kinds[i] == "whole" else b
                    theirs = ins[i].at[pl.ds(part * 2 * h + (1 - core) * h, h), :]
                    ours = ins[i].at[pl.ds(part * 2 * h + core * h, h), :]
                    to, keep = other[i].at[b], own[i].at[b]
                r = pltpu.make_async_remote_copy(
                    src_ref=theirs,
                    dst_ref=to,
                    send_sem=s_send.at[i, b],
                    recv_sem=s_recv.at[i, b],
                    **pair,
                )
                l = pltpu.make_async_copy(ours, keep, s_loc.at[i, b])
                r.start()
                l.start()
                copies.extend([(i, r), (i, l)])

        return start, self.first_steps(
            own, other, packed, ya, xz, copies, everywhere, begin, flight, sums, s_send, s_recv,
            (send_all, wait, add, quarter),
        )

    def first_steps(
        self, own, other, packed, ya, xz, copies, everywhere, begin, flight, sums, s_send, s_recv,
        helpers,
    ):
        send_all, wait, add, quarter = helpers
        ta, tb = sums
        count = len(own)
        core, x, y, z = (lax.axis_index(a) for a in ("core", "x", "y", "z"))
        pair = dict(device_id={"core": 1 - core}, device_id_type=MESH)
        starts = [sum(self.parts[:k]) for k in range(4)]
        for i in range(count):
            if self.kinds[i] != "each":
                continue
            h, c = self.halves[i]
            wait(everywhere)
            add(other[i].at[0], [own[i].at[j] for j in range(4)], 2 * h)
            r = pltpu.make_async_remote_copy(
                src_ref=other[i].at[0, pl.ds((1 - core) * h, h), :],
                dst_ref=other[i].at[1, pl.ds(0, h), :],
                send_sem=s_send.at[i, 0],
                recv_sem=s_recv.at[i, 0],
                **pair,
            )
            r.start()
            copies.append((i, r))
        if self.rows > self.used:
            gap = self.rows - self.used
            for b in range(4):
                packed[b, pl.ds(self.used, gap), :] = jnp.zeros((gap, D), BF16)
        for i in range(count):
            for j, c in copies:
                if j == i:
                    c.wait()
            h, c = self.halves[i]
            at = self.offsets[i]
            tiles = c // 128
            if self.kinds[i] == "each":
                here = other[i][0, pl.ds(pl.multiple_of(core * h, 16), h), :]
                packed[0, pl.ds(at, h), :] = here + other[i][1, pl.ds(0, h), :]
                for b in range(1, 4):
                    packed[b, pl.ds(at, h), :] = jnp.zeros((h, c), BF16)
            elif self.kinds[i] != "cols":

                @pl.loop(0, h, step=16)
                def _(r):
                    row = pl.ds(pl.multiple_of(r, 16), 16)
                    to = pl.ds(pl.multiple_of(at + r, 16), 16)
                    for b in range(4):
                        packed[b, to, :] = own[i][b, row, :] + other[i][b, row, :]

            elif tiles == 4:

                @pl.loop(0, h, step=16)
                def _(r):
                    row = pl.ds(pl.multiple_of(r, 16), 16)
                    to = pl.ds(pl.multiple_of(at + r, 16), 16)
                    for b in range(4):
                        col = pl.ds(b * D, D)
                        packed[b, to, :] = own[i][row, col] + other[i][row, col]

            else:
                q = h // 4
                for g in range(4):
                    for t in range(tiles):
                        k = g * tiles + t
                        for b in range(4):
                            row, col = pl.ds(g * q, q), pl.ds(b * c + t * 128, 128)
                            to, tile = pl.ds(at + k // 4 * q, q), pl.ds(k % 4 * 128, 128)
                            packed[b, to, tile] = own[i][row, col] + other[i][row, col]

            begin(self.offsets[i + 1] if i + 1 < count else self.rows)

        yield
        for k in range(4):
            at, n = starts[k], self.parts[k]
            wait(flight[k])
            if n and k < 2:
                terms = [packed.at[0, pl.ds(at, n)]] + [ya.at[k, s] for s in range(3)]
                add(ta.at[k], terms, n)
            elif n:
                i = (x, z)[k - 2]
                terms = [packed.at[:, quarter(at, n, i), :]] + [xz.at[k - 2, s] for s in range(3)]
                add(tb.at[k - 2], terms, n // 4, 4)

    def second(self, sums, outs, scratch):
        ta, tb = sums
        ra, rb, fa, fb, g_send, g_recv = scratch
        out = outs[0]
        send_all, wait, add, quarter = self.helpers(g_send, g_recv)
        core, x, y, z = (lax.axis_index(a) for a in ("core", "x", "y", "z"))
        mine = {"x": x, "z": z}
        pair = dict(device_id={"core": 1 - core}, device_id_type=MESH)
        starts = [sum(self.parts[:k]) for k in range(4)]
        flight = []
        for k in range(4):
            n = self.parts[k]
            q = pl.ds(0, n // 4)
            if n == 0:
                c = []
            elif k < 2:
                c = send_all(
                    "xz"[k],
                    lambda p, _: ta.at[k, quarter(0, n, p), :],
                    lambda s: ra.at[k, s, q, :],
                )
            else:
                c = send_all(
                    "y", lambda p, o: tb.at[k - 2, o, q, :], lambda s: rb.at[k - 2, s, q, :]
                )
            flight.append(c)
        yield
        held = [(fa, fa, fb, fb)[k].at[k % 2] for k in range(4)]
        for k in range(4):
            n = self.parts[k]
            if n == 0:
                continue
            wait(flight[k])
            last_axis = "zx"[k % 2]
            here = held[k].at[mine[last_axis], pl.ds(0, n // 4), :]
            if k < 2:
                terms = [ta.at[k, quarter(0, n, (x, z)[k]), :]] + [ra.at[k, s] for s in range(3)]
            else:
                terms = [tb.at[k - 2, 0]] + [rb.at[k - 2, s] for s in range(3)]
            add(here, terms, n // 4)
            flight[k] = send_all(last_axis, lambda p, _: here, lambda s: here)
        yield
        for k in range(4):
            n = self.parts[k]
            if n == 0:
                continue
            wait(flight[k])
            piece = out.at[core, quarter(starts[k], n, (x, z)[k % 2]), :]
            add(piece, [held[k].at[j] for j in range(4)], n // 4)
            flight[k] = send_all("xz"[k % 2], lambda p, _: piece, lambda s: piece)
        yield
        for k in range(4):
            wait(flight[k])
        last = pltpu.make_async_remote_copy(
            src_ref=out.at[core],
            dst_ref=out.at[core],
            send_sem=g_send.at[14, 0],
            recv_sem=g_recv.at[14, 0],
            **pair,
        )
        last.start()
        if not self.shared:
            yield
            last.wait()
            return
        every = outs[1]
        start = self.used - self.shared
        every[y, core] = out[core, pl.ds(start, self.shared), :]
        spread = send_all("y", lambda p, _: every.at[y, core], lambda s: every.at[y, core])
        yield
        wait(spread)
        more = pltpu.make_async_remote_copy(
            src_ref=every.at[:, core],
            dst_ref=every.at[:, core],
            send_sem=g_send.at[15, 0],
            recv_sem=g_recv.at[15, 0],
            **pair,
        )
        more.start()
        yield
        last.wait()
        more.wait()

    def unpack(self, i, owned, dests):
        h, c = self.halves[i]
        at = self.offsets[i]
        tiles = c // 128
        if tiles == 4:
            for core in range(2):

                @pl.loop(0, h, step=16)
                def _(r):
                    to = pl.ds(pl.multiple_of(core * h + r, 16), 16)
                    row = pl.ds(pl.multiple_of(at + r, 16), 16)
                    dests[0][to, :] = owned[core, row, :].astype(F32)

            return
        q = h // 4
        each = tiles // len(dests)
        for core in range(2):
            for g in range(4):
                for t in range(tiles):
                    k = g * tiles + t
                    value = owned[core, pl.ds(at + k // 4 * q, q), pl.ds(k % 4 * 128, 128)]
                    to = pl.ds(core * h + g * q, q)
                    dests[t // each][to, pl.ds(t % each * 128, 128)] = value.astype(F32)


def write_gradients(late, owned, last, owned_last, mid, owned_mid, early, owned_early, every_early, channels):
    large = [(512, 512)] * 4 + [(512, channels)] * 2 + [(128, 512), (channels, 512), (1024, 512)]
    shapes = large[:4] + [(512, 2, channels)] + large[6:] + [(512, 128)] * 4 + [(31, 1024)] + [(1, 512)] * 10
    shapes += [(31, channels), (1, channels), (1, channels), (2, 64), (2, 64)]
    count = len(large)
    sources = (owned_early, every_early, owned_mid, owned, owned_last)

    def kernel(*refs):
        given, refs = refs[:5], refs[5:]
        outs, refs = refs[: count - 1], refs[count - 1 :]
        outs = [*outs[:4], outs[4].at[:, 0, :], outs[4].at[:, 1, :], *outs[5:]]
        wq, wk, wv, pos, taps = refs[:5]
        vectors, refs = refs[5:15], refs[15:]
        gate_taps, gain, shift, content, position, small, sem, load_sem = refs[:8]
        held, refs = refs[8 : 8 + count], refs[8 + count :]
        oe_ref, ee_ref, om_ref, o_ref, ol_ref = refs
        loads = [
            pltpu.make_async_copy(a, b, load_sem.at[k]) for k, (a, b) in enumerate(zip(given, refs))
        ]
        for c in loads:
            c.start()
        copies = []

        def send(k):
            c = pltpu.make_async_copy(held[k], outs[k], sem.at[k])
            c.start()
            copies.append(c)

        loads[0].wait()
        early.unpack(0, oe_ref, [held[2]])
        send(2)
        early.unpack(1, oe_ref, [held[3]])
        send(3)
        loads[1].wait()
        for y in range(4):
            for core in range(2):

                @pl.loop(0, 128, step=16)
                def _(r):
                    to = pl.ds(pl.multiple_of(y * 256 + core * 128 + r, 16), 16)
                    row = pl.ds(pl.multiple_of(r, 16), 16)
                    held[8][to, :] = ee_ref[y, core, row, :].astype(F32)

        send(8)
        loads[2].wait()
        for k, i in ((4, 0), (5, 1), (6, 2), (7, 3)):
            mid.unpack(i, om_ref, [held[k]])
            send(k)
        loads[3].wait()
        late.unpack(3, o_ref, [held[1]])
        send(1)
        loads[4].wait()
        last.unpack(0, ol_ref, [held[0]])
        send(0)
        late.unpack(0, o_ref, [wq, wk, wv])
        late.unpack(1, o_ref, [small])
        late.unpack(2, o_ref, [pos])
        at = last.offsets[1]
        rest = jnp.concatenate([ol_ref[core, pl.ds(at, 48), :].astype(F32) for core in range(2)])
        taps[:, pl.ds(0, 512)] = rest[0:31]
        taps[:, pl.ds(512, 512)] = rest[32:63]
        for k in range(10):
            vectors[k][...] = rest[64 + k : 65 + k]
        gate_taps[...] = small[pl.ds(0, 31), :]
        gain[...] = small[pl.ds(32, 1), :]
        shift[...] = small[pl.ds(33, 1), :]
        for k, ref in enumerate((content, position)):
            both = small[pl.ds(34 + k, 1), pl.ds(0, 128)]
            ref[pl.ds(0, 1), :] = both[:, :64]
            ref[pl.ds(1, 1), :] = both[:, 64:]
        for c in copies:
            c.wait()

    return pl.pallas_call(
        kernel,
        out_shape=[jax.ShapeDtypeStruct(s, F32) for s in shapes],
        in_specs=[ANY] * 5,
        out_specs=[ANY] * (count - 1) + [VM] * (len(shapes) - count + 1),
        scratch_shapes=[
            pltpu.VMEM((128, channels), F32),
            pltpu.SemaphoreType.DMA((count,)),
            pltpu.SemaphoreType.DMA((5,)),
        ]
        + [pltpu.VMEM(s, F32) for s in large]
        + [pltpu.VMEM(a.shape, a.dtype) for a in sources],
        compiler_params=pltpu.CompilerParams(vmem_limit_bytes=62 * 2**20),
        name="write_gradients",
    )(*sources)


def back(tensors, smalls, vectors, arrays, plans, cid):
    mid, late, last = plans
    n_tensors, n_small, n_vec = len(tensors), len(smalls), len(vectors)
    hidden = tensors[4].shape[1]

    def kernel(*refs):
        gqkv, wide_in, x_ref, middle, act_in, up_in, down_in, g_cg_in, g_merged, v_ref = refs[:10]
        refs = refs[n_tensors:]
        gate_taps, gain, shift, bias, pos, merge_taps = refs[:n_small]
        rows, refs = refs[n_small : n_small + n_vec], refs[n_small + n_vec :]
        ins, refs = refs[:4], refs[4:]
        g_features, o_late, o_last, o_mid = refs[:4]
        refs = refs[4:]
        small_f, shared_f, small, wide_pos, shared, g_wide, g_down, g_up, in1, g_mid, acc = refs[:11]
        wide, act, up1, down1, load_sem = refs[11:16]
        refs = refs[16:]
        sums_late, sums_last, sums_mid, refs = refs[:2], refs[2:4], refs[4:6], refs[6:]
        loads = [
            pltpu.make_async_copy(a, b, load_sem.at[k])
            for k, (a, b) in enumerate(
                ((wide_in, wide), (act_in, act), (down_in, down1), (up_in, up1))
            )
        ]
        for c in loads:
            c.start()

        def take(n):
            nonlocal refs
            got, refs = refs[:n], refs[n:]
            return got

        start1, l1 = late.first(
            [g_wide, small, wide_pos, g_down], sums_late, take(len(late.first_scratch))
        )
        start2, l2 = last.first([g_up, shared], sums_last, take(len(last.first_scratch)))
        s1 = late.second(sums_late, [o_late], take(len(late.scratch)))
        s2 = last.second(sums_last, [o_last], take(len(last.scratch)))
        start0, m1 = mid.first(ins, sums_mid, take(len(mid.first_scratch)))
        m2 = mid.second(sums_mid, [o_mid], take(len(mid.scratch)))
        vec = lambda k: v_ref[pl.ds(k, 1), :]
        slot = lambda k: pl.ds(k * D, D)
        total = lambda a: jnp.sum(a, 0, keepdims=True)

        greet(y=True, xz=True, pair=True)
        for k in range(4):
            start0(k)
        u2, inv2 = unit_norm(middle[...])
        attn_in = (u2 * vec(2) + vec(3)).astype(BF16)
        for k in range(3):
            g_wide[:, slot(k)] = contract_rows(attn_in, gqkv[:, slot(k)]).astype(BF16)
        start1(0)
        small_f[...] = jnp.zeros_like(small_f)
        small_f[pl.ds(0, 32), :] = gate_taps[...]
        small_f[pl.ds(32, 1), :] = gain[...]
        small_f[pl.ds(33, 1), :] = shift[...]
        small_f[pl.ds(34, 2), pl.ds(0, 128)] = bias[pl.ds(0, 2), :]
        small[...] = small_f[...].astype(BF16)
        start1(1)
        wide_pos[...] = jnp.zeros_like(wide_pos)
        wide_pos[:, pl.ds(0, 128)] = pos[...].astype(BF16)
        start1(2)
        shared_f[...] = jnp.zeros_like(shared_f)
        shared_f[pl.ds(0, 32), :] = merge_taps[:, pl.ds(0, D)]
        shared_f[pl.ds(32, 32), :] = merge_taps[:, pl.ds(D, D)]
        loads[0].wait()
        g_attn_in = times_transpose(gqkv[...], wide[...])
        g_gated = g_cg_in[...]
        shared_f[pl.ds(66, 1), :] = total(g_attn_in * u2)
        shared_f[pl.ds(67, 1), :] = total(g_attn_in)
        shared_f[pl.ds(68, 1), :] = total(g_gated * u2)
        shared_f[pl.ds(69, 1), :] = total(g_gated)
        for k, v in enumerate(rows):
            shared_f[pl.ds(70 + k, 1), :] = v[...]
        g_middle = g_merged[...] + norm_back(g_attn_in * vec(2) + g_gated * vec(4), u2, inv2)
        g_mid[...] = g_middle
        next(m1)
        gy1 = (0.5 * g_middle).astype(BF16)
        loads[1].wait()
        for k in range(hidden // D):
            a = act[:, slot(k)]
            hid = (a * jax.nn.sigmoid(a)).astype(BF16)
            g_down[slot(k), :] = contract_rows(hid, gy1).astype(BF16)
        start1(3)
        loads[2].wait()
        loads[3].wait()
        u1, inv1 = unit_norm(x_ref[...].astype(F32))
        in1[...] = (u1 * vec(0) + vec(1)).astype(BF16)
        acc[...] = jnp.zeros_like(acc)
        for k in range(hidden // D):
            a = act[:, slot(k)]
            sig = jax.nn.sigmoid(a)
            g_act = times_transpose(gy1, down1[slot(k), :]) * sig * (1.0 + a * (1.0 - sig))
            g_act = g_act.astype(BF16)
            g_up[:, slot(k)] = contract_rows(in1[...], g_act).astype(BF16)
            acc[...] += times_transpose(g_act, up1[k])
            if k == 2:
                next(l1)
        start2(0)
        u1, inv1 = unit_norm(x_ref[...].astype(F32))
        g_in1 = acc[...]
        shared_f[pl.ds(64, 1), :] = total(g_in1 * u1)
        shared_f[pl.ds(65, 1), :] = total(g_in1)
        shared[...] = shared_f[...].astype(BF16)
        start2(1)
        g_features[...] = g_mid[...] + norm_back(g_in1 * vec(0), u1, inv1)
        for _ in m1:
            pass
        next(m2)
        next(l2)
        for _ in l1:
            pass
        next(s1)
        next(m2)
        for _ in l2:
            pass
        next(s2)
        next(s1)
        next(m2)
        next(s2)
        next(s1)
        next(m2)
        next(s2)
        next(s1)
        next(s2)
        for g in (m2, s1, s2):
            for _ in g:
                pass

    bf = lambda *shape: pltpu.VMEM(shape, BF16)
    outs = [jax.ShapeDtypeStruct((ROWS, D), F32)] + late.outs + last.outs + mid.outs
    return pl.pallas_call(
        kernel,
        out_shape=outs,
        in_specs=[VM, ANY, VM, VM, ANY, ANY, ANY] + [VM] * (n_tensors - 7 + n_small + n_vec) + [ANY] * 4,
        out_specs=[VM] * len(outs),
        scratch_shapes=[
            pltpu.VMEM((128, GATE), F32),
            pltpu.VMEM((96, D), F32),
            bf(128, GATE),
            bf(D, D),
            bf(96, D),
            bf(D, 3 * D),
            bf(hidden, D),
            bf(D, hidden),
            bf(ROWS, D),
            pltpu.VMEM((ROWS, D), F32),
            pltpu.VMEM((ROWS, D), F32),
            bf(D, 3 * D),
            pltpu.VMEM((ROWS, hidden), F32),
            bf(GROUP, D, D),
            bf(hidden, D),
            pltpu.SemaphoreType.DMA((4,)),
        ]
        + [pltpu.VMEM(o.shape, BF16) for o in late.first_outs + last.first_outs + mid.first_outs]
        + late.first_scratch
        + last.first_scratch
        + late.scratch
        + last.scratch
        + mid.first_scratch
        + mid.scratch,
        compiler_params=params(cid, 60),
        name="back",
    )(*tensors, *smalls, *vectors, *arrays)


def local(
    features,
    lengths,
    first_gain,
    first_shift,
    first_up,
    first_down,
    attn_gain,
    attn_shift,
    w_query,
    w_key,
    w_value,
    w_pos,
    bias_content,
    bias_position,
    attn_out,
    cgmlp_gain,
    cgmlp_shift,
    cgmlp_up,
    gate_gain,
    gate_shift,
    gate_taps,
    cgmlp_down,
    merge_taps,
    merge_proj,
    second_gain,
    second_shift,
    second_up,
    second_down,
    final_gain,
    final_shift,
    cotangent,
):
    frames = ROWS * GROUP
    channels = gate_gain.shape[0]
    me = lax.axis_index("y")
    length = lengths[0]
    live = (jnp.arange(ROWS, dtype=jnp.int32) + me * ROWS < length).astype(F32)[:, None]
    mask = jnp.where(jnp.arange(frames, dtype=jnp.int32) < length, 0.0, -1e30)[None].astype(F32)
    rows_f, wide, small, *halves = prepare(
        (
            first_gain, first_shift, attn_gain, attn_shift, cgmlp_gain, cgmlp_shift, second_gain,
            second_shift, final_gain, final_shift,
        ),
        w_query, w_key, w_value, gate_taps, gate_gain, gate_shift, cgmlp_up,
    )
    (
        first_gain, first_shift, attn_gain, attn_shift, cgmlp_gain, cgmlp_shift, second_gain,
        second_shift, final_gain, final_shift,
    ) = (rows_f[k : k + 1] for k in range(10))
    sin, cos = position_factors(frames, D)
    biases = jnp.concatenate(
        [
            jnp.concatenate([bias_content, bias_position]).reshape(2, 128).astype(F32),
            jnp.zeros((6, 128), F32),
        ]
    )
    middle, invg, gate_out, act1, c0, c1, ug, gate_conv, gate_pad, qkv, *gathered = front(
        features,
        live,
        rows_f,
        (
            first_up, first_down, wide, halves[0], halves[1], small, attn_out, cgmlp_down,
            second_up, second_down,
        ),
        0,
    )
    up1, down1, qkv_w, cg0, cg1, small_all, out_w, cg_down, up2, down2 = gathered
    flat = lambda w: w.reshape(-1, w.shape[-1])
    down1, out_w, cg_down, down2 = flat(down1), flat(out_w), flat(cg_down), flat(down2)
    gate_taps_f = small_all[:32].astype(F32)
    gate_gain_f = small_all[31:32].astype(F32)
    merge_taps_f = jnp.pad(merge_taps.astype(F32), ((0, 1), (0, 0)))
    attended, attended_rows, weights = attention_forward(
        qkv, w_pos, biases, mask, sin, cos, 2
    )
    joined = jnp.concatenate([product(attended_rows, out_w), product(gate_out, cg_down)], axis=1)
    joined_live = joined * live
    merge_conv, joined_pad = conv_forward(joined_live, merge_taps_f, 3)
    mixed = (joined + merge_conv).astype(BF16)
    merged = middle + product(mixed, merge_proj)
    u3, inv3 = unit_norm(merged)
    in2 = (u3 * second_gain + second_shift).astype(BF16)
    act2 = product(in2, up2)
    sig2 = jax.nn.sigmoid(act2)
    hid2 = (act2 * sig2).astype(BF16)
    last = merged + 0.5 * product(hid2, down2)
    u4, inv4 = unit_norm(last)
    encoded = u4 * final_gain + final_shift

    u2, _ = unit_norm(middle)
    cg_in = (u2 * cgmlp_gain + cgmlp_shift).astype(BF16)
    root = 1.0 / math.sqrt(2.0)
    phi0 = 0.5 * (1.0 + lax.erf(c0 * root))
    phi1 = 0.5 * (1.0 + lax.erf(c1 * root))
    half0 = c0 * phi0

    cot = cotangent.astype(F32)
    g_final_gain = jnp.sum(cot * u4, 0)
    g_final_shift = jnp.sum(cot, 0)
    g_last = norm_back(cot * final_gain, u4, inv4)
    gy2 = (0.5 * g_last).astype(BF16)
    g_act2 = (times_transpose(gy2, down2) * sig2 * (1.0 + act2 * (1.0 - sig2))).astype(BF16)
    g_in2 = times_transpose(g_act2, up2)
    g_second_gain = jnp.sum(g_in2 * u3, 0)
    g_second_shift = jnp.sum(g_in2, 0)
    g_merged = g_last + norm_back(g_in2 * second_gain, u3, inv3)
    gm = g_merged.astype(BF16)
    gx = times_transpose(gm, merge_proj)
    merge_back, g_merge_taps, *early = conv_backward(
        gx, joined_pad, merge_taps_f, 4, factors=(in2, g_act2, hid2, gy2, mixed, gm)
    )
    g_joined = (gx + live * merge_back).astype(BF16)
    ga, gb = g_joined[:, :D], g_joined[:, D:]
    g_attended_rows = times_transpose(ga, out_w).astype(BF16)
    gg = times_transpose(gb, cg_down)
    g_conv = gg * half0
    plan_early = Reduction(
        [a.shape for a in early], ("cols", "rows", "whole"), (64, 64, 256, 256), 128
    )
    g_norm_raw, g_gate_taps, g_attended, *begun = conv_backward(
        g_conv, gate_pad, gate_taps_f, 5, g_attended_rows, early, plan_early
    )
    g_gate_norm = g_norm_raw * live
    g_gate_gain = jnp.sum(g_gate_norm * ug, 0)
    g_gate_shift = jnp.sum(g_gate_norm, 0)
    g_half1 = norm_back(g_gate_norm * gate_gain_f, ug, invg)
    density = 1.0 / math.sqrt(2.0 * math.pi)
    g_c0 = (gg * gate_conv * (phi0 + c0 * (density * jnp.exp(-0.5 * c0 * c0)))).astype(BF16)
    g_c1 = (g_half1 * (phi1 + c1 * (density * jnp.exp(-0.5 * c1 * c1)))).astype(BF16)
    g_cg_in = times_transpose(g_c0, cg0) + times_transpose(g_c1, cg1)
    plan_mid = Reduction(
        [(D, GATE), (D, GATE), (D, D), (GATE, D)],
        ("cols", "cols", "rows", "rows"),
        (64, 64, 256, 256),
    )
    g_qkv, g_w_pos, g_bias, owned_early, every_early, *mid = attention_backward(
        qkv, weights, attended, g_attended, w_pos, biases, sin, cos, plan_early, begun,
        (cg_in, g_c0, g_c1, attended_rows, gate_out, g_joined), 6,
    )
    plan_late = Reduction(
        [(D, 3 * D), (128, GATE), (D, D), (4 * D, D)],
        ("cols", "cols", "cols", "rows"),
        (64, 128, 192, 192),
    )
    plan_last = Reduction([(D, 4 * D), (96, D)], ("cols", "each"), (64, 0, 128, 128))
    g_features, owned, owned_last, owned_mid = back(
        (g_qkv, qkv_w, features, middle, act1, up1, down1, g_cg_in, g_merged, rows_f),
        (g_gate_taps, g_gate_gain[None], g_gate_shift[None], g_bias, g_w_pos, g_merge_taps),
        [v[None] for v in (g_second_gain, g_second_shift, g_final_gain, g_final_shift)],
        mid,
        (plan_mid, plan_late, plan_last),
        7,
    )
    (
        d_up1, d_down1, d_up2, d_down2, d_gated, d_out, d_cg_down, d_proj, d_query, d_key,
        d_value, d_pos, d_taps, *vectors, d_gate_taps, d_gain, d_shift, d_content,
        d_position,
    ) = write_gradients(
        plan_late, owned, plan_last, owned_last, plan_mid, owned_mid, plan_early, owned_early,
        every_early, channels,
    )
    vectors = [v.reshape(D) for v in vectors]
    return (
        encoded,
        g_features,
        vectors[0],
        vectors[1],
        d_up1,
        d_down1,
        vectors[2],
        vectors[3],
        d_query,
        d_key,
        d_value,
        d_pos,
        d_content,
        d_position,
        d_out,
        vectors[4],
        vectors[5],
        d_gated,
        d_gain.reshape(channels),
        d_shift.reshape(channels),
        d_gate_taps,
        d_cg_down,
        d_taps,
        d_proj,
        vectors[6],
        vectors[7],
        d_up2,
        d_down2,
        vectors[8],
        vectors[9],
    )


def solution(mesh):
    devices = mesh.devices.reshape(4, 4, 2, GROUP)
    fine = Mesh(devices, ("z", "x", "core", "y"))
    rows = P(("z", "x", "core", "y"), None)
    column, row = P(None, "y"), P("y", None)
    placed = (
        rows,
        P(("z", "x", "core")),
        P(),
        P(),
        column,
        row,
        P(),
        P(),
        column,
        column,
        column,
        column,
        row,
        row,
        row,
        P(),
        P(),
        P(None, None, "y"),
        P("y"),
        P("y"),
        column,
        row,
        P(),
        P(),
        P(),
        P(),
        column,
        row,
        P(),
        P(),
        rows,
    )
    return jax.shard_map(
        local,
        mesh=fine,
        in_specs=placed,
        out_specs=(rows,) + (rows,) + placed[2:30],
        check_vma=False,
    )
```

```python
import math

import jax
import jax.numpy as jnp
from jax import lax
from jax.experimental import pallas as pl
from jax.experimental.pallas import tpu as pltpu
from jax.sharding import Mesh, PartitionSpec as P

GATE = 1536
KERNEL = 31
D = 512
ROWS = 320
HALO = 16
GROUP = 4
EPS = 1e-05
F32 = jnp.float32
BF16 = jnp.bfloat16
MESH = pl.DeviceIdType.MESH
ANY = pl.BlockSpec(memory_space=pl.ANY)
VM = pl.BlockSpec(memory_space=pltpu.VMEM)


def product(a, b):
    return jnp.dot(a, b, preferred_element_type=F32)


def contract_rows(a, b):
    return lax.dot_general(a, b, (((0,), (0,)), ((), ())), preferred_element_type=F32)


def times_transpose(a, b):
    return lax.dot_general(a, b, (((1,), (1,)), ((), ())), preferred_element_type=F32)


def unit_norm(rows):
    center = rows - jnp.mean(rows, -1, keepdims=True)
    inverse = lax.rsqrt(jnp.mean(center * center, -1, keepdims=True) + EPS)
    return center * inverse, inverse


def norm_back(scaled, unit, inverse):
    inner = (
        scaled
        - jnp.mean(scaled, -1, keepdims=True)
        - unit * jnp.mean(scaled * unit, -1, keepdims=True)
    )
    return inner * inverse


def params(cid, vmem=48, **more):
    return pltpu.CompilerParams(
        collective_id=cid, has_side_effects=True, vmem_limit_bytes=vmem * 2**20, **more
    )


def ring():
    me = lax.axis_index("y")
    return me, lax.rem(me + 1, GROUP), lax.rem(me + GROUP - 1, GROUP), lax.rem(me + 2, GROUP)


def to_y(where):
    return dict(device_id={"y": where}, device_id_type=MESH)


def greet_ring(offsets):
    me = lax.axis_index("y")
    barrier = pltpu.get_barrier_semaphore()
    for off in offsets:
        pl.semaphore_signal(barrier, inc=1, **to_y(lax.rem(me + off, GROUP)))
    pl.semaphore_wait(barrier, len(offsets))


def greet(y=False, xz=False, pair=False):
    barrier = pltpu.get_barrier_semaphore()
    count = 0
    for axis in (("y",) if y else ()) + (("x", "z") if xz else ()):
        me = lax.axis_index(axis)
        for off in (1, 2, 3):
            where = {axis: lax.rem(me + off, 4)}
            pl.semaphore_signal(barrier, inc=1, device_id=where, device_id_type=MESH)
            count += 1
    if pair:
        where = {"core": 1 - lax.axis_index("core")}
        pl.semaphore_signal(barrier, inc=1, device_id=where, device_id_type=MESH)
        count += 1
    pl.semaphore_wait(barrier, count)


class Gather:
    def __init__(self, shards, kinds, entries):
        self.kinds = kinds
        self.entries = entries
        self.shapes = [s.shape for s in shards]
        count = len(entries)
        self.outs = []
        for s, kind in zip(shards, kinds):
            rows, cols = s.shape
            shape = (GROUP, rows, cols) if kind == "rows" else (rows, GROUP * cols)
            self.outs.append(jax.ShapeDtypeStruct(shape, s.dtype))
        self.scratch = [
            pltpu.SemaphoreType.DMA((count,)),
            pltpu.SemaphoreType.DMA((count, 10)),
            pltpu.SemaphoreType.DMA((count, 10)),
        ]

    def open(self, srcs, dsts, scratch):
        local_sem, send, recv = scratch
        core, x, y, z = (lax.axis_index(a) for a in ("core", "x", "y", "z"))
        mine = {"x": x, "y": y, "z": z}
        pair = dict(device_id={"core": 1 - core}, device_id_type=MESH)

        def spot(e, slot, slots, start, size, lane=None):
            i, first, width, _ = self.entries[e]
            cols = self.shapes[i][1]
            if self.kinds[i] == "rows":
                at = pl.ds(first, width) if lane is None else lane
                return dsts[i].at[pl.ds(slot, slots), pl.ds(start, size), at]
            return dsts[i].at[pl.ds(start, size), pl.ds(slot * cols, slots * cols)]

        def cut(e, level):
            i, first, width, route = self.entries[e]
            half = self.shapes[i][0] // 2
            if level == 2 or route == "A":
                return core * half, half, None
            if half % 256:
                lane = pl.ds(pl.multiple_of(z * (width // 4), 128), width // 4)
                row, size = core * half + x * (half // 4), half // 4
                if level == 0:
                    return row, size, lane
                return (row, size, None) if route == "B" else (core * half, half, lane)
            a, b = (x, z) if route == "B" else (z, x)
            if level == 0:
                return core * half + (a * 4 + b) * (half // 16), half // 16, None
            return core * half + a * (half // 4), half // 4, None

        def remote(src, dst, e, k, where):
            return pltpu.make_async_remote_copy(
                src_ref=src, dst_ref=dst, send_sem=send.at[e, k], recv_sem=recv.at[e, k], **where
            )

        def spread(e, axis, level, k):
            at = spot(e, 1, 3, *cut(e, level))
            copies = []
            for off in (2, 1, 3):
                where = dict(device_id={axis: lax.rem(mine[axis] + off, 4)}, device_id_type=MESH)
                copies.append(remote(at, at, e, k + off - 1, where))
                copies[-1].start()
            return copies

        def to_pair(e):
            at = spot(e, 1, 3, *cut(e, 2))
            c = remote(at, at, e, 9, pair)
            c.start()
            return c

        flight, level = {}, {}

        def start(e):
            i, first, width, _ = self.entries[e]
            row, size, lane = cut(e, 0)
            at = pl.ds(first, width) if lane is None else lane
            piece = srcs[i].at[pl.ds(row, size), at]
            copies = []
            for off in (2, 1, 3):
                there = spot(e, 4 - off, 1, row, size, lane)
                there = there.at[0] if self.kinds[i] == "rows" else there
                copies.append(remote(piece, there, e, off - 1, to_y(lax.rem(y + off, 4))))
                copies[-1].start()
            there = spot(e, 0, 1, 0, self.shapes[i][0])
            there = there.at[0] if self.kinds[i] == "rows" else there
            own = pltpu.make_async_copy(srcs[i].at[:, pl.ds(first, width)], there, local_sem.at[e])
            own.start()
            flight[e], level[e] = copies, 0
            return own

        def step(e):
            for c in flight[e]:
                c.wait()
            route, at = self.entries[e][3], level[e]
            if route == "A" and at == 0:
                at = 2
            if at == 0:
                flight[e] = spread(e, "z" if route == "B" else "x", 0, 3)
            elif at == 1:
                flight[e] = spread(e, "x" if route == "B" else "z", 1, 6)
            elif at == 2:
                flight[e] = [to_pair(e)]
            level[e] = at + 1

        return start, step


def split_copies(src, dst, send, recv, local_sem):
    me = lax.axis_index("y")
    width = src.shape[1] // GROUP
    there = dst.at[pl.ds(pl.multiple_of(me * ROWS, ROWS), ROWS), :]
    copies = []
    for off in (2, 1, 3):
        c = pltpu.make_async_remote_copy(
            src_ref=src.at[:, pl.ds(off * width, width)],
            dst_ref=there,
            send_sem=send.at[off],
            recv_sem=recv.at[off],
            **to_y(lax.rem(me + off, GROUP)),
        )
        c.start()
        copies.append(c)
    own = pltpu.make_async_copy(src.at[:, pl.ds(0, width)], there, local_sem)
    own.start()
    copies.append(own)
    return copies


def start_halo(edges, prev, nxt, send, recv, slots):
    _, up, down, _ = ring()
    cols = prev.shape[1]
    w = cols // GROUP
    turns = ((w, 0, 3 * w), (0, 3 * w, w)) if slots else ((0, 0, cols),)
    copies = []
    for t, (here, there, size) in enumerate(turns):
        for side, ref, where in ((1, prev, up), (0, nxt, down)):
            a, b = (here, there) if side else (there, here)
            c = pltpu.make_async_remote_copy(
                src_ref=edges.at[side, :, pl.ds(a, size)],
                dst_ref=ref.at[:, pl.ds(b, size)],
                send_sem=send.at[side, t],
                recv_sem=recv.at[side, t],
                **to_y(where),
            )
            c.start()
            copies.append(c)
    return copies


def lanes(b):
    return pl.ds(pl.multiple_of(b * 128, 128), 128)


CHUNK = 64


def conv_block(pad, taps, b, flip):
    weights = [taps[pl.ds(KERNEL - 1 - o if flip else o, 1), lanes(b)] for o in range(KERNEL)]
    for r in range(0, ROWS, CHUNK):
        total = None
        for o in range(KERNEL):
            term = weights[o] * pad[b, pl.ds(r + o + 1, CHUNK), :]
            total = term if total is None else total + term
        yield r, total


def taps_block(pad, g_pad, b, out):
    sums = [None] * KERNEL
    for r in range(0, ROWS, CHUNK):
        g = g_pad[b, pl.ds(HALO + r, CHUNK), :]
        for o in range(KERNEL):
            term = g * pad[b, pl.ds(r + o + 1, CHUNK), :]
            term = jnp.sum(term.reshape(CHUNK // 8, 8, 128), 0)
            sums[o] = term if sums[o] is None else sums[o] + term
    for o in range(KERNEL):
        out[pl.ds(o, 1), lanes(b)] = jnp.sum(sums[o], 0, keepdims=True)


def fill_middle(x_ref, pad, blocks):
    @pl.loop(0, blocks)
    def _(b):
        pad[b, pl.ds(HALO, ROWS), :] = x_ref[:, lanes(b)].astype(F32)


def fill_ends(prev, nxt, pad, blocks):
    me = lax.axis_index("y")
    has_prev = jnp.where(me > 0, 1.0, 0.0)
    has_next = jnp.where(me < GROUP - 1, 1.0, 0.0)

    @pl.loop(0, blocks)
    def _(b):
        pad[b, pl.ds(0, HALO), :] = prev[:, lanes(b)].astype(F32) * has_prev
        pad[b, pl.ds(HALO + ROWS, HALO), :] = nxt[:, lanes(b)].astype(F32) * has_next


def set_edges(x_ref, edges):
    edges[0] = x_ref[pl.ds(0, HALO), :].astype(BF16)
    edges[1] = x_ref[pl.ds(ROWS - HALO, HALO), :].astype(BF16)


def conv_forward(x, taps, cid):
    cols = x.shape[1]
    blocks = cols // 128

    def kernel(x_ref, t_ref, o_ref, pad, edges, prev, nxt, hs, hr):
        greet_ring((1, 3))
        set_edges(x_ref, edges)
        halos = start_halo(edges, prev, nxt, hs, hr, False)
        fill_middle(x_ref, pad, blocks)
        for c in halos:
            c.wait()
        fill_ends(prev, nxt, pad, blocks)

        @pl.loop(0, blocks)
        def _(blk):
            for r, value in conv_block(pad, t_ref, blk, False):
                o_ref[pl.ds(r, CHUNK), lanes(blk)] = value

    return pl.pallas_call(
        kernel,
        out_shape=[
            jax.ShapeDtypeStruct((ROWS, cols), F32),
            jax.ShapeDtypeStruct((blocks, ROWS + 2 * HALO, 128), F32),
        ],
        in_specs=[VM, VM],
        out_specs=[VM, VM],
        scratch_shapes=[
            pltpu.VMEM((2, HALO, cols), BF16),
            pltpu.VMEM((HALO, cols), BF16),
            pltpu.VMEM((HALO, cols), BF16),
            pltpu.SemaphoreType.DMA((2, 2)),
            pltpu.SemaphoreType.DMA((2, 2)),
        ],
        compiler_params=params(cid),
        name="conv_forward",
    )(x, taps)


def erf(v):
    v = jnp.clip(v, -3.832506856900711, 3.832506856900711)
    w = v * v
    top = jnp.full_like(w, -2.72614225801306e-10)
    for c in (
        2.77068142495902e-08, -2.10102402082508e-06, -5.69250639462346e-05, -7.34990630326855e-04,
        -2.95459980854025e-03, -1.60960333262415e-02,
    ):
        top = top * w + c
    low = jnp.full_like(w, -1.45660718464996e-05)
    for c in (-2.13374055278905e-04, -1.68282697438203e-03, -7.37332916720468e-03, -1.42647390514189e-02):
        low = low * w + c
    return v * top / low


def prepare(vectors, w_query, w_key, w_value, gate_taps, gate_gain, gate_shift, gated):
    count = len(vectors)
    cols = gate_taps.shape[1]

    def kernel(*refs):
        wq, wk, wv, taps, gain, shift, both = refs[count : count + 7]
        rows, wide, small, first, second, small_f = refs[count + 7 :]
        first[...] = both[:, 0, :]
        second[...] = both[:, 1, :]
        rows[...] = jnp.zeros_like(rows)
        for k in range(count):
            rows[pl.ds(k, 1), :] = refs[k][...].astype(F32).reshape(1, D)
        for k, w in enumerate((wq, wk, wv)):
            wide[:, pl.ds(k * 128, 128)] = w[...]
        small_f[...] = jnp.zeros_like(small_f)
        small_f[pl.ds(0, KERNEL), :] = taps[...].astype(F32)
        small_f[pl.ds(31, 1), :] = gain[...].astype(F32).reshape(1, cols)
        small_f[pl.ds(32, 1), :] = shift[...].astype(F32).reshape(1, cols)
        small[...] = small_f[...].astype(BF16)

    return pl.pallas_call(
        kernel,
        out_shape=[
            jax.ShapeDtypeStruct((16, D), F32),
            jax.ShapeDtypeStruct((D, 384), BF16),
            jax.ShapeDtypeStruct((64, cols), BF16),
            jax.ShapeDtypeStruct((D, cols), BF16),
            jax.ShapeDtypeStruct((D, cols), BF16),
        ],
        in_specs=[VM] * (count + 7),
        out_specs=[VM] * 5,
        scratch_shapes=[pltpu.VMEM((64, cols), F32)],
        name="prepare",
    )(*vectors, w_query, w_key, w_value, gate_taps, gate_gain, gate_shift, gated)


def front(features, live, vectors, shards, cid):
    kinds = ("rows", "rows", "cols", "cols", "cols", "cols", "rows", "rows", "cols", "rows")
    up1, down1, wide, cg0, cg1, small, out, cgd, up2, down2 = range(10)
    half = D // 2
    entries = (
        (up1, 0, half, "A"),
        (down1, 0, half, "A"),
        (up1, half, half, "B"),
        (down1, half, half, "C"),
        (wide, 0, 384, "B"),
        (cg0, 0, 384, "C"),
        (cg1, 0, 384, "A"),
        (small, 0, 384, "A"),
        (out, 0, D, "B"),
        (cgd, 0, D, "C"),
        (up2, 0, D, "B"),
        (down2, 0, D, "C"),
    )
    plan = Gather(shards, kinds, entries)
    blocks = GATE // 128
    hidden = GROUP * D

    def kernel(*refs):
        x_ref, live_ref, v_ref = refs[:3]
        srcs, refs = refs[3:13], refs[13:]
        middle, inv, gate_out = refs[:3]
        act_out, c0_out, c1_out, ug_out, conv_out, pad_out, qkv_out = refs[3:10]
        w_out, refs = refs[10:20], refs[20:]
        w_in, refs = refs[:6], refs[6:]
        act, c0, c1, ug, conv, pad, qkv, acc, cg_in, half, taps, edges, prev, nxt = refs[:14]
        hs, hr, ss, sr, sl, out_sem = refs[14:20]
        dsts = [*w_in, *w_out[6:]]
        start, step = plan.open(srcs, dsts, refs[20:])
        greet(y=True, xz=True, pair=True)
        own = {}
        for e in (2, 3, 4, 5, 0, 1, 10, 11, 8, 9, 6, 7):
            own[e] = start(e)
        saves = []

        def save(src, dst):
            c = pltpu.make_async_copy(src, dst, out_sem.at[len(saves)])
            c.start()
            saves.append(c)

        rows = x_ref[...].astype(F32)
        unit, _ = unit_norm(rows)
        in1 = (unit * v_ref[pl.ds(0, 1), :] + v_ref[pl.ds(1, 1), :]).astype(BF16)

        def hidden_slot(k):
            at = pl.ds(k * D, D)
            a = product(in1, w_in[up1][k])
            act[:, at] = a
            return product((a * jax.nn.sigmoid(a)).astype(BF16), w_in[down1][k])

        for e in range(4):
            own[e].wait()
        acc[...] = hidden_slot(0)
        for e in (2, 3, 4, 5, 2, 3, 4, 5):
            step(e)
        for e in (0, 1, 2, 3, 10, 11, 8, 9, 0, 1, 2, 3):
            step(e)
        total = acc[...]
        for k in range(1, 4):
            total = total + hidden_slot(k)
        save(act, act_out)
        save(w_in[up1], w_out[up1])
        save(w_in[down1], w_out[down1])
        rows = rows + 0.5 * total
        middle[...] = rows
        unit, _ = unit_norm(rows)
        attn_in = (unit * v_ref[pl.ds(2, 1), :] + v_ref[pl.ds(3, 1), :]).astype(BF16)
        cg_in[...] = (unit * v_ref[pl.ds(4, 1), :] + v_ref[pl.ds(5, 1), :]).astype(BF16)
        for e in (4, 5, 10, 11, 8, 9, 6, 7):
            step(e)
        step(4)
        own[4].wait()
        for k in range(4):
            at = pl.ds(k * 384, 384)
            qkv[:, at] = product(attn_in, w_in[wide][:, at]).astype(BF16)
        waits = split_copies(qkv, qkv_out, ss, sr, sl)
        save(w_in[wide], w_out[wide])
        for e in (6, 7, 5):
            step(e)
            own[e].wait()
        for k in range(3):
            at = pl.ds(k * D, D)
            c1[:, at] = product(cg_in[...], w_in[cg1][:, at])
        save(c1, c1_out)
        save(w_in[cg1], w_out[cg1])
        gain = w_in[small][pl.ds(16, 16), :][15:16].astype(F32)
        shift = w_in[small][pl.ds(32, 16), :][0:1].astype(F32)
        root = 1.0 / math.sqrt(2.0)

        @pl.loop(0, ROWS, step=16)
        def _(r):
            at = pl.ds(pl.multiple_of(r, 16), 16)
            c = c1[at, :]
            unit, inverse = unit_norm(c * (0.5 * (1.0 + erf(c * root))))
            ug[at, :] = unit
            inv[at, :] = inverse
            norm = (unit * gain + shift) * live_ref[at, :]
            for b in range(blocks):
                pad[b, pl.ds(pl.multiple_of(HALO + r, 16), 16), :] = norm[:, b * 128 : b * 128 + 128]

        save(ug, ug_out)
        for side, r in ((0, HALO), (1, ROWS)):
            for b in range(blocks):
                edges[side, :, pl.ds(b * 128, 128)] = pad[b, pl.ds(r, HALO), :].astype(BF16)
        halos = start_halo(edges, prev, nxt, hs, hr, True)
        for k in range(3):
            at = pl.ds(k * D, D)
            c0[:, at] = product(cg_in[...], w_in[cg0][:, at])
        save(c0, c0_out)
        save(w_in[cg0], w_out[cg0])
        save(w_in[small], w_out[small])

        @pl.loop(0, ROWS, step=16)
        def _(r):
            at = pl.ds(pl.multiple_of(r, 16), 16)
            c = c0[at, :]
            half[at, :] = c * (0.5 * (1.0 + erf(c * root)))

        for c in halos:
            c.wait()
        fill_ends(prev, nxt, pad, blocks)
        save(pad, pad_out)
        for e in (10, 11, 8, 9):
            step(e)
        taps[...] = w_in[small][pl.ds(0, 32), :].astype(F32)

        @pl.loop(0, blocks)
        def _(blk):
            for r, value in conv_block(pad, taps, blk, False):
                at = pl.ds(r, CHUNK)
                conv[at, lanes(blk)] = value
                gate_out[at, lanes(blk)] = (value * half[at, lanes(blk)]).astype(BF16)

        save(conv, conv_out)
        for e in (10, 11, 8, 9):
            step(e)
            own[e].wait()
        for c in waits + saves:
            c.wait()

    f32 = lambda *shape: jax.ShapeDtypeStruct(shape, F32)
    pad_shape = (blocks, ROWS + 2 * HALO, 128)
    outs = [f32(ROWS, D), f32(ROWS, 1), jax.ShapeDtypeStruct((ROWS, GATE), BF16)]
    outs += [f32(ROWS, hidden)] + [f32(ROWS, GATE)] * 4 + [f32(*pad_shape)]
    outs += [jax.ShapeDtypeStruct((ROWS * GROUP, 3 * 128), BF16)]
    return pl.pallas_call(
        kernel,
        out_shape=outs + plan.outs,
        in_specs=[VM] * 3 + [ANY] * 10,
        out_specs=[VM] * 3 + [ANY] * 17,
        scratch_shapes=[pltpu.VMEM(o.shape, o.dtype) for o in plan.outs[:6]]
        + [
            pltpu.VMEM((ROWS, hidden), F32),
            pltpu.VMEM((ROWS, GATE), F32),
            pltpu.VMEM((ROWS, GATE), F32),
            pltpu.VMEM((ROWS, GATE), F32),
            pltpu.VMEM((ROWS, GATE), F32),
            pltpu.VMEM(pad_shape, F32),
            pltpu.VMEM((ROWS, 3 * D), BF16),
            pltpu.VMEM((ROWS, D), F32),
            pltpu.VMEM((ROWS, D), BF16),
            pltpu.VMEM((ROWS, GATE), F32),
            pltpu.VMEM((32, GATE), F32),
            pltpu.VMEM((2, HALO, GATE), BF16),
            pltpu.VMEM((HALO, GATE), BF16),
            pltpu.VMEM((HALO, GATE), BF16),
            pltpu.SemaphoreType.DMA((2, 2)),
            pltpu.SemaphoreType.DMA((2, 2)),
            pltpu.SemaphoreType.DMA((GROUP,)),
            pltpu.SemaphoreType.DMA((GROUP,)),
            pltpu.SemaphoreType.DMA,
            pltpu.SemaphoreType.DMA((12,)),
        ]
        + plan.scratch,
        compiler_params=params(cid, 60),
        name="front",
    )(features, live, vectors, *shards)


def conv_backward(g, pad, taps, cid, heads_in=None, arrays=(), plan=None, factors=()):
    cols = g.shape[1]
    blocks = cols // 128
    extra = heads_in is not None
    count = len(arrays)
    firsts = len(plan.first_outs) if extra else 0
    pairs = len(factors) // 2
    shapes = [(factors[2 * k].shape[1], factors[2 * k + 1].shape[1]) for k in range(pairs)]

    def kernel(*refs):
        g_ref, pad_in, t_ref = refs[:3]
        if extra:
            h_ref, refs = refs[3], refs[4:]
            ins, refs = refs[:count], refs[count:]
            o_ref, tg_ref, ho_ref = refs[:3]
            sums, refs = refs[3 : 3 + firsts], refs[3 + firsts :]
            g_pad, pad, load_sem, edges, prev, nxt, hs, hr, ss, sr, sl = refs[:11]
            start, riding = plan.first(ins, sums, refs[11:])
        else:
            given, refs = refs[3 : 3 + 2 * pairs], refs[3 + 2 * pairs :]
            o_ref, tg_ref = refs[:2]
            made, refs = refs[2 : 2 + pairs], refs[2 + pairs :]
            g_pad, pad, load_sem, edges, prev, nxt, hs, hr = refs[:8]
            held, results = refs[8 : 8 + 2 * pairs], refs[8 + 2 * pairs : 8 + 3 * pairs]
            in_sem, out_sem = refs[8 + 3 * pairs :]
            needed = [
                pltpu.make_async_copy(a, b, in_sem.at[k])
                for k, (a, b) in enumerate(zip(given, held))
            ]
            for c in needed:
                c.start()
        load = pltpu.make_async_copy(pad_in, pad, load_sem)
        load.start()
        if extra:
            greet(y=True, xz=True, pair=True)
        else:
            greet_ring((1, 3))
        set_edges(g_ref, edges)
        halos = start_halo(edges, prev, nxt, hs, hr, extra)
        waits = split_copies(h_ref, ho_ref, ss, sr, sl) if extra else []
        for i in range(count):
            start(i)
        fill_middle(g_ref, g_pad, blocks)
        tg_ref[pl.ds(24, 8), :] = jnp.zeros((8, cols), F32)
        load.wait()
        parts = ((0, 7), (7, blocks)) if extra else ((0, blocks),)
        for low, high in parts:

            @pl.loop(low, high)
            def _(blk):
                taps_block(pad, g_pad, blk, tg_ref)

            if extra and low == 0:
                next(riding)

        saves = []
        if not extra:
            for c in needed:
                c.wait()
            for k in range(pairs):
                left, right, result = held[2 * k], held[2 * k + 1], results[k]
                for at in range(0, max(result.shape), D):
                    part = pl.ds(at, D)
                    if result.shape[0] > result.shape[1]:
                        result[part, :] = contract_rows(left[:, part], right[...]).astype(BF16)
                    else:
                        result[:, part] = contract_rows(left[...], right[:, part]).astype(BF16)
                saves.append(pltpu.make_async_copy(result, made[k], out_sem.at[k]))
                saves[-1].start()
        for c in halos:
            c.wait()
        fill_ends(prev, nxt, g_pad, blocks)

        @pl.loop(0, blocks)
        def _(blk):
            for r, value in conv_block(g_pad, t_ref, blk, True):
                o_ref[pl.ds(r, CHUNK), lanes(blk)] = value

        for c in waits + saves:
            c.wait()
        if extra:
            for _ in riding:
                pass

    outs = [jax.ShapeDtypeStruct((ROWS, cols), F32), jax.ShapeDtypeStruct((32, cols), F32)]
    ins = [g, pad, taps]
    scratch = [
        pltpu.VMEM((blocks, ROWS + 2 * HALO, 128), F32),
        pltpu.VMEM((blocks, ROWS + 2 * HALO, 128), F32),
        pltpu.SemaphoreType.DMA,
        pltpu.VMEM((2, HALO, cols), BF16),
        pltpu.VMEM((HALO, cols), BF16),
        pltpu.VMEM((HALO, cols), BF16),
        pltpu.SemaphoreType.DMA((2, 2)),
        pltpu.SemaphoreType.DMA((2, 2)),
    ]
    in_specs, out_specs = [VM, ANY, VM], [VM, VM]
    if extra:
        ins += [heads_in, *arrays]
        in_specs += [ANY] * (1 + count)
        outs.append(
            jax.ShapeDtypeStruct((ROWS * GROUP, heads_in.shape[1] // GROUP), heads_in.dtype)
        )
        outs += plan.first_outs
        out_specs += [ANY] + [VM] * firsts
        scratch += [
            pltpu.SemaphoreType.DMA((GROUP,)),
            pltpu.SemaphoreType.DMA((GROUP,)),
            pltpu.SemaphoreType.DMA,
        ] + plan.first_scratch
    else:
        ins += factors
        in_specs += [ANY] * (2 * pairs)
        outs += [jax.ShapeDtypeStruct(s, BF16) for s in shapes]
        out_specs += [ANY] * pairs
        scratch += [pltpu.VMEM(a.shape, BF16) for a in factors]
        scratch += [pltpu.VMEM(s, BF16) for s in shapes]
        scratch += [pltpu.SemaphoreType.DMA((2 * pairs,)), pltpu.SemaphoreType.DMA((pairs,))]
    return pl.pallas_call(
        kernel,
        out_shape=outs,
        in_specs=in_specs,
        out_specs=out_specs,
        scratch_shapes=scratch,
        compiler_params=params(cid),
        name="conv_backward",
    )(*ins)


def position_factors(frames, width):
    frequency = jnp.exp(
        jnp.arange(width // 2, dtype=jnp.int32).astype(F32) * (-2.0 * math.log(10000.0) / width)
    )
    steps = jnp.concatenate(
        [32 * jnp.arange(frames // 32, dtype=jnp.int32), jnp.arange(32, dtype=jnp.int32)]
    )
    angles = steps.astype(F32)[:, None] * frequency[None]
    return jnp.sin(angles), jnp.cos(angles)


def fill_table(sin_parts, cos_parts, sin, cos, table):
    frames, half = sin.shape
    sb, cb = sin_parts[pl.ds(frames // 32, 32), :], cos_parts[pl.ds(frames // 32, 32), :]

    @pl.loop(0, frames // 32)
    def _(a):
        at = pl.ds(pl.multiple_of(a * 32, 32), 32)
        sa, ca = sin_parts[pl.ds(a, 1), :], cos_parts[pl.ds(a, 1), :]
        s, c = sa * cb + ca * sb, ca * cb - sa * sb
        sin[at, :] = s
        cos[at, :] = c
        table[at, pl.ds(0, half)] = s.astype(BF16)
        table[at, pl.ds(half, half)] = c.astype(BF16)


def head_mask(h):
    column = lax.broadcasted_iota(jnp.int32, (1, 128), 1)
    return jnp.where((column >= 64 * h) & (column < 64 * h + 64), 1.0, 0.0)


def rotated(query, sin, cos, w_pos):
    z = times_transpose(query, w_pos)
    zs, zc = z[:, : D // 2], z[:, D // 2 :]
    return jnp.concatenate([zc * sin - zs * cos, zs * sin + zc * cos], axis=1).astype(BF16)


def attention_forward(qkv, w_pos, biases, mask, sin, cos, cid):
    frames = qkv.shape[0]

    def kernel(
        x_ref, wp_ref, b_ref, m_ref, sp_ref, cp_ref, o_ref, rows_ref, p_ref,
        p_buf, t_ref, s_ref, c_ref, p_sem, ss, sr, sl,
    ):
        me = lax.axis_index("y")
        greet_ring((1, 2, 3))
        fill_table(sp_ref, cp_ref, s_ref, c_ref, t_ref)
        saves, sends = [], []
        for k in range(GROUP):
            peer = lax.rem(me + 1 + k, GROUP)
            at = pl.ds(pl.multiple_of(peer * ROWS, ROWS), ROWS)
            query = x_ref[at, pl.ds(0, 128)].astype(F32)
            if k >= 2:
                saves[k - 2].wait()
            total = jnp.zeros((ROWS, 128), F32)
            for h in range(2):
                keep = head_mask(h)
                content = ((query + b_ref[pl.ds(0, 1), :]) * (0.125 * keep)).astype(BF16)
                position = ((query + b_ref[pl.ds(1, 1), :]) * (0.125 * keep)).astype(BF16)
                turned = rotated(position, s_ref[at, :], c_ref[at, :], wp_ref[...])
                scores = times_transpose(turned, t_ref[...])
                scores = scores + times_transpose(content, x_ref[:, pl.ds(128, 128)])
                scores = scores + m_ref[...]
                top = jnp.max(scores, -1, keepdims=True)
                weights = jnp.exp(scores - top)
                weights = (weights * (1.0 / jnp.sum(weights, -1, keepdims=True))).astype(BF16)
                p_buf[k % 2, h] = weights
                total = total + product(weights, x_ref[:, pl.ds(256, 128)]) * keep
            o_ref[at, :] = total.astype(BF16)
            save = pltpu.make_async_copy(p_buf.at[k % 2], p_ref.at[:, at, :], p_sem.at[k % 2])
            save.start()
            saves.append(save)
            into = rows_ref.at[:, pl.ds((3 - k) * 128, 128)]
            if k < GROUP - 1:
                c = pltpu.make_async_remote_copy(
                    src_ref=o_ref.at[at, :],
                    dst_ref=into,
                    send_sem=ss.at[k],
                    recv_sem=sr.at[k],
                    **to_y(peer),
                )
            else:
                c = pltpu.make_async_copy(o_ref.at[at, :], into, sl)
            c.start()
            sends.append(c)
        saves[2].wait()
        saves[3].wait()
        for c in sends:
            c.wait()

    return pl.pallas_call(
        kernel,
        in_specs=[VM] * 6,
        out_specs=[VM, ANY, ANY],
        out_shape=[
            jax.ShapeDtypeStruct((frames, 128), BF16),
            jax.ShapeDtypeStruct((ROWS, D), BF16),
            jax.ShapeDtypeStruct((2, frames, frames), BF16),
        ],
        scratch_shapes=[
            pltpu.VMEM((2, 2, ROWS, frames), BF16),
            pltpu.VMEM((frames, D), BF16),
            pltpu.VMEM((frames, D // 2), F32),
            pltpu.VMEM((frames, D // 2), F32),
            pltpu.SemaphoreType.DMA((2,)),
            pltpu.SemaphoreType.DMA((3,)),
            pltpu.SemaphoreType.DMA((3,)),
            pltpu.SemaphoreType.DMA,
        ],
        compiler_params=params(cid),
        name="attention_forward",
    )(qkv, w_pos, biases, mask, sin, cos)


def attention_backward(
    qkv, weights, attended, g_attended, w_pos, biases, sin, cos, plan, begun, factors,
    cid,
):
    frames = qkv.shape[0]

    def kernel(*refs):
        x_ref, p_ref, a_ref, ga_ref, wp_ref, b_ref, sp_ref, cp_ref = refs[:8]
        begun_refs, given, refs = refs[8:10], refs[10:16], refs[16:]
        rows_ref, gw_ref, gb_ref = refs[:3]
        finished, made, refs = refs[3:5], refs[5:9], refs[9:]
        p_buf, gq_buf, kv_buf, gk_acc, gv_acc, p_sem, qs, qr, ql, ks, kr, kl = refs[:12]
        t_ref, s_ref, c_ref = refs[12:15]
        cg_in, g_c0, g_c1, rows_in, gate_in, g_joined = held = refs[15:21]
        results, load_sem, save_sem = refs[21:25], refs[25], refs[26]
        riding = plan.second(begun_refs, finished, refs[27:])
        needed = [
            pltpu.make_async_copy(a, b, load_sem.at[k]) for k, (a, b) in enumerate(zip(given, held))
        ]
        me = lax.axis_index("y")

        def block(k):
            peer = lax.rem(me + 1 + k, GROUP)
            return peer, pl.ds(pl.multiple_of(peer * ROWS, ROWS), ROWS)

        def load(k):
            c = pltpu.make_async_copy(p_ref.at[:, block(k)[1], :], p_buf.at[k % 2], p_sem.at[k % 2])
            c.start()
            return c

        loads = [load(0), load(1)]
        greet(y=True, xz=True, pair=True)
        next(riding)
        fill_table(sp_ref, cp_ref, s_ref, c_ref, t_ref)
        gk_acc[...] = jnp.zeros_like(gk_acc)
        gv_acc[...] = jnp.zeros_like(gv_acc)
        gw_ref[...] = jnp.zeros_like(gw_ref)
        gb_ref[...] = jnp.zeros_like(gb_ref)
        sends = []
        for k in range(GROUP):
            peer, at = block(k)
            query = x_ref[at, pl.ds(0, 128)].astype(F32)
            g_out = ga_ref[at, :]
            dots = g_out.astype(F32) * a_ref[at, :].astype(F32)
            sin_, cos_ = s_ref[at, :], c_ref[at, :]
            g_content = jnp.zeros((ROWS, 128), F32)
            g_position = jnp.zeros((ROWS, 128), F32)
            loads[k].wait()
            for h in range(2):
                keep = head_mask(h)
                content = ((query + b_ref[pl.ds(0, 1), :]) * (0.125 * keep)).astype(BF16)
                position = ((query + b_ref[pl.ds(1, 1), :]) * (0.125 * keep)).astype(BF16)
                g_head = (g_out.astype(F32) * keep).astype(BF16)
                p = p_buf[k % 2, h]
                g_weights = times_transpose(g_head, x_ref[:, pl.ds(256, 128)])
                inner = jnp.sum(dots * keep, -1, keepdims=True)
                g_scores = (p.astype(F32) * (g_weights - inner)).astype(BF16)
                gv_acc[...] += contract_rows(g_head, p)
                gk_acc[...] += contract_rows(content, g_scores)
                g_content = g_content + product(g_scores, x_ref[:, pl.ds(128, 128)]) * keep
                turned = product(g_scores, t_ref[...])
                ts, tc = turned[:, : D // 2], turned[:, D // 2 :]
                g_z = jnp.concatenate([tc * sin_ - ts * cos_, ts * sin_ + tc * cos_], axis=1)
                g_z = g_z.astype(BF16)
                g_position = g_position + product(g_z, wp_ref[...]) * keep
                gw_ref[...] += contract_rows(g_z, position)
                if (k, h) in ((1, 0), (2, 0), (3, 0)):
                    next(riding)
            g_content = g_content * 0.125
            g_position = g_position * 0.125
            gq_buf[at, :] = (g_content + g_position).astype(BF16)
            gb_ref[pl.ds(0, 1), :] += jnp.sum(g_content, 0, keepdims=True)
            gb_ref[pl.ds(1, 1), :] += jnp.sum(g_position, 0, keepdims=True)
            if k < 2:
                loads.append(load(k + 2))
            into = rows_ref.at[:, pl.ds((3 - k) * 384, 128)]
            if k < GROUP - 1:
                c = pltpu.make_async_remote_copy(
                    src_ref=gq_buf.at[at, :],
                    dst_ref=into,
                    send_sem=qs.at[k],
                    recv_sem=qr.at[k],
                    **to_y(peer),
                )
            else:
                c = pltpu.make_async_copy(gq_buf.at[at, :], into, ql)
            c.start()
            sends.append(c)
            if k == 0:
                for c in needed:
                    c.start()
        kv_buf[:, pl.ds(0, 128)] = gk_acc[...].T.astype(BF16)
        kv_buf[:, pl.ds(128, 128)] = gv_acc[...].T.astype(BF16)
        for k in range(GROUP):
            into = rows_ref.at[:, pl.ds((3 - k) * 384 + 128, 256)]
            peer, at = block(k)
            if k < GROUP - 1:
                c = pltpu.make_async_remote_copy(
                    src_ref=kv_buf.at[at, :],
                    dst_ref=into,
                    send_sem=ks.at[k],
                    recv_sem=kr.at[k],
                    **to_y(peer),
                )
            else:
                c = pltpu.make_async_copy(kv_buf.at[at, :], into, kl)
            c.start()
            sends.append(c)
        for c in needed:
            c.wait()
        for k in range(3):
            at = pl.ds(k * D, D)
            results[0][:, at] = contract_rows(cg_in[...], g_c0[:, at]).astype(BF16)
            results[1][:, at] = contract_rows(cg_in[...], g_c1[:, at]).astype(BF16)
            results[3][at, :] = contract_rows(gate_in[:, at], g_joined[:, pl.ds(D, D)]).astype(BF16)
        results[2][...] = contract_rows(rows_in[...], g_joined[:, pl.ds(0, D)]).astype(BF16)
        for k in range(4):
            c = pltpu.make_async_copy(results[k], made[k], save_sem.at[k])
            c.start()
            sends.append(c)
        for _ in riding:
            pass
        for c in sends:
            c.wait()

    shapes = [(D, GATE), (D, GATE), (D, D), (GATE, D)]

    return pl.pallas_call(
        kernel,
        in_specs=[VM, ANY] + [VM] * 8 + [ANY] * 6,
        out_specs=[ANY, VM, VM] + [VM] * 2 + [ANY] * 4,
        out_shape=[
            jax.ShapeDtypeStruct((ROWS, 3 * D), BF16),
            jax.ShapeDtypeStruct((D, 128), F32),
            jax.ShapeDtypeStruct((8, 128), F32),
        ]
        + plan.outs
        + [jax.ShapeDtypeStruct(s, BF16) for s in shapes],
        scratch_shapes=[
            pltpu.VMEM((2, 2, ROWS, frames), BF16),
            pltpu.VMEM((frames, 128), BF16),
            pltpu.VMEM((frames, 256), BF16),
            pltpu.VMEM((128, frames), F32),
            pltpu.VMEM((128, frames), F32),
            pltpu.SemaphoreType.DMA((2,)),
            pltpu.SemaphoreType.DMA((3,)),
            pltpu.SemaphoreType.DMA((3,)),
            pltpu.SemaphoreType.DMA,
            pltpu.SemaphoreType.DMA((3,)),
            pltpu.SemaphoreType.DMA((3,)),
            pltpu.SemaphoreType.DMA,
            pltpu.VMEM((frames, D), BF16),
            pltpu.VMEM((frames, D // 2), F32),
            pltpu.VMEM((frames, D // 2), F32),
        ]
        + [pltpu.VMEM(a.shape, BF16) for a in factors]
        + [pltpu.VMEM(s, BF16) for s in shapes]
        + [pltpu.SemaphoreType.DMA((6,)), pltpu.SemaphoreType.DMA((4,))]
        + plan.scratch,
        compiler_params=params(cid, 58),
        name="attention_backward",
    )(qkv, weights, attended, g_attended, w_pos, biases, sin, cos, *begun, *factors)


class Reduction:
    def __init__(self, shapes, kinds, parts, shared_rows=0):
        self.kinds = kinds
        self.halves = []
        self.offsets = []
        at = 0
        for (rows, cols), kind in zip(shapes, kinds):
            h, c = (rows // 2, cols // 4) if kind == "cols" else (rows // 8, cols)
            if kind == "each":
                h = rows // 2
            self.halves.append((h, c))
            self.offsets.append(at)
            at += h * c // D
        self.used = at
        self.parts = parts
        self.rows = sum(parts)
        self.shared = shared_rows
        count = len(shapes)
        n_a, n_b = max(parts[:2]), max(parts[2:])
        self.first_scratch = []
        for (h, c), kind in zip(self.halves, kinds):
            shape = (h, 4 * c) if kind == "cols" else (4, h, c)
            if kind == "each":
                shape = (4, 2 * h, c)
            self.first_scratch += [pltpu.VMEM(shape, BF16)] * 2
        self.first_scratch += [
            pltpu.VMEM((4, self.rows, D), BF16),
            pltpu.VMEM((2, 3, n_a, D), BF16),
            pltpu.VMEM((2, 3, 4, n_b // 4, D), BF16),
            pltpu.SemaphoreType.DMA((count, 4)),
            pltpu.SemaphoreType.DMA((count, 4)),
            pltpu.SemaphoreType.DMA((count, 4)),
            pltpu.SemaphoreType.DMA((5, 3)),
            pltpu.SemaphoreType.DMA((5, 3)),
        ]
        self.first_outs = [
            jax.ShapeDtypeStruct((2, n_a, D), BF16),
            jax.ShapeDtypeStruct((2, 4, n_b // 4, D), BF16),
        ]
        self.scratch = [
            pltpu.VMEM((2, 3, n_a // 4, D), BF16),
            pltpu.VMEM((2, 3, n_b // 4, D), BF16),
            pltpu.VMEM((2, 4, n_a // 4, D), BF16),
            pltpu.VMEM((2, 4, n_b // 4, D), BF16),
            pltpu.SemaphoreType.DMA((16, 3)),
            pltpu.SemaphoreType.DMA((16, 3)),
        ]
        self.outs = [jax.ShapeDtypeStruct((2, self.rows, D), BF16)]
        if shared_rows:
            self.outs.append(jax.ShapeDtypeStruct((4, 2, shared_rows, D), BF16))

    def helpers(self, g_send, g_recv):
        mine = {a: lax.axis_index(a) for a in ("x", "y", "z")}
        group = [0]

        def send_all(axis, src, dst):
            g = group[0]
            group[0] += 1
            copies = []
            for off in (2, 1, 3):
                peer = lax.rem(mine[axis] + off, 4)
                c = pltpu.make_async_remote_copy(
                    src_ref=src(peer, off),
                    dst_ref=dst(off - 1),
                    send_sem=g_send.at[g, off - 1],
                    recv_sem=g_recv.at[g, off - 1],
                    device_id={axis: peer},
                    device_id_type=MESH,
                )
                c.start()
                copies.append(c)
            return copies

        def wait(copies):
            for c in copies:
                c.wait()

        def add(dest, terms, rows, lead=None):
            step = 32 if rows % 32 == 0 else 16

            @pl.loop(0, rows, step=step)
            def _(r):
                at = pl.ds(pl.multiple_of(r, step), step)
                for b in range(lead or 1):
                    key = (b, at) if lead else (at,)
                    total = terms[0][key].astype(F32)
                    for t in terms[1:]:
                        total = total + t[key].astype(F32)
                    dest[key] = total.astype(BF16)

        def quarter(start, n, i):
            q = n // 4
            return pl.ds(pl.multiple_of(start + i * q, 16), q)

        return send_all, wait, add, quarter

    def first(self, ins, sums, scratch):
        count = len(ins)
        own, other = scratch[0 : 2 * count : 2], scratch[1 : 2 * count : 2]
        packed, ya, xz, s_loc, s_send, s_recv, g_send, g_recv = scratch[2 * count :]
        ta, tb = sums
        send_all, wait, add, quarter = self.helpers(g_send, g_recv)
        core, x, y, z = (lax.axis_index(a) for a in ("core", "x", "y", "z"))
        starts = [sum(self.parts[:k]) for k in range(4)]
        flight = []

        def begin(ready):
            while len(flight) < 4 and starts[len(flight)] + self.parts[len(flight)] <= ready:
                k = len(flight)
                at, n = starts[k], self.parts[k]
                if n == 0:
                    c = []
                elif k < 2:
                    c = send_all(
                        "y",
                        lambda p, o: packed.at[o, pl.ds(at, n), :],
                        lambda s: ya.at[k, s, pl.ds(0, n), :],
                    )
                else:
                    c = send_all(
                        "xz"[k - 2],
                        lambda p, o: packed.at[:, quarter(at, n, p), :],
                        lambda s: xz.at[k - 2, s, :, pl.ds(0, n // 4), :],
                    )
                flight.append(c)

        pair = dict(device_id={"core": 1 - core}, device_id_type=MESH)
        copies, everywhere = [], []

        def start(i):
            h, c = self.halves[i]
            if self.kinds[i] == "each":
                own[i][y] = ins[i][...]
                everywhere.extend(
                    send_all("y", lambda p, _: own[i].at[y], lambda s: own[i].at[y])
                )
                return
            for b in range(1 if self.kinds[i] == "cols" else 4):
                if self.kinds[i] == "cols":
                    theirs = ins[i].at[pl.ds((1 - core) * h, h), :]
                    ours = ins[i].at[pl.ds(core * h, h), :]
                    to, keep = other[i], own[i]
                else:
                    part = lax.rem(y + b, 4) if self.kinds[i] == "whole" else b
                    theirs = ins[i].at[pl.ds(part * 2 * h + (1 - core) * h, h), :]
                    ours = ins[i].at[pl.ds(part * 2 * h + core * h, h), :]
                    to, keep = other[i].at[b], own[i].at[b]
                r = pltpu.make_async_remote_copy(
                    src_ref=theirs,
                    dst_ref=to,
                    send_sem=s_send.at[i, b],
                    recv_sem=s_recv.at[i, b],
                    **pair,
                )
                l = pltpu.make_async_copy(ours, keep, s_loc.at[i, b])
                r.start()
                l.start()
                copies.extend([(i, r), (i, l)])

        return start, self.first_steps(
            own, other, packed, ya, xz, copies, everywhere, begin, flight, sums, s_send, s_recv,
            (send_all, wait, add, quarter),
        )

    def first_steps(
        self, own, other, packed, ya, xz, copies, everywhere, begin, flight, sums, s_send, s_recv,
        helpers,
    ):
        send_all, wait, add, quarter = helpers
        ta, tb = sums
        count = len(own)
        core, x, y, z = (lax.axis_index(a) for a in ("core", "x", "y", "z"))
        pair = dict(device_id={"core": 1 - core}, device_id_type=MESH)
        starts = [sum(self.parts[:k]) for k in range(4)]
        for i in range(count):
            if self.kinds[i] != "each":
                continue
            h, c = self.halves[i]
            wait(everywhere)
            add(other[i].at[0], [own[i].at[j] for j in range(4)], 2 * h)
            r = pltpu.make_async_remote_copy(
                src_ref=other[i].at[0, pl.ds((1 - core) * h, h), :],
                dst_ref=other[i].at[1, pl.ds(0, h), :],
                send_sem=s_send.at[i, 0],
                recv_sem=s_recv.at[i, 0],
                **pair,
            )
            r.start()
            copies.append((i, r))
        if self.rows > self.used:
            gap = self.rows - self.used
            for b in range(4):
                packed[b, pl.ds(self.used, gap), :] = jnp.zeros((gap, D), BF16)
        for i in range(count):
            for j, c in copies:
                if j == i:
                    c.wait()
            h, c = self.halves[i]
            at = self.offsets[i]
            tiles = c // 128
            if self.kinds[i] == "each":
                here = other[i][0, pl.ds(pl.multiple_of(core * h, 16), h), :]
                packed[0, pl.ds(at, h), :] = here + other[i][1, pl.ds(0, h), :]
                for b in range(1, 4):
                    packed[b, pl.ds(at, h), :] = jnp.zeros((h, c), BF16)
            elif self.kinds[i] != "cols":

                @pl.loop(0, h, step=16)
                def _(r):
                    row = pl.ds(pl.multiple_of(r, 16), 16)
                    to = pl.ds(pl.multiple_of(at + r, 16), 16)
                    for b in range(4):
                        packed[b, to, :] = own[i][b, row, :] + other[i][b, row, :]

            elif tiles == 4:

                @pl.loop(0, h, step=16)
                def _(r):
                    row = pl.ds(pl.multiple_of(r, 16), 16)
                    to = pl.ds(pl.multiple_of(at + r, 16), 16)
                    for b in range(4):
                        col = pl.ds(b * D, D)
                        packed[b, to, :] = own[i][row, col] + other[i][row, col]

            else:
                q = h // 4
                for g in range(4):
                    for t in range(tiles):
                        k = g * tiles + t
                        for b in range(4):
                            row, col = pl.ds(g * q, q), pl.ds(b * c + t * 128, 128)
                            to, tile = pl.ds(at + k // 4 * q, q), pl.ds(k % 4 * 128, 128)
                            packed[b, to, tile] = own[i][row, col] + other[i][row, col]

            begin(self.offsets[i + 1] if i + 1 < count else self.rows)

        yield
        for k in range(4):
            at, n = starts[k], self.parts[k]
            wait(flight[k])
            if n and k < 2:
                terms = [packed.at[0, pl.ds(at, n)]] + [ya.at[k, s] for s in range(3)]
                add(ta.at[k], terms, n)
            elif n:
                i = (x, z)[k - 2]
                terms = [packed.at[:, quarter(at, n, i), :]] + [xz.at[k - 2, s] for s in range(3)]
                add(tb.at[k - 2], terms, n // 4, 4)

    def second(self, sums, outs, scratch):
        ta, tb = sums
        ra, rb, fa, fb, g_send, g_recv = scratch
        out = outs[0]
        send_all, wait, add, quarter = self.helpers(g_send, g_recv)
        core, x, y, z = (lax.axis_index(a) for a in ("core", "x", "y", "z"))
        mine = {"x": x, "z": z}
        pair = dict(device_id={"core": 1 - core}, device_id_type=MESH)
        starts = [sum(self.parts[:k]) for k in range(4)]
        flight = []
        for k in range(4):
            n = self.parts[k]
            q = pl.ds(0, n // 4)
            if n == 0:
                c = []
            elif k < 2:
                c = send_all(
                    "xz"[k],
                    lambda p, _: ta.at[k, quarter(0, n, p), :],
                    lambda s: ra.at[k, s, q, :],
                )
            else:
                c = send_all(
                    "y", lambda p, o: tb.at[k - 2, o, q, :], lambda s: rb.at[k - 2, s, q, :]
                )
            flight.append(c)
        yield
        held = [(fa, fa, fb, fb)[k].at[k % 2] for k in range(4)]
        for k in range(4):
            n = self.parts[k]
            if n == 0:
                continue
            wait(flight[k])
            last_axis = "zx"[k % 2]
            here = held[k].at[mine[last_axis], pl.ds(0, n // 4), :]
            if k < 2:
                terms = [ta.at[k, quarter(0, n, (x, z)[k]), :]] + [ra.at[k, s] for s in range(3)]
            else:
                terms = [tb.at[k - 2, 0]] + [rb.at[k - 2, s] for s in range(3)]
            add(here, terms, n // 4)
            flight[k] = send_all(last_axis, lambda p, _: here, lambda s: here)
        yield
        for k in range(4):
            n = self.parts[k]
            if n == 0:
                continue
            wait(flight[k])
            piece = out.at[core, quarter(starts[k], n, (x, z)[k % 2]), :]
            add(piece, [held[k].at[j] for j in range(4)], n // 4)
            flight[k] = send_all("xz"[k % 2], lambda p, _: piece, lambda s: piece)
        yield
        for k in range(4):
            wait(flight[k])
        last = pltpu.make_async_remote_copy(
            src_ref=out.at[core],
            dst_ref=out.at[core],
            send_sem=g_send.at[14, 0],
            recv_sem=g_recv.at[14, 0],
            **pair,
        )
        last.start()
        if not self.shared:
            yield
            last.wait()
            return
        every = outs[1]
        start = self.used - self.shared
        every[y, core] = out[core, pl.ds(start, self.shared), :]
        spread = send_all("y", lambda p, _: every.at[y, core], lambda s: every.at[y, core])
        yield
        wait(spread)
        more = pltpu.make_async_remote_copy(
            src_ref=every.at[:, core],
            dst_ref=every.at[:, core],
            send_sem=g_send.at[15, 0],
            recv_sem=g_recv.at[15, 0],
            **pair,
        )
        more.start()
        yield
        last.wait()
        more.wait()

    def unpack(self, i, owned, dests):
        h, c = self.halves[i]
        at = self.offsets[i]
        tiles = c // 128
        if tiles == 4:
            for core in range(2):

                @pl.loop(0, h, step=16)
                def _(r):
                    to = pl.ds(pl.multiple_of(core * h + r, 16), 16)
                    row = pl.ds(pl.multiple_of(at + r, 16), 16)
                    dests[0][to, :] = owned[core, row, :].astype(F32)

            return
        q = h // 4
        each = tiles // len(dests)
        for core in range(2):
            for g in range(4):
                for t in range(tiles):
                    k = g * tiles + t
                    value = owned[core, pl.ds(at + k // 4 * q, q), pl.ds(k % 4 * 128, 128)]
                    to = pl.ds(core * h + g * q, q)
                    dests[t // each][to, pl.ds(t % each * 128, 128)] = value.astype(F32)


def write_gradients(late, owned, last, owned_last, mid, owned_mid, early, owned_early, every_early, channels):
    large = [(512, 512)] * 4 + [(512, channels)] * 2 + [(128, 512), (channels, 512), (1024, 512)]
    shapes = large[:4] + [(512, 2, channels)] + large[6:] + [(512, 128)] * 4 + [(31, 1024)] + [(1, 512)] * 10
    shapes += [(31, channels), (channels,), (channels,), (2, 64), (2, 64)]
    count = len(large)
    sources = (owned_early, every_early, owned_mid, owned, owned_last)

    def kernel(*refs):
        given, refs = refs[:5], refs[5:]
        outs, refs = refs[: count - 1], refs[count - 1 :]
        outs = [*outs[:4], outs[4].at[:, 0, :], outs[4].at[:, 1, :], *outs[5:]]
        wq, wk, wv, pos, taps = refs[:5]
        vectors, refs = refs[5:15], refs[15:]
        gate_taps, gain, shift, content, position, small, sem, load_sem = refs[:8]
        held, refs = refs[8 : 8 + count], refs[8 + count :]
        oe_ref, ee_ref, om_ref, o_ref, ol_ref = refs
        loads = [
            pltpu.make_async_copy(a, b, load_sem.at[k]) for k, (a, b) in enumerate(zip(given, refs))
        ]
        for c in loads:
            c.start()
        copies = []

        def send(k):
            c = pltpu.make_async_copy(held[k], outs[k], sem.at[k])
            c.start()
            copies.append(c)

        loads[0].wait()
        early.unpack(0, oe_ref, [held[2]])
        send(2)
        early.unpack(1, oe_ref, [held[3]])
        send(3)
        loads[1].wait()
        for y in range(4):
            for core in range(2):

                @pl.loop(0, 128, step=16)
                def _(r):
                    to = pl.ds(pl.multiple_of(y * 256 + core * 128 + r, 16), 16)
                    row = pl.ds(pl.multiple_of(r, 16), 16)
                    held[8][to, :] = ee_ref[y, core, row, :].astype(F32)

        send(8)
        loads[2].wait()
        for k, i in ((4, 0), (5, 1), (6, 2), (7, 3)):
            mid.unpack(i, om_ref, [held[k]])
            send(k)
        loads[3].wait()
        late.unpack(3, o_ref, [held[1]])
        send(1)
        loads[4].wait()
        last.unpack(0, ol_ref, [held[0]])
        send(0)
        late.unpack(0, o_ref, [wq, wk, wv])
        late.unpack(1, o_ref, [small])
        late.unpack(2, o_ref, [pos])
        at = last.offsets[1]
        rest = jnp.concatenate([ol_ref[core, pl.ds(at, 48), :].astype(F32) for core in range(2)])
        taps[:, pl.ds(0, 512)] = rest[0:31]
        taps[:, pl.ds(512, 512)] = rest[32:63]
        for k in range(10):
            vectors[k][...] = rest[64 + k : 65 + k]
        gate_taps[...] = small[pl.ds(0, 31), :]
        gain[...] = small[pl.ds(32, 1), :].reshape(channels)
        shift[...] = small[pl.ds(33, 1), :].reshape(channels)
        for k, ref in enumerate((content, position)):
            both = small[pl.ds(34 + k, 1), pl.ds(0, 128)]
            ref[pl.ds(0, 1), :] = both[:, :64]
            ref[pl.ds(1, 1), :] = both[:, 64:]
        for c in copies:
            c.wait()

    return pl.pallas_call(
        kernel,
        out_shape=[jax.ShapeDtypeStruct(s, F32) for s in shapes],
        in_specs=[ANY] * 5,
        out_specs=[ANY] * (count - 1) + [VM] * (len(shapes) - count + 1),
        scratch_shapes=[
            pltpu.VMEM((128, channels), F32),
            pltpu.SemaphoreType.DMA((count,)),
            pltpu.SemaphoreType.DMA((5,)),
        ]
        + [pltpu.VMEM(s, F32) for s in large]
        + [pltpu.VMEM(a.shape, a.dtype) for a in sources],
        compiler_params=pltpu.CompilerParams(vmem_limit_bytes=62 * 2**20),
        name="write_gradients",
    )(*sources)


def back(tensors, smalls, vectors, arrays, plans, cid):
    mid, late, last = plans
    n_tensors, n_small, n_vec = len(tensors), len(smalls), len(vectors)
    hidden = tensors[4].shape[1]

    def kernel(*refs):
        gqkv, wide_in, x_ref, middle, act_in, up_in, down_in, g_cg_in, g_merged, v_ref = refs[:10]
        refs = refs[n_tensors:]
        gate_taps, gain, shift, bias, pos, merge_taps = refs[:n_small]
        rows, refs = refs[n_small : n_small + n_vec], refs[n_small + n_vec :]
        ins, refs = refs[:4], refs[4:]
        g_features, o_late, o_last, o_mid = refs[:4]
        refs = refs[4:]
        small_f, shared_f, small, wide_pos, shared, g_wide, g_down, g_up, in1, g_mid, acc = refs[:11]
        wide, act, up1, down1, load_sem = refs[11:16]
        refs = refs[16:]
        sums_late, sums_last, sums_mid, refs = refs[:2], refs[2:4], refs[4:6], refs[6:]
        loads = [
            pltpu.make_async_copy(a, b, load_sem.at[k])
            for k, (a, b) in enumerate(
                ((wide_in, wide), (act_in, act), (down_in, down1), (up_in, up1))
            )
        ]
        for c in loads:
            c.start()

        def take(n):
            nonlocal refs
            got, refs = refs[:n], refs[n:]
            return got

        start1, l1 = late.first(
            [g_wide, small, wide_pos, g_down], sums_late, take(len(late.first_scratch))
        )
        start2, l2 = last.first([g_up, shared], sums_last, take(len(last.first_scratch)))
        s1 = late.second(sums_late, [o_late], take(len(late.scratch)))
        s2 = last.second(sums_last, [o_last], take(len(last.scratch)))
        start0, m1 = mid.first(ins, sums_mid, take(len(mid.first_scratch)))
        m2 = mid.second(sums_mid, [o_mid], take(len(mid.scratch)))
        vec = lambda k: v_ref[pl.ds(k, 1), :]
        slot = lambda k: pl.ds(k * D, D)
        total = lambda a: jnp.sum(a, 0, keepdims=True)

        greet(y=True, xz=True, pair=True)
        for k in range(4):
            start0(k)
        u2, inv2 = unit_norm(middle[...])
        attn_in = (u2 * vec(2) + vec(3)).astype(BF16)
        for k in range(3):
            g_wide[:, slot(k)] = contract_rows(attn_in, gqkv[:, slot(k)]).astype(BF16)
        start1(0)
        small_f[...] = jnp.zeros_like(small_f)
        small_f[pl.ds(0, 32), :] = gate_taps[...]
        small_f[pl.ds(32, 1), :] = gain[...]
        small_f[pl.ds(33, 1), :] = shift[...]
        small_f[pl.ds(34, 2), pl.ds(0, 128)] = bias[pl.ds(0, 2), :]
        small[...] = small_f[...].astype(BF16)
        start1(1)
        wide_pos[...] = jnp.zeros_like(wide_pos)
        wide_pos[:, pl.ds(0, 128)] = pos[...].astype(BF16)
        start1(2)
        shared_f[...] = jnp.zeros_like(shared_f)
        shared_f[pl.ds(0, 32), :] = merge_taps[:, pl.ds(0, D)]
        shared_f[pl.ds(32, 32), :] = merge_taps[:, pl.ds(D, D)]
        loads[0].wait()
        g_attn_in = times_transpose(gqkv[...], wide[...])
        g_gated = g_cg_in[...]
        shared_f[pl.ds(66, 1), :] = total(g_attn_in * u2)
        shared_f[pl.ds(67, 1), :] = total(g_attn_in)
        shared_f[pl.ds(68, 1), :] = total(g_gated * u2)
        shared_f[pl.ds(69, 1), :] = total(g_gated)
        for k, v in enumerate(rows):
            shared_f[pl.ds(70 + k, 1), :] = v[...]
        g_middle = g_merged[...] + norm_back(g_attn_in * vec(2) + g_gated * vec(4), u2, inv2)
        g_mid[...] = g_middle
        next(m1)
        gy1 = (0.5 * g_middle).astype(BF16)
        loads[1].wait()
        for k in range(hidden // D):
            a = act[:, slot(k)]
            hid = (a * jax.nn.sigmoid(a)).astype(BF16)
            g_down[slot(k), :] = contract_rows(hid, gy1).astype(BF16)
        start1(3)
        loads[2].wait()
        loads[3].wait()
        u1, inv1 = unit_norm(x_ref[...].astype(F32))
        in1[...] = (u1 * vec(0) + vec(1)).astype(BF16)
        acc[...] = jnp.zeros_like(acc)
        for k in range(hidden // D):
            a = act[:, slot(k)]
            sig = jax.nn.sigmoid(a)
            g_act = times_transpose(gy1, down1[slot(k), :]) * sig * (1.0 + a * (1.0 - sig))
            g_act = g_act.astype(BF16)
            g_up[:, slot(k)] = contract_rows(in1[...], g_act).astype(BF16)
            acc[...] += times_transpose(g_act, up1[k])
            if k == 2:
                next(l1)
        start2(0)
        u1, inv1 = unit_norm(x_ref[...].astype(F32))
        g_in1 = acc[...]
        shared_f[pl.ds(64, 1), :] = total(g_in1 * u1)
        shared_f[pl.ds(65, 1), :] = total(g_in1)
        shared[...] = shared_f[...].astype(BF16)
        start2(1)
        g_features[...] = g_mid[...] + norm_back(g_in1 * vec(0), u1, inv1)
        for _ in m1:
            pass
        next(m2)
        next(l2)
        for _ in l1:
            pass
        next(s1)
        next(m2)
        for _ in l2:
            pass
        next(s2)
        next(s1)
        next(m2)
        next(s2)
        next(s1)
        next(m2)
        next(s2)
        next(s1)
        next(s2)
        for g in (m2, s1, s2):
            for _ in g:
                pass

    bf = lambda *shape: pltpu.VMEM(shape, BF16)
    outs = [jax.ShapeDtypeStruct((ROWS, D), F32)] + late.outs + last.outs + mid.outs
    return pl.pallas_call(
        kernel,
        out_shape=outs,
        in_specs=[VM, ANY, VM, VM, ANY, ANY, ANY] + [VM] * (n_tensors - 7 + n_small + n_vec) + [ANY] * 4,
        out_specs=[VM] * len(outs),
        scratch_shapes=[
            pltpu.VMEM((128, GATE), F32),
            pltpu.VMEM((96, D), F32),
            bf(128, GATE),
            bf(D, D),
            bf(96, D),
            bf(D, 3 * D),
            bf(hidden, D),
            bf(D, hidden),
            bf(ROWS, D),
            pltpu.VMEM((ROWS, D), F32),
            pltpu.VMEM((ROWS, D), F32),
            bf(D, 3 * D),
            pltpu.VMEM((ROWS, hidden), F32),
            bf(GROUP, D, D),
            bf(hidden, D),
            pltpu.SemaphoreType.DMA((4,)),
        ]
        + [pltpu.VMEM(o.shape, BF16) for o in late.first_outs + last.first_outs + mid.first_outs]
        + late.first_scratch
        + last.first_scratch
        + late.scratch
        + last.scratch
        + mid.first_scratch
        + mid.scratch,
        compiler_params=params(cid, 60),
        name="back",
    )(*tensors, *smalls, *vectors, *arrays)


def local(
    features,
    lengths,
    first_gain,
    first_shift,
    first_up,
    first_down,
    attn_gain,
    attn_shift,
    w_query,
    w_key,
    w_value,
    w_pos,
    bias_content,
    bias_position,
    attn_out,
    cgmlp_gain,
    cgmlp_shift,
    cgmlp_up,
    gate_gain,
    gate_shift,
    gate_taps,
    cgmlp_down,
    merge_taps,
    merge_proj,
    second_gain,
    second_shift,
    second_up,
    second_down,
    final_gain,
    final_shift,
    cotangent,
):
    frames = ROWS * GROUP
    channels = gate_gain.shape[0]
    me = lax.axis_index("y")
    length = lengths[0]
    live = (jnp.arange(ROWS, dtype=jnp.int32) + me * ROWS < length).astype(F32)[:, None]
    mask = jnp.where(jnp.arange(frames, dtype=jnp.int32) < length, 0.0, -1e30)[None].astype(F32)
    rows_f, wide, small, *halves = prepare(
        (
            first_gain, first_shift, attn_gain, attn_shift, cgmlp_gain, cgmlp_shift, second_gain,
            second_shift, final_gain, final_shift,
        ),
        w_query, w_key, w_value, gate_taps, gate_gain, gate_shift, cgmlp_up,
    )
    (
        first_gain, first_shift, attn_gain, attn_shift, cgmlp_gain, cgmlp_shift, second_gain,
        second_shift, final_gain, final_shift,
    ) = (rows_f[k : k + 1] for k in range(10))
    sin, cos = position_factors(frames, D)
    biases = jnp.concatenate(
        [
            jnp.concatenate([bias_content, bias_position]).reshape(2, 128).astype(F32),
            jnp.zeros((6, 128), F32),
        ]
    )
    middle, invg, gate_out, act1, c0, c1, ug, gate_conv, gate_pad, qkv, *gathered = front(
        features,
        live,
        rows_f,
        (
            first_up, first_down, wide, halves[0], halves[1], small, attn_out, cgmlp_down,
            second_up, second_down,
        ),
        0,
    )
    up1, down1, qkv_w, cg0, cg1, small_all, out_w, cg_down, up2, down2 = gathered
    flat = lambda w: w.reshape(-1, w.shape[-1])
    down1, out_w, cg_down, down2 = flat(down1), flat(out_w), flat(cg_down), flat(down2)
    gate_taps_f = small_all[:32].astype(F32)
    gate_gain_f = small_all[31:32].astype(F32)
    merge_taps_f = jnp.pad(merge_taps.astype(F32), ((0, 1), (0, 0)))
    attended, attended_rows, weights = attention_forward(
        qkv, w_pos, biases, mask, sin, cos, 2
    )
    joined = jnp.concatenate([product(attended_rows, out_w), product(gate_out, cg_down)], axis=1)
    joined_live = joined * live
    merge_conv, joined_pad = conv_forward(joined_live, merge_taps_f, 3)
    mixed = (joined + merge_conv).astype(BF16)
    merged = middle + product(mixed, merge_proj)
    u3, inv3 = unit_norm(merged)
    in2 = (u3 * second_gain + second_shift).astype(BF16)
    act2 = product(in2, up2)
    sig2 = jax.nn.sigmoid(act2)
    hid2 = (act2 * sig2).astype(BF16)
    last = merged + 0.5 * product(hid2, down2)
    u4, inv4 = unit_norm(last)
    encoded = u4 * final_gain + final_shift

    u2, _ = unit_norm(middle)
    cg_in = (u2 * cgmlp_gain + cgmlp_shift).astype(BF16)
    root = 1.0 / math.sqrt(2.0)
    phi0 = 0.5 * (1.0 + lax.erf(c0 * root))
    phi1 = 0.5 * (1.0 + lax.erf(c1 * root))
    half0 = c0 * phi0

    cot = cotangent.astype(F32)
    g_final_gain = jnp.sum(cot * u4, 0)
    g_final_shift = jnp.sum(cot, 0)
    g_last = norm_back(cot * final_gain, u4, inv4)
    gy2 = (0.5 * g_last).astype(BF16)
    g_act2 = (times_transpose(gy2, down2) * sig2 * (1.0 + act2 * (1.0 - sig2))).astype(BF16)
    g_in2 = times_transpose(g_act2, up2)
    g_second_gain = jnp.sum(g_in2 * u3, 0)
    g_second_shift = jnp.sum(g_in2, 0)
    g_merged = g_last + norm_back(g_in2 * second_gain, u3, inv3)
    gm = g_merged.astype(BF16)
    gx = times_transpose(gm, merge_proj)
    merge_back, g_merge_taps, *early = conv_backward(
        gx, joined_pad, merge_taps_f, 4, factors=(in2, g_act2, hid2, gy2, mixed, gm)
    )
    g_joined = (gx + live * merge_back).astype(BF16)
    ga, gb = g_joined[:, :D], g_joined[:, D:]
    g_attended_rows = times_transpose(ga, out_w).astype(BF16)
    gg = times_transpose(gb, cg_down)
    g_conv = gg * half0
    plan_early = Reduction(
        [a.shape for a in early], ("cols", "rows", "whole"), (64, 64, 256, 256), 128
    )
    g_norm_raw, g_gate_taps, g_attended, *begun = conv_backward(
        g_conv, gate_pad, gate_taps_f, 5, g_attended_rows, early, plan_early
    )
    g_gate_norm = g_norm_raw * live
    g_gate_gain = jnp.sum(g_gate_norm * ug, 0)
    g_gate_shift = jnp.sum(g_gate_norm, 0)
    g_half1 = norm_back(g_gate_norm * gate_gain_f, ug, invg)
    density = 1.0 / math.sqrt(2.0 * math.pi)
    g_c0 = (gg * gate_conv * (phi0 + c0 * (density * jnp.exp(-0.5 * c0 * c0)))).astype(BF16)
    g_c1 = (g_half1 * (phi1 + c1 * (density * jnp.exp(-0.5 * c1 * c1)))).astype(BF16)
    g_cg_in = times_transpose(g_c0, cg0) + times_transpose(g_c1, cg1)
    plan_mid = Reduction(
        [(D, GATE), (D, GATE), (D, D), (GATE, D)],
        ("cols", "cols", "rows", "rows"),
        (64, 64, 256, 256),
    )
    g_qkv, g_w_pos, g_bias, owned_early, every_early, *mid = attention_backward(
        qkv, weights, attended, g_attended, w_pos, biases, sin, cos, plan_early, begun,
        (cg_in, g_c0, g_c1, attended_rows, gate_out, g_joined), 6,
    )
    plan_late = Reduction(
        [(D, 3 * D), (128, GATE), (D, D), (4 * D, D)],
        ("cols", "cols", "cols", "rows"),
        (64, 128, 192, 192),
    )
    plan_last = Reduction([(D, 4 * D), (96, D)], ("cols", "each"), (64, 0, 128, 128))
    g_features, owned, owned_last, owned_mid = back(
        (g_qkv, qkv_w, features, middle, act1, up1, down1, g_cg_in, g_merged, rows_f),
        (g_gate_taps, g_gate_gain[None], g_gate_shift[None], g_bias, g_w_pos, g_merge_taps),
        [v[None] for v in (g_second_gain, g_second_shift, g_final_gain, g_final_shift)],
        mid,
        (plan_mid, plan_late, plan_last),
        7,
    )
    (
        d_up1, d_down1, d_up2, d_down2, d_gated, d_out, d_cg_down, d_proj, d_query, d_key,
        d_value, d_pos, d_taps, *vectors, d_gate_taps, d_gain, d_shift, d_content,
        d_position,
    ) = write_gradients(
        plan_late, owned, plan_last, owned_last, plan_mid, owned_mid, plan_early, owned_early,
        every_early, channels,
    )
    vectors = [v.reshape(D) for v in vectors]
    return (
        encoded,
        g_features,
        vectors[0],
        vectors[1],
        d_up1,
        d_down1,
        vectors[2],
        vectors[3],
        d_query,
        d_key,
        d_value,
        d_pos,
        d_content,
        d_position,
        d_out,
        vectors[4],
        vectors[5],
        d_gated,
        d_gain,
        d_shift,
        d_gate_taps,
        d_cg_down,
        d_taps,
        d_proj,
        vectors[6],
        vectors[7],
        d_up2,
        d_down2,
        vectors[8],
        vectors[9],
    )


def solution(mesh):
    devices = mesh.devices.reshape(4, 4, 2, GROUP)
    fine = Mesh(devices, ("z", "x", "core", "y"))
    rows = P(("z", "x", "core", "y"), None)
    column, row = P(None, "y"), P("y", None)
    placed = (
        rows,
        P(("z", "x", "core")),
        P(),
        P(),
        column,
        row,
        P(),
        P(),
        column,
        column,
        column,
        column,
        row,
        row,
        row,
        P(),
        P(),
        P(None, None, "y"),
        P("y"),
        P("y"),
        column,
        row,
        P(),
        P(),
        P(),
        P(),
        column,
        row,
        P(),
        P(),
        rows,
    )
    return jax.shard_map(
        local,
        mesh=fine,
        in_specs=placed,
        out_specs=(rows,) + (rows,) + placed[2:30],
        check_vma=False,
    )
```
